32 devices in a mesh: dp: 16 (over z, y, x), mp: 2 (over core).
Axes of the slice: x: 2, y: 2, z: 4, core: 2. Of those that a mesh axis runs over, the one named last changes fastest.
Arguments:
- tokens: bfloat16 [24576, 768], P(('dp', 'mp')), may hold values from -6 to 6
- cotangent: bfloat16 [24576, 768], P(('dp', 'mp')), may hold values from -6 to 6
- mask: int32 [24576], P('dp'), may hold values 0 or 1
- lengths: int32 [16], P('dp'), may hold values from 128 to 512, as said below
- counts: int32 [16], P('dp'), may hold values from 1 to 12, as said below
- w_qkv: bfloat16 [3, 768, 768], P(None, None, 'mp'), may hold values from -0.21875 to 0.21875
- qv_bias: bfloat16 [2, 768], P(None, 'mp'), may hold values from -3 to 3
- w_out: bfloat16 [768, 768], P('mp'), may hold values from -0.875 to 0.875
- b_out: bfloat16 [768], replicated, may hold values from -3 to 3
- gain1: bfloat16 [768], replicated, may hold values from 0.099609375 to 1.8984375
- shift1: bfloat16 [768], replicated, may hold values from -3 to 3
- w_up: bfloat16 [768, 3072], P(None, 'mp'), may hold values from -0.21875 to 0.21875
- b_up: bfloat16 [3072], P('mp'), may hold values from -3 to 3
- w_down: bfloat16 [3072, 768], P('mp'), may hold values from -0.109375 to 0.109375
- b_down: bfloat16 [768], replicated, may hold values from -3 to 3
- gain2: bfloat16 [768], replicated, may hold values from 0.099609375 to 1.8984375
- shift2: bfloat16 [768], replicated, may hold values from -3 to 3
Outputs:
- out: bfloat16 [24576, 768], P(('dp', 'mp'))
- grad_tokens: float32 [24576, 768], P(('dp', 'mp'))
- grad_w_qkv: float32 [3, 768, 768], P(None, None, 'mp')
- grad_qv_bias: float32 [2, 768], P(None, 'mp')
- grad_w_out: float32 [768, 768], P('mp')
- grad_b_out: float32 [768], replicated
- grad_gain1: float32 [768], replicated
- grad_shift1: float32 [768], replicated
- grad_w_up: float32 [768, 3072], P(None, 'mp')
- grad_b_up: float32 [3072], P('mp')
- grad_w_down: float32 [3072, 768], P('mp')
- grad_b_down: float32 [768], replicated
- grad_gain2: float32 [768], replicated
- grad_shift2: float32 [768], replicated
The draws below stay inside these ranges and needn't reach their ends.
Inputs may be any that keep to these rules, and one draw needn't show every extreme that they name: `lengths`: each group's bucket length is 512, 256 or 128. `counts`: a group of bucket length L holds between 1 and 1536 / L sequences, in its first slots.
All inputs are finite; a program needn't handle non-finite values. No bound on the sum of `mask` on one device may be relied on, other than what follows from the above.
Results may differ from the reference program's by a relative error of at most 0.013.
Values may be sent and summed in bfloat16 or wider, within the bound.
No kernel may reach another device: no remote copies, remote signals or barrier semaphores. Data moves between devices by JAX's collectives and lax.ppermute only.
A program may use at most 128 MiB of HBM per device.

```python
import jax
import jax.numpy as jnp
from jax import lax

D = 768
HEADS = 12
HEAD_DIM = 64
FF = 3072
ROWS = 1536
SPAN = 512
TOKENS = 24576
N_DP = 16


def bucket_plan(key):
    level_key, count_key, pick_key, other_key = jax.random.split(key, 4)
    levels = jax.random.randint(level_key, (N_DP,), 0, 3)
    first = jax.random.randint(pick_key, (), 0, N_DP)
    second = (first + jax.random.randint(other_key, (), 1, N_DP)) % N_DP
    levels = levels.at[first].set(2).at[second].set(0)
    bucket = jnp.where(levels == 0, SPAN, jnp.where(levels == 1, SPAN // 2, SPAN // 4)).astype(jnp.int32)
    most = (ROWS // bucket).astype(jnp.int32)
    number = jax.random.randint(count_key, (N_DP,), 1, most + 1).astype(jnp.int32)
    number = number.at[first].set(4 * ROWS // SPAN).at[second].set(1)
    return (bucket, number)


def draw_lengths(key, part):
    plan = bucket_plan(key)
    return plan[0]


def draw_counts(key, part):
    plan = bucket_plan(key)
    return plan[1]


def touch_ends(drawn, key, smallest, top_value):
    longest = drawn.shape.index(max(drawn.shape))
    spots = []
    for shift in (0, 1):
        where = [jax.random.randint(jax.random.fold_in(key, axis), (), 0, length) for axis, length in enumerate(drawn.shape)]
        where[longest] = (where[longest] + shift) % drawn.shape[longest]
        spots.append(tuple(where))
    return drawn.at[spots[0]].set(smallest).at[spots[1]].set(top_value)


def level_of(key, extent, cuts, smallest, top_value):
    def one(position, blocks):
        draws = jax.random.uniform(jax.random.fold_in(jax.random.fold_in(key, 6), position), (blocks,), jnp.float32, smallest / len(cuts), top_value / len(cuts))
        return jnp.repeat(jnp.exp(draws), extent[position] // blocks).reshape((-1,) + (1,) * (len(extent) - position - 1))

    factor_of = one(*cuts[0])
    for cut in cuts[1:]:
        factor_of = factor_of * one(*cut)
    return factor_of


def bell_draw(key, shape, scale, bound, shards=(), held_as=jnp.bfloat16):
    array = jax.random.normal(key, shape, jnp.float32) * scale
    if len(shards) > 0:
        array = level_of(key, shape, shards, -0.22, 0.18) * array
    return jnp.clip(array, min=-bound, max=bound).astype(held_as)


def setup_inputs(seed: int = 0) -> dict:
    key_of = jax.random.split(jax.random.key(seed), 18)
    return {
        "tokens": bell_draw(key_of[0], (TOKENS, D), 1.0, 6.0, ((0, 32),)),
        "cotangent": bell_draw(key_of[1], (TOKENS, D), 1.0, 6.0, ((0, 32),)),
        "mask": touch_ends((jax.random.randint(key_of[2], (TOKENS,), 0, 8) < 7).astype(jnp.int32), jax.random.fold_in(key_of[2], 1), 0, 1),
        "lengths": draw_lengths(jax.random.fold_in(key_of[17], 71), 0),
        "counts": draw_counts(jax.random.fold_in(key_of[17], 71), 0),
        "w_qkv": bell_draw(key_of[5], (3, D, D), D ** -0.5, 0.21875, ((2, 2),)),
        "qv_bias": bell_draw(key_of[6], (2, D), 0.5, 3.0, ((1, 2),)),
        "w_out": bell_draw(key_of[7], (D, D), (D // 16) ** -0.5, 0.875, ((0, 2),)),
        "b_out": bell_draw(key_of[8], (D,), 0.5, 3.0),
        "gain1": jnp.clip(1.0 + 0.18 * jax.random.normal(key_of[9], (D,), jnp.float32), 0.099609375, 1.8984375).astype(jnp.bfloat16),
        "shift1": bell_draw(key_of[10], (D,), 0.5, 3.0),
        "w_up": bell_draw(key_of[11], (D, FF), D ** -0.5, 0.21875, ((1, 2),)),
        "b_up": bell_draw(key_of[12], (FF,), 0.5, 3.0, ((0, 2),)),
        "w_down": bell_draw(key_of[13], (FF, D), FF ** -0.5, 0.109375, ((0, 2),)),
        "b_down": bell_draw(key_of[14], (D,), 0.5, 3.0),
        "gain2": jnp.clip(1.0 + 0.18 * jax.random.normal(key_of[15], (D,), jnp.float32), 0.099609375, 1.8984375).astype(jnp.bfloat16),
        "shift2": bell_draw(key_of[16], (D,), 0.5, 3.0),
    }


@jax.custom_vjp
def low(v):
    return lax.optimization_barrier(v.astype(jnp.bfloat16)).astype(jnp.float32)

@jax.custom_vjp
def low_back(v):
    return v

def low_keep(v):
    return (low(v), None)

def low_pass(kept, grad):
    return (grad,)

def back_keep(v):
    return (v, None)

def back_low(kept, grad):
    return (low(grad),)
low.defvjp(low_keep, low_pass)
low_back.defvjp(back_keep, back_low)

def matmul(left, right):
    return jnp.dot(left, right, precision=lax.Precision.HIGHEST)

def layer_norm(hidden, gain, shift):
    centre = lax.optimization_barrier(jnp.mean(hidden, axis=-1, keepdims=True))
    centred = hidden - centre
    spread = lax.optimization_barrier(jnp.mean(centred * centred, axis=-1, keepdims=True))
    return centred * lax.rsqrt(spread + 1e-05) * gain + shift

def attend_block(pieces):
    query, keys, values, seq_ids, live = pieces
    scores = jnp.einsum('qhd,khd->hqk', query, keys, precision=lax.Precision.HIGHEST) * HEAD_DIM ** (-0.5)
    scores = low_back(scores)
    places = jnp.arange(SPAN, dtype=jnp.int32)
    allowed = (seq_ids[:, None] == seq_ids[None, :]) & ((live[None, :] > 0) | (places[:, None] == places[None, :]))
    masked = jnp.where(allowed[None], scores, -1e+30)
    row_max = lax.optimization_barrier(jnp.max(masked, axis=-1, keepdims=True))
    weights = jnp.exp(masked - row_max)
    probs = weights / lax.optimization_barrier(jnp.sum(weights, axis=-1, keepdims=True))
    mixed = jnp.einsum('hqk,khd->qhd', low(probs), values, precision=lax.Precision.HIGHEST)
    return mixed.reshape(SPAN, D)

def forward(seq_ids, live, tokens, w_qkv, qv_bias, w_out, b_out, gain1, shift1, w_up, b_up, w_down, b_down, gain2, shift2):
    all_rows = tokens.shape[0]
    query = low(low_back(matmul(tokens, w_qkv[0]) + qv_bias[0]))
    keys = low(low_back(matmul(tokens, w_qkv[1])))
    values = low(low_back(matmul(tokens, w_qkv[2]) + qv_bias[1]))
    blocks = all_rows // SPAN
    shaped = (blocks, SPAN, HEADS, HEAD_DIM)
    mixed = lax.map(jax.checkpoint(attend_block), (query.reshape(shaped), keys.reshape(shaped), values.reshape(shaped), seq_ids.reshape(blocks, SPAN), live.reshape(blocks, SPAN)))
    mixed = low(low_back(mixed.reshape(all_rows, D)))
    attn = low_back(matmul(mixed, w_out))
    normed = layer_norm(tokens + attn + b_out, gain1, shift1)
    up_value = low_back(matmul(low(normed), w_up) + b_up)
    activated = low(jax.nn.gelu(up_value, approximate=False))
    down = low_back(matmul(activated, w_down))
    return layer_norm(normed + down + b_down, gain2, shift2)

def reference(tokens, cotangent, mask, lengths, counts, w_qkv, qv_bias, w_out, b_out, gain1, shift1, w_up, b_up, w_down, b_down, gain2, shift2):
    params = tuple((p.astype(jnp.float32) for p in (w_qkv, qv_bias, w_out, b_out, gain1, shift1, w_up, b_up, w_down, b_down, gain2, shift2)))
    inputs = tokens.astype(jnp.float32).reshape(N_DP, ROWS, D)
    cotangents = cotangent.astype(jnp.float32).reshape(N_DP, ROWS, D)
    masks = mask.reshape(N_DP, ROWS)

    def group(carry, item):
        rows_in, rows_cot, rows_mask, length, count = item
        seq_ids = jnp.arange(ROWS, dtype=jnp.int32) // length
        live = ((rows_mask == 1) & (seq_ids < count)).astype(jnp.float32)

        def layer(*values):
            return forward(seq_ids, live, *values)
        result, pull = jax.vjp(layer, rows_in, *params)
        grads = pull(rows_cot * live[:, None])
        carry = tuple((c + g for c, g in zip(carry, grads[1:])))
        return (carry, (result.astype(jnp.bfloat16), grads[0]))
    start = tuple((jnp.zeros_like(p) for p in params))
    sums, (outputs, grad_inputs) = lax.scan(group, start, (inputs, cotangents, masks, lengths, counts))
    return (outputs.reshape(TOKENS, D), grad_inputs.reshape(TOKENS, D), sums[0], sums[1], sums[2], sums[3], sums[4], sums[5], sums[6], sums[7], sums[8], sums[9], sums[10], sums[11])
```

```python
import functools

import jax
import jax.numpy as jnp
from jax import lax
from jax.experimental import pallas as pl
from jax.experimental.pallas import tpu as pltpu
from jax.sharding import PartitionSpec as P

HEAD_DIM = 64
PAIR = 2 * HEAD_DIM
SPAN = 512
EDGE = SPAN // 2
LOG2E = 1.4426950408889634
MIB = 1 << 20
BF16 = jnp.bfloat16
F32 = jnp.float32


def nn(a, b):
    return lax.dot_general(a, b, (((1,), (0,)), ((), ())), preferred_element_type=F32)


def nt(a, b):
    return lax.dot_general(a, b, (((1,), (1,)), ((), ())), preferred_element_type=F32)


def tn(a, b):
    return lax.dot_general(a, b, (((0,), (0,)), ((), ())), preferred_element_type=F32)


def head_of(pair, index):
    lane = lax.broadcasted_iota(jnp.int32, pair.shape, 1)
    keep = lane < HEAD_DIM if index == 0 else lane >= HEAD_DIM
    return jnp.where(keep, pair, jnp.zeros_like(pair))


def stacked(refs):
    return jnp.concatenate([r[...] for r in refs], axis=0) if len(refs) > 1 else refs[0][...]


def forward_kernel(parts, *refs):
    query_ref, key_refs, value_refs = refs[0], refs[1 : 1 + parts], refs[1 + parts : 1 + 2 * parts]
    bias_ref, mixed_ref, lse_ref = refs[1 + 2 * parts :]
    query, keys, values = query_ref[...], stacked(key_refs), stacked(value_refs)
    values_t = values.astype(F32).T.astype(BF16)
    outs = []
    for index in range(2):
        scores = nt(keys, head_of(query, index)) * LOG2E + bias_ref[...]
        top = jnp.max(scores, axis=0, keepdims=True)
        weights = jnp.exp2(scores - top)
        total = jnp.sum(weights, axis=0, keepdims=True)
        rows = values_t[index * HEAD_DIM : (index + 1) * HEAD_DIM]
        outs.append(nn(rows, weights.astype(BF16)) * (1.0 / total))
        lse_ref[index : index + 1, :] = top + jnp.log2(total)
    mixed_ref[...] = jnp.concatenate(outs, axis=0).T.astype(BF16)


def backward_kernel(parts, *refs):
    query_ref, key_refs, value_refs = refs[0], refs[1 : 1 + parts], refs[1 + parts : 1 + 2 * parts]
    bias_ref, mixed_ref, grad_ref, lse_ref = refs[1 + 2 * parts : 5 + 2 * parts]
    out_refs = refs[5 + 2 * parts :]
    query, keys, values = query_ref[...], stacked(key_refs), stacked(value_refs)
    grad = grad_ref[...]
    keys_t = keys.astype(F32).T.astype(BF16)
    delta_terms = (mixed_ref[...].astype(F32) * grad.astype(F32)).T
    grad_q, grad_k, grad_v = [], 0.0, 0.0
    for index in range(2):
        query_h, grad_h = head_of(query, index), head_of(grad, index)
        scores = nt(keys, query_h) * LOG2E + bias_ref[...]
        probs = jnp.exp2(scores - lse_ref[index : index + 1, :])
        grad_probs = nt(values, grad_h)
        half = slice(index * HEAD_DIM, (index + 1) * HEAD_DIM)
        delta = jnp.sum(delta_terms[half], axis=0, keepdims=True)
        grad_scores = (probs * (grad_probs - delta)).astype(BF16)
        grad_v += nn(probs.astype(BF16), grad_h)
        grad_k += nn(grad_scores, query_h)
        grad_q.append(nn(keys_t[half], grad_scores))
    out_refs[0][...] = (jnp.concatenate(grad_q, axis=0).T * HEAD_DIM**-0.5).astype(BF16)
    at = 0
    for ref_k, ref_v in zip(out_refs[1 : 1 + parts], out_refs[1 + parts :]):
        rows = ref_k.shape[0]
        ref_k[...] = grad_k[at : at + rows].astype(ref_k.dtype)
        ref_v[...] = grad_v[at : at + rows].astype(ref_v.dtype)
        at += rows


def pairs_of(width):
    return width // PAIR


def full_specs(width):
    rows = pl.BlockSpec((SPAN, PAIR), lambda j: (0, j))
    return rows


def edge_spec():
    return pl.BlockSpec((EDGE, PAIR), lambda j: (SPAN // EDGE, j))


def cost(keys, queries, pairs, products):
    return pl.CostEstimate(
        flops=2 * keys * queries * PAIR * products * 2 * pairs,
        bytes_accessed=pairs * (keys + queries) * PAIR * 8,
        transcendentals=keys * queries * 2 * pairs,
    )


PARAMS = pltpu.CompilerParams(vmem_limit_bytes=40 * MIB)


def attend_full(query, keys, values, bias):
    pairs = pairs_of(query.shape[1])
    rows = pl.BlockSpec((SPAN, PAIR), lambda j: (0, j))
    return pl.pallas_call(
        functools.partial(forward_kernel, 1),
        grid=(pairs,),
        in_specs=[rows, rows, rows, pl.BlockSpec((SPAN, SPAN), lambda j: (0, 0))],
        out_specs=[rows, pl.BlockSpec((None, 2, SPAN), lambda j: (j, 0, 0))],
        out_shape=[
            jax.ShapeDtypeStruct((SPAN, query.shape[1]), BF16),
            jax.ShapeDtypeStruct((pairs, 2, SPAN), F32),
        ],
        compiler_params=PARAMS,
        cost_estimate=cost(SPAN, SPAN, pairs, 2),
        name="attend_full",
    )(query, keys, values, bias)


def far_spec(which, pairs):
    return pl.BlockSpec((None, EDGE, PAIR), lambda j: (which, 0, (j + pairs // 2) % pairs))


def attend_edge(query, keys, values, far, bias):
    pairs = pairs_of(query.shape[1])
    near = edge_spec()
    return pl.pallas_call(
        functools.partial(forward_kernel, 2),
        grid=(pairs,),
        in_specs=[near, near, far_spec(0, pairs), near, far_spec(1, pairs)]
        + [pl.BlockSpec((SPAN, EDGE), lambda j: (0, 0))],
        out_specs=[
            pl.BlockSpec((EDGE, PAIR), lambda j: (0, j)),
            pl.BlockSpec((None, 2, EDGE), lambda j: (j, 0, 0)),
        ],
        out_shape=[
            jax.ShapeDtypeStruct((EDGE, query.shape[1]), BF16),
            jax.ShapeDtypeStruct((pairs, 2, EDGE), F32),
        ],
        compiler_params=PARAMS,
        cost_estimate=cost(SPAN, EDGE, pairs, 2),
        name="attend_edge",
    )(query, keys, far, values, far, bias)


def attend_full_back(query, keys, values, bias, mixed, grad, lse):
    width = query.shape[1]
    pairs = pairs_of(width)
    rows = pl.BlockSpec((SPAN, PAIR), lambda j: (0, j))
    return pl.pallas_call(
        functools.partial(backward_kernel, 1),
        grid=(pairs,),
        in_specs=[rows, rows, rows, pl.BlockSpec((SPAN, SPAN), lambda j: (0, 0)), rows, rows]
        + [pl.BlockSpec((None, 2, SPAN), lambda j: (j, 0, 0))],
        out_specs=[rows] * 3,
        out_shape=[jax.ShapeDtypeStruct((SPAN, width), BF16)] * 3,
        compiler_params=PARAMS,
        cost_estimate=cost(SPAN, SPAN, pairs, 5),
        name="attend_full_back",
    )(query, keys, values, bias, mixed, grad, lse)


def attend_edge_back(query, keys, values, far, bias, mixed, grad, lse):
    width = query.shape[1]
    pairs = pairs_of(width)
    near = edge_spec()
    own = pl.BlockSpec((EDGE, PAIR), lambda j: (0, j))
    away = pl.BlockSpec((EDGE, PAIR), lambda j: (0, (j + pairs // 2) % pairs))
    return pl.pallas_call(
        functools.partial(backward_kernel, 2),
        grid=(pairs,),
        in_specs=[near, near, far_spec(0, pairs), near, far_spec(1, pairs)]
        + [pl.BlockSpec((SPAN, EDGE), lambda j: (0, 0)), own, near]
        + [pl.BlockSpec((None, 2, EDGE), lambda j: (j, 0, 0))],
        out_specs=[own, own, away, own, away],
        out_shape=[jax.ShapeDtypeStruct((EDGE, width), d) for d in (BF16, F32, BF16, F32, BF16)],
        compiler_params=PARAMS,
        cost_estimate=cost(SPAN, EDGE, pairs, 5),
        name="attend_edge_back",
    )(query, keys, far, values, far, bias, mixed, grad, lse)


def normal_parts(value):
    size = jnp.abs(value)
    t = 1.0 / (1.0 + (0.3275911 * 0.5**0.5) * size)
    bell = jnp.exp(-0.5 * value * value)
    poly = t * (
        0.127414796 + t * (-0.142248368 + t * (0.7107068705 + t * (-0.7265760135 + t * 0.5307027145)))
    )
    tail = poly * bell
    return jnp.where(value >= 0, 1.0 - tail, tail), bell * 0.3989422804014327


def standardize(hidden):
    centred = hidden - jnp.mean(hidden, axis=-1, keepdims=True)
    scale = lax.rsqrt(jnp.mean(centred * centred, axis=-1, keepdims=True) + 1e-05)
    return centred * scale, scale


def standardize_back(grad, xhat, scale):
    mean_grad = jnp.mean(grad, axis=-1, keepdims=True)
    mean_both = jnp.mean(grad * xhat, axis=-1, keepdims=True)
    return scale * (grad - mean_grad - xhat * mean_both)


def program(n_dp):
    steps = n_dp.bit_length() - 1
    assert 1 << steps == n_dp
    orders = (list(range(steps)), [1, 0, *range(2, steps)])

    def swap(array):
        return lax.ppermute(array, "mp", [(0, 1), (1, 0)])

    def partner(array, step):
        pairs = [
            (2 * d + m, 2 * (d ^ (1 << orders[m][step])) + m) for d in range(n_dp) for m in range(2)
        ]
        return lax.ppermute(array, ("dp", "mp"), pairs)

    def total(own, sibling):
        dp, mp = lax.axis_index("dp"), lax.axis_index("mp")
        bits = [jnp.where(mp == 0, dp >> orders[0][s], dp >> orders[1][s]) & 1 for s in range(steps)]
        held = own + swap(sibling.astype(BF16)).astype(F32)
        for step in range(steps):
            half = held.shape[0] // 2
            away = lax.dynamic_slice_in_dim(held, (1 - bits[step]) * half, half).astype(BF16)
            kept = lax.dynamic_slice_in_dim(held, bits[step] * half, half)
            held = kept + partner(away, step).astype(F32)
        piece = held.astype(BF16)
        for step in reversed(range(steps)):
            other = partner(piece, step)
            piece = jnp.where(
                bits[step] == 0,
                jnp.concatenate([piece, other], axis=0),
                jnp.concatenate([other, piece], axis=0),
            )
        return piece

    def per_device(
        tokens, cotangent, mask, lengths, counts, w_qkv, qv_bias, w_out, b_out, gain1, shift1,
        w_up, b_up, w_down, b_down, gain2, shift2,
    ):
        rows, width = tokens.shape
        mp = lax.axis_index("mp")

        def rolled(array, amount):
            return lax.dynamic_slice_in_dim(
                jnp.concatenate([array, array], axis=0), amount, array.shape[0]
            )

        def both(own, axis):
            return jnp.concatenate([own, swap(own)], axis=axis)

        ahead = mp * EDGE
        x = rolled(tokens, ahead)
        w_qkv_all = both(w_qkv, 2)
        small = both(jnp.concatenate([qv_bias[0], qv_bias[1], b_up])[None], 0)
        local = qv_bias.shape[1]
        q_bias = small[:, :local].reshape(-1).astype(F32)
        v_bias = small[:, local : 2 * local].reshape(-1).astype(F32)
        up_bias = small[:, 2 * local :].reshape(-1).astype(F32)
        w_out_all, w_up_all, w_down_all = both(w_out, 0), both(w_up, 1), both(w_down, 0)

        length, live_end = lengths[0], counts[0] * lengths[0]
        own_place = mp * rows + (jnp.arange(rows, dtype=jnp.int32) + ahead) % rows
        places = jnp.arange(mask.shape[0], dtype=jnp.int32)
        live_all = (mask == 1) & (places < live_end)
        live_rows = rolled(lax.dynamic_slice_in_dim(live_all, mp * rows, rows), ahead)

        def bias_of(key_place, query_place, key_live):
            allowed = (key_place[:, None] // length == query_place[None, :] // length) & (
                key_live[:, None] | (key_place[:, None] == query_place[None, :])
            )
            return jnp.where(allowed, 0.0, -1e30).astype(F32)

        edge_place = own_place[SPAN:]
        far_place = EDGE * (3 - mp) + jnp.arange(EDGE, dtype=jnp.int32)
        far_live = lax.dynamic_slice_in_dim(live_all, EDGE * (3 - mp), EDGE)
        bias_full = bias_of(own_place[:SPAN], own_place[:SPAN], live_rows[:SPAN])
        bias_edge = bias_of(
            jnp.concatenate([edge_place, far_place]),
            edge_place,
            jnp.concatenate([live_rows[SPAN:], far_live]),
        )

        projected = jnp.einsum("td,cde->cte", x, w_qkv_all, preferred_element_type=F32)
        query = (projected[0] + q_bias).astype(BF16) * BF16(HEAD_DIM**-0.5)
        keys = projected[1].astype(BF16)
        values = (projected[2] + v_bias).astype(BF16)
        far = swap(jnp.stack([keys[SPAN:], values[SPAN:]]))
        mixed_full, lse_full = attend_full(query, keys, values, bias_full)
        mixed_edge, lse_edge = attend_edge(query, keys, values, far, bias_edge)
        mixed = jnp.concatenate([mixed_full, mixed_edge], axis=0)

        resid1 = x.astype(F32) + nn(mixed, w_out_all) + b_out.astype(F32)
        xhat1, scale1 = standardize(resid1)
        normed = xhat1 * gain1.astype(F32) + shift1.astype(F32)
        normed_low = normed.astype(BF16)
        up_value = nn(normed_low, w_up_all) + up_bias
        phi_sum, phi = normal_parts(up_value)
        act_low = (up_value * phi_sum).astype(BF16)
        slope = phi_sum + up_value * phi
        resid2 = normed + nn(act_low, w_down_all) + b_down.astype(F32)
        xhat2, scale2 = standardize(resid2)
        out = rolled((xhat2 * gain2.astype(F32) + shift2.astype(F32)).astype(BF16), rows - ahead)

        grad_result = rolled(cotangent, ahead).astype(F32) * live_rows.astype(F32)[:, None]
        grad_gain2 = jnp.sum(grad_result * xhat2, axis=0)
        grad_shift2 = jnp.sum(grad_result, axis=0)
        grad_resid2 = standardize_back(grad_result * gain2.astype(F32), xhat2, scale2)
        grad_b_down = jnp.sum(grad_resid2, axis=0)
        grad_down = grad_resid2.astype(BF16)
        hidden = w_up.shape[1]
        gw_down = tn(act_low, grad_down)
        gw_down = total(gw_down[:hidden], gw_down[hidden:])

        grad_up = (nt(grad_down, w_down_all) * slope).astype(BF16)
        gw_up = tn(normed_low, grad_up)
        halved = [gw_up[:, i * width : (i + 1) * width] for i in range(2 * hidden // width)]
        mid = len(halved) // 2
        gw_up = total(jnp.concatenate(halved[:mid], axis=0), jnp.concatenate(halved[mid:], axis=0))
        gw_up = jnp.concatenate([gw_up[i * width : (i + 1) * width] for i in range(mid)], axis=1)
        grad_b_up = jnp.sum(grad_up, axis=0, dtype=F32)
        grad_normed = grad_resid2 + nt(grad_up, w_up_all)
        grad_gain1 = jnp.sum(grad_normed * xhat1, axis=0)
        grad_shift1 = jnp.sum(grad_normed, axis=0)
        grad_resid1 = standardize_back(grad_normed * gain1.astype(F32), xhat1, scale1)
        grad_b_out = jnp.sum(grad_resid1, axis=0)
        grad_attn = grad_resid1.astype(BF16)
        gw_out = tn(mixed, grad_attn)
        grad_mixed = nt(grad_attn, w_out_all).astype(BF16)

        edge_q, edge_k, far_k, edge_v, far_v = attend_edge_back(
            query, keys, values, far, bias_edge, mixed_edge, grad_mixed, lse_edge
        )
        far_back = swap(jnp.stack([far_k, far_v])).astype(F32)
        full_q, full_k, full_v = attend_full_back(
            query, keys, values, bias_full, mixed_full, grad_mixed, lse_full
        )
        grad_q = jnp.concatenate([full_q, edge_q], axis=0)
        grad_k = jnp.concatenate([full_k, (edge_k + far_back[0]).astype(BF16)], axis=0)
        grad_v = jnp.concatenate([full_v, (edge_v + far_back[1]).astype(BF16)], axis=0)

        gw = [tn(x, g) for g in (grad_q, grad_k, grad_v)]
        sum_q = jnp.sum(grad_q, axis=0, dtype=F32)
        sum_v = jnp.sum(grad_v, axis=0, dtype=F32)

        def packed(start):
            part = [g[:, start : start + local] for g in gw]
            top, low = slice(0, local), slice(local, 2 * local)
            split = [jnp.concatenate([p[top], p[low]], axis=1) for p in part]
            heads = gw_out[start : start + local]
            one = jnp.concatenate([sum_q[start : start + local], sum_v[start : start + local]])
            first = (start // local) * hidden
            two = grad_b_up[first : first + hidden].reshape(-1, width)
            flat = [grad_b_out, grad_gain1, grad_shift1, grad_b_down, grad_gain2, grad_shift2]
            tail = jnp.concatenate([one[None], two, jnp.stack(flat)], axis=0)
            unit = 16 * n_dp
            count = 4 * local + tail.shape[0]
            tail = jnp.pad(tail, ((0, -count % unit), (0, 0)))
            return jnp.concatenate([*split, heads, tail], axis=0)

        last = total(packed(0), packed(local))
        gw_qkv = jnp.stack(
            [
                jnp.concatenate(
                    [last[c * local : (c + 1) * local, :local], last[c * local : (c + 1) * local, local:]],
                    axis=0,
                )
                for c in range(3)
            ]
        )
        gw_out = last[3 * local : 4 * local]
        tail = last[4 * local :]
        vectors = 1 + hidden // width
        g_qv_bias = tail[0].reshape(2, local)
        g_b_up = tail[1:vectors].reshape(-1)
        singles = [tail[vectors + i].astype(F32) for i in range(6)]

        grad_tokens = grad_resid1
        for g, c in ((grad_q, 0), (grad_k, 1), (grad_v, 2)):
            grad_tokens = grad_tokens + nt(g, w_qkv_all[c])
        grad_tokens = rolled(grad_tokens, rows - ahead)
        g_b_out, g_gain1, g_shift1, g_b_down, g_gain2, g_shift2 = singles
        return (
            out,
            grad_tokens,
            gw_qkv.astype(F32),
            g_qv_bias.astype(F32),
            gw_out.astype(F32),
            g_b_out,
            g_gain1,
            g_shift1,
            gw_up.astype(F32),
            g_b_up.astype(F32),
            gw_down.astype(F32),
            g_b_down,
            g_gain2,
            g_shift2,
        )

    return per_device


def solution(mesh):
    rows, cols, one = P(("dp", "mp"), None), P(None, "mp"), P()
    in_specs = (
        rows, rows, P("dp"), P("dp"), P("dp"),
        P(None, None, "mp"), cols, P("mp", None), one, one, one,
        cols, P("mp"), P("mp", None), one, one, one,
    )
    out_specs = (
        rows, rows, P(None, None, "mp"), cols, P("mp", None), one, one, one,
        cols, P("mp"), P("mp", None), one, one, one,
    )
    return jax.shard_map(
        program(mesh.shape["dp"]), mesh=mesh, in_specs=in_specs, out_specs=out_specs, check_vma=False
    )
```

```python
import functools

import jax
import jax.numpy as jnp
from jax import lax
from jax.experimental import pallas as pl
from jax.experimental.pallas import tpu as pltpu
from jax.sharding import PartitionSpec as P

HEAD_DIM = 64
PAIR = 2 * HEAD_DIM
SPAN = 512
EDGE = SPAN // 2
LOG2E = 1.4426950408889634
MIB = 1 << 20
RATE = 3.3e6
BF16 = jnp.bfloat16
F32 = jnp.float32
WHOLE = pl.BlockSpec(memory_space=pltpu.VMEM)
UNREAD = pl.BlockSpec(memory_space=pl.ANY)


def shape(dims, dtype):
    return jax.ShapeDtypeStruct(tuple(dims), dtype)


def nn(a, b):
    return lax.dot_general(a, b, (((1,), (0,)), ((), ())), preferred_element_type=F32)


def nt(a, b):
    return lax.dot_general(a, b, (((1,), (1,)), ((), ())), preferred_element_type=F32)


def tn(a, b):
    return lax.dot_general(a, b, (((0,), (0,)), ((), ())), preferred_element_type=F32)


def call(
    kernel, grid, inputs, outputs, scalars, name, after=(), aliases=None, limit=32, scratch=(), us=1.0, carry=(), stream=(), settle=()
):
    n_in, n_out = len(inputs), len(outputs)
    inputs = [
        (pltpu.with_memory_space_constraint(a, pltpu.HBM) if i in stream else a, spec)
        for i, (a, spec) in enumerate(inputs)
    ]
    outputs = [
        (pltpu.HBM(o.shape, o.dtype) if i in settle else o, spec) for i, (o, spec) in enumerate(outputs)
    ]
    held = (*after, *carry)
    aliases = {1 + k: v for k, v in (aliases or {}).items()}
    aliases |= {1 + n_in + len(after) + k: n_out + k for k in range(len(carry))}

    def body(scalar_ref, *refs):
        first = n_in + len(held)
        kernel(scalar_ref, refs[:n_in], refs[first : first + n_out], *refs[first + n_out + len(carry) :])

    return pl.pallas_call(
        body,
        grid_spec=pltpu.PrefetchScalarGridSpec(
            num_scalar_prefetch=1,
            grid=grid,
            in_specs=[s for _, s in inputs] + [UNREAD] * len(held),
            out_specs=[s for _, s in outputs] + [UNREAD] * len(carry),
            scratch_shapes=scratch,
        ),
        out_shape=[o for o, _ in outputs] + [shape(a.shape, a.dtype) for a in carry],
        input_output_aliases=aliases,
        compiler_params=pltpu.CompilerParams(vmem_limit_bytes=limit * MIB),
        cost_estimate=pl.CostEstimate(flops=0, bytes_accessed=int(us * RATE), transcendentals=0),
        name=name,
    )(scalars, *[a for a, _ in inputs], *held)


MP, LENGTH, LIVE, BITS = range(4)


def lay(tiles):
    return lambda i, sc: ((jnp.minimum(i, tiles - 1) + sc[MP]) % tiles, 0)


def prepare(mask, rows, scalars):
    slots = mask.shape[0]

    def kernel(sc, ins, outs, wide_ref):
        mp, length = sc[MP], sc[LENGTH]
        place = lax.broadcasted_iota(jnp.int32, (1, slots), 1)
        live = jnp.where((ins[0][...].reshape(1, slots) == 1) & (place < sc[LIVE]), 1.0, 0.0)
        wide_ref[...] = jnp.broadcast_to(live, (128, slots)).T

        def rows_at(start, count):
            return wide_ref[pl.ds(pl.multiple_of(start, EDGE), count), :]

        def sequence(slot):
            return sum((slot >= times * length).astype(jnp.int32) for times in (1, 2, 3))

        def masked(keys, queries, live_keys):
            repeats = [live_keys] * (queries.shape[1] // 128)
            allowed = (sequence(keys) == sequence(queries)) & (
                (jnp.concatenate(repeats, axis=1) > 0.5) | (keys == queries)
            )
            return jnp.where(allowed, 0.0, -1e30)

        whole = rows_at(mp * (slots - SPAN), SPAN)
        near = rows_at(SPAN + mp * EDGE, EDGE)
        far = rows_at(SPAN + (1 - mp) * EDGE, EDGE)
        outs[2][:SPAN], outs[2][SPAN:] = whole, near
        square = (SPAN, SPAN)
        outs[0][...] = masked(
            lax.broadcasted_iota(jnp.int32, square, 0), lax.broadcasted_iota(jnp.int32, square, 1), whole
        )
        tall = (SPAN, EDGE)
        keys = lax.broadcasted_iota(jnp.int32, tall, 0) + mp * EDGE
        keys = jnp.where(keys >= SPAN, keys - SPAN, keys)
        queries = lax.broadcasted_iota(jnp.int32, tall, 1) + mp * EDGE
        outs[1][...] = masked(keys, queries, jnp.concatenate([near, far], axis=0))

    outputs = [(shape((SPAN, SPAN), F32), WHOLE), (shape((SPAN, EDGE), F32), WHOLE), (shape((rows, 128), F32), WHOLE)]
    scratch = [pltpu.VMEM((slots, 128), F32)]
    return call(kernel, (1,), [(mask, WHOLE)], outputs, scalars, "prepare", scratch=scratch)


def project(x, weights, bias, half, scalars, held):
    rows, width = x.shape
    tiles, local = rows // EDGE, weights.shape[2]

    def kernel(sc, ins, outs):
        x_ref, w_ref, b_ref = ins[:3]
        step = pl.program_id(0)

        def each_tile(finish, extra=None):
            for tile in range(tiles):
                at = pl.multiple_of(((tile + sc[MP]) % tiles) * EDGE, EDGE)
                block = x_ref[pl.ds(at, EDGE), :]
                finish(tile, slice(tile * EDGE, (tile + 1) * EDGE), nn(block, w_ref[...]), block)

        def bias_of(row):
            return b_ref[row : row + 1, :].astype(F32)

        @pl.when(step == 0)
        def _():
            def put(tile, where, value, block):
                outs[0][where, :] = (value + bias_of(0)).astype(BF16) * BF16(HEAD_DIM**-0.5)
                outs[4][where, :] = block

            each_tile(put)

        @pl.when(step == 1)
        def _():
            def put(tile, where, value, block):
                outs[1][where, :] = value.astype(BF16)
                if tile == tiles - 1:
                    outs[3][0] = value.astype(BF16)

            each_tile(put)

        @pl.when(step == 2)
        def _():
            def put(tile, where, value, block):
                value = (value + bias_of(1)).astype(BF16)
                outs[2][where, :] = value
                if tile == tiles - 1:
                    outs[3][1] = value

            each_tile(put)

    part = pl.BlockSpec((rows, local), lambda i, sc: (0, half))
    everything = pl.BlockSpec((rows, width), lambda i, sc: (0, 0))
    outputs = [(shape((rows, 2 * local), BF16), part)] * 3
    outputs.append((shape((2, EDGE, 2 * local), BF16), pl.BlockSpec((2, EDGE, local), lambda i, sc: (0, 0, half))))
    outputs.append((shape((rows, width), BF16), everything))
    inputs = [(x, everything), (weights, pl.BlockSpec((None, width, local), lambda i, sc: (i, 0, 0))), (bias, WHOLE)]
    inputs += [(a, UNREAD) for a in held]
    aliases = {3 + i: i for i in range(len(held))}
    return call(
        kernel, (3,), inputs, outputs, scalars, f"project_{half}", aliases=aliases, us=3.5, stream=(0,), settle=(4,)
    )


def head_of(pair, index):
    lane = lax.broadcasted_iota(jnp.int32, pair.shape, 1)
    keep = lane < HEAD_DIM if index == 0 else lane >= HEAD_DIM
    return jnp.where(keep, pair, jnp.zeros_like(pair))


def stacked(refs):
    return jnp.concatenate([r[...] for r in refs], axis=0) if len(refs) > 1 else refs[0][...]


def attend_kernel(parts, _, ins, outs):
    query_ref, key_refs, value_refs = ins[0], ins[1 : 1 + parts], ins[1 + parts : 1 + 2 * parts]
    bias_ref = ins[1 + 2 * parts]
    mixed_ref, lse_ref = outs
    query, keys, values = query_ref[...], stacked(key_refs), stacked(value_refs)
    values_t = values.astype(F32).T.astype(BF16)
    mixed = []
    for index in range(2):
        scores = nt(keys, head_of(query, index)) * LOG2E + bias_ref[...]
        top = jnp.max(scores, axis=0, keepdims=True)
        weights = jnp.exp2(scores - top)
        total = jnp.sum(weights, axis=0, keepdims=True)
        rows = values_t[index * HEAD_DIM : (index + 1) * HEAD_DIM]
        mixed.append(nn(rows, weights.astype(BF16)) * (1.0 / total))
        lse_ref[index : index + 1, :] = top + jnp.log2(total)
    mixed_ref[...] = jnp.concatenate(mixed, axis=0).T.astype(BF16)


def attend_back_kernel(parts, _, ins, outs):
    query_ref, key_refs, value_refs = ins[0], ins[1 : 1 + parts], ins[1 + parts : 1 + 2 * parts]
    bias_ref, mixed_ref, grad_ref, lse_ref = ins[1 + 2 * parts : 5 + 2 * parts]
    query, keys, values = query_ref[...], stacked(key_refs), stacked(value_refs)
    grad = grad_ref[...]
    keys_t = keys.astype(F32).T.astype(BF16)
    delta_terms = (mixed_ref[...].astype(F32) * grad.astype(F32)).T
    grad_q, grad_k, grad_v = [], 0.0, 0.0
    for index in range(2):
        query_h, grad_h = head_of(query, index), head_of(grad, index)
        scores = nt(keys, query_h) * LOG2E + bias_ref[...]
        probs = jnp.exp2(scores - lse_ref[index : index + 1, :])
        grad_probs = nt(values, grad_h)
        half = slice(index * HEAD_DIM, (index + 1) * HEAD_DIM)
        delta = jnp.sum(delta_terms[half], axis=0, keepdims=True)
        grad_scores = (probs * (grad_probs - delta)).astype(BF16)
        grad_v += nn(probs.astype(BF16), grad_h)
        grad_k += nn(grad_scores, query_h)
        grad_q.append(nn(keys_t[half], grad_scores))
    grad_q = (jnp.concatenate(grad_q, axis=0).T * HEAD_DIM**-0.5).astype(BF16)
    if parts == 1:
        outs[0][0], outs[0][1], outs[0][2] = grad_q, grad_k.astype(BF16), grad_v.astype(BF16)
    else:
        outs[0][...] = grad_q
        outs[1][0], outs[1][1] = grad_k[:EDGE], grad_v[:EDGE]
        outs[2][0], outs[2][1] = grad_k[EDGE:].astype(BF16), grad_v[EDGE:].astype(BF16)


FULL_ROWS = pl.BlockSpec((SPAN, PAIR), lambda j, sc: (0, j))
FULL_LSE = pl.BlockSpec((None, 2, SPAN), lambda j, sc: (j, 0, 0))
FULL_BIAS = pl.BlockSpec((SPAN, SPAN), lambda j, sc: (0, 0))
EDGE_ROWS = pl.BlockSpec((EDGE, PAIR), lambda j, sc: (SPAN // EDGE, j))
EDGE_LSE = pl.BlockSpec((None, 2, EDGE), lambda j, sc: (j, 0, 0))
EDGE_BIAS = pl.BlockSpec((SPAN, EDGE), lambda j, sc: (0, 0))


def far_part(which, pairs):
    return pl.BlockSpec((None, EDGE, PAIR), lambda j, sc: (which, 0, (j + pairs // 2) % pairs))


def attend(query, keys, values, bias, scalars):
    rows, width = query.shape
    inputs = [(a, FULL_ROWS) for a in (query, keys, values)] + [(bias, FULL_BIAS)]
    outputs = [
        (shape((rows, width), BF16), FULL_ROWS),
        (shape((width // PAIR, 2, SPAN), F32), FULL_LSE),
    ]
    kernel = functools.partial(attend_kernel, 1)
    return call(kernel, (width // PAIR,), inputs, outputs, scalars, "attend", us=8)


def attend_edge(query, keys, values, far, bias, mixed, scalars):
    rows, width = query.shape
    pairs = width // PAIR
    inputs = [(query, EDGE_ROWS), (keys, EDGE_ROWS), (far, far_part(0, pairs))]
    inputs += [(values, EDGE_ROWS), (far, far_part(1, pairs)), (bias, EDGE_BIAS), (mixed, UNREAD)]
    outputs = [
        (shape((rows, width), BF16), EDGE_ROWS),
        (shape((pairs, 2, EDGE), F32), EDGE_LSE),
    ]
    kernel = functools.partial(attend_kernel, 2)
    return call(kernel, (pairs,), inputs, outputs, scalars, "attend_edge", aliases={6: 0}, us=7)


def attend_back(query, keys, values, bias, mixed, grad, lse, held, scalars, after):
    rows, width = query.shape
    pairs = width // PAIR
    inputs = [(a, FULL_ROWS) for a in (query, keys, values)] + [(bias, FULL_BIAS)]
    inputs += [(mixed, FULL_ROWS), (grad, FULL_ROWS), (lse, FULL_LSE), (held, UNREAD)]
    outputs = [(shape((3, rows, width), BF16), pl.BlockSpec((3, SPAN, PAIR), lambda j, sc: (0, 0, j)))]
    kernel = functools.partial(attend_back_kernel, 1)
    return call(kernel, (pairs,), inputs, outputs, scalars, "attend_back", after, {7: 0}, us=11)[0]


def attend_edge_back(query, keys, values, far, bias, mixed, grad, lse, scalars, after):
    rows, width = query.shape
    pairs = width // PAIR
    inputs = [(query, EDGE_ROWS), (keys, EDGE_ROWS), (far, far_part(0, pairs))]
    inputs += [(values, EDGE_ROWS), (far, far_part(1, pairs)), (bias, EDGE_BIAS)]
    inputs += [(mixed, EDGE_ROWS), (grad, EDGE_ROWS), (lse, EDGE_LSE)]
    own = pl.BlockSpec((2, EDGE, PAIR), lambda j, sc: (0, 0, j))
    away = pl.BlockSpec((2, EDGE, PAIR), lambda j, sc: (0, 0, (j + pairs // 2) % pairs))
    outputs = [
        (shape((3, rows, width), BF16), pl.BlockSpec((None, EDGE, PAIR), lambda j, sc: (0, SPAN // EDGE, j))),
        (shape((2, EDGE, width), F32), own),
        (shape((2, EDGE, width), BF16), away),
    ]
    kernel = functools.partial(attend_back_kernel, 2)
    return call(kernel, (pairs,), inputs, outputs, scalars, "attend_edge_back", after, us=7)


def merge_edge(near, far, held, scalars, after):
    width = near.shape[2]

    def kernel(_, ins, outs):
        outs[0][...] = (ins[0][...] + ins[1][...].astype(F32)).astype(BF16)

    part = pl.BlockSpec((None, EDGE, width), lambda i, sc: (i, 0, 0))
    into = pl.BlockSpec((None, EDGE, width), lambda i, sc: (1 + i, SPAN // EDGE, 0))
    inputs = [(near, part), (far, part), (held, UNREAD)]
    return call(kernel, (2,), inputs, [(shape(held.shape, BF16), into)], scalars, "merge_edge", after, {2: 0})[0]


def normal_parts(value):
    size = jnp.abs(value)
    t = 1.0 / (1.0 + (0.3275911 * 0.5**0.5) * size)
    bell = jnp.exp2((-0.5 * LOG2E) * (value * value))
    poly = t * (
        0.127414796 + t * (-0.142248368 + t * (0.7107068705 + t * (-0.7265760135 + t * 0.5307027145)))
    )
    tail = poly * bell
    return jnp.where(value >= 0, 1.0 - tail, tail), bell * 0.3989422804014327


def standardize(hidden):
    centred = hidden - jnp.mean(hidden, axis=-1, keepdims=True)
    scale = lax.rsqrt(jnp.mean(centred * centred, axis=-1, keepdims=True) + 1e-05)
    return centred * scale, scale


def standardize_back(grad, xhat, scale):
    mean_grad = jnp.mean(grad, axis=-1, keepdims=True)
    mean_both = jnp.mean(grad * xhat, axis=-1, keepdims=True)
    return scale * (grad - mean_grad - xhat * mean_both)


def add_rows(ref, values):
    @pl.when(pl.program_id(0) == 0)
    def _():
        ref[...] = jnp.zeros_like(ref)

    for row, value in enumerate(values):
        ref[row : row + 1, :] += jnp.sum(value, axis=0, keepdims=True)


CHUNK = 768
B_OUT, GAIN1, SHIFT1, B_DOWN, GAIN2, SHIFT2 = range(6)


def tile_spec(tiles, columns):
    return pl.BlockSpec((EDGE, columns), lambda i, sc: (jnp.minimum(i, tiles - 1), 0))


def fixed_spec(columns):
    return pl.BlockSpec((8, columns), lambda i, sc: (0, 0))


def layer_forward(mixed, tokens, cotangent, live, vectors, up_bias, w_out, w_up, w_down, scalars):
    rows, width = tokens.shape
    tiles, hidden = rows // EDGE, w_up[0].shape[1]
    block = hidden // 4

    def kernel(_, ins, outs, act_all, low_all):
        mixed_ref, tokens_ref, cot_ref, live_ref = ins[:4]
        vecs, bias, wo, wu, wd = ins[4:10], ins[10:12], ins[12:14], ins[14:16], ins[16:18]
        out_ref, act_ref, slope_ref, normed_ref, xhat_ref, scale_ref, grad_ref, low_ref, sums_ref, gw_ref = outs
        step = pl.program_id(0)

        def vec(row):
            return vecs[row][...].astype(F32)[None, :]

        @pl.when(step < tiles)
        def _():
            mine = pl.ds(pl.multiple_of(step * EDGE, EDGE), EDGE)
            local = width // 2
            attn = nn(mixed_ref[:, :local], wo[0][...]) + nn(mixed_ref[:, local:], wo[1][...])
            xhat1, scale1 = standardize(tokens_ref[...].astype(F32) + attn + vec(B_OUT))
            xhat_ref[...] = xhat1
            scale_ref[...] = jnp.broadcast_to(scale1, scale_ref.shape)
            normed = xhat1 * vec(GAIN1) + vec(SHIFT1)
            low = normed.astype(BF16)
            normed_ref[...] = low
            resid2 = normed + vec(B_DOWN)
            for side in range(2):
                for at in range(0, hidden, CHUNK):
                    where = slice(at, at + CHUNK)
                    up = nn(low, wu[side][:, where]) + bias[side][where].astype(F32)[None, :]
                    big, small = normal_parts(up)
                    act = (up * big).astype(BF16)
                    if side == 0:
                        act_ref[:, where] = act
                    else:
                        act_all[mine, where] = act
                    slope_ref[:, side * hidden + at : side * hidden + at + CHUNK] = (big + up * small).astype(BF16)
                    resid2 += nn(act, wd[side][where, :])
            xhat2, scale2 = standardize(resid2)
            out_ref[...] = (xhat2 * vec(GAIN2) + vec(SHIFT2)).astype(BF16)
            grad = cot_ref[...].astype(F32) * live_ref[:, 0:1]
            grad_resid2 = standardize_back(grad * vec(GAIN2), xhat2, scale2)
            grad_ref[...] = grad_resid2
            low_grad = grad_resid2.astype(BF16)
            low_ref[...] = low_grad
            low_all[mine, :] = low_grad
            add_rows(sums_ref, (grad * xhat2, grad, grad_resid2))

        @pl.when(step >= tiles)
        def _():
            units = pl.ds(pl.multiple_of((step - tiles) * block, 128), block)
            gw_ref[...] = tn(act_all[:, units], low_all[...]).astype(BF16)

    there = pl.BlockSpec((EDGE, width), lay(tiles))
    tile = functools.partial(tile_spec, tiles)
    inputs = [(mixed, tile(width)), (tokens, there), (cotangent, there), (live, tile(128))]
    inputs += [(a, WHOLE) for a in (*vectors, *up_bias, *w_out, *w_up, *w_down)]
    outputs = [
        (shape((rows, width), BF16), there),
        (shape((rows, hidden), BF16), tile(hidden)),
        (shape((rows, 2 * hidden), BF16), tile(2 * hidden)),
        (shape((rows, width), BF16), tile(width)),
        (shape((rows, width), F32), tile(width)),
        (shape((rows, 128), F32), tile(128)),
        (shape((rows, width), F32), tile(width)),
        (shape((rows, width), BF16), tile(width)),
        (shape((8, width), F32), fixed_spec(width)),
        (shape((hidden, width), BF16), pl.BlockSpec((block, width), lambda i, sc: (jnp.maximum(i - tiles, 0), 0))),
    ]
    scratch = [pltpu.VMEM((rows, hidden), BF16), pltpu.VMEM((rows, width), BF16)]
    return call(kernel, (tiles + 4,), inputs, outputs, scalars, "layer_forward", scratch=scratch, us=22, limit=40,
                stream=(0, 1, 2, 3), settle=tuple(range(9)))


def layer_backward(
    grad_down, grad_resid2, slope, xhat1, scale1, normed, gain1, w_out, w_up, w_down, scalars, after
):
    rows, width = grad_down.shape
    tiles, hidden = rows // EDGE, w_up[0].shape[1]
    block = width // 2

    def kernel(_, ins, outs, up_all):
        low_ref, grad_ref, slope_ref, xhat_ref, scale_ref, normed_ref, gain_ref = ins[:7]
        wo, wu, wd = ins[7:9], ins[9:11], ins[11:13]
        up_ref, resid_ref, attn_ref, mixed_ref, sums_ref, bias_ref, gw_ref = outs
        step = pl.program_id(0)

        @pl.when(step == 0)
        def _():
            bias_ref[...] = jnp.zeros_like(bias_ref)

        @pl.when(step < tiles)
        def _():
            mine = pl.ds(pl.multiple_of(step * EDGE, EDGE), EDGE)
            low = low_ref[...]
            grad_normed = grad_ref[...]
            for side in range(2):
                for at in range(0, hidden, CHUNK):
                    where = slice(at, at + CHUNK)
                    both = slice(side * hidden + at, side * hidden + at + CHUNK)
                    grad_act = nt(low, wd[side][where, :])
                    grad_up = (grad_act * slope_ref[:, both].astype(F32)).astype(BF16)
                    if side == 0:
                        up_ref[:, where] = grad_up
                    else:
                        up_all[mine, where] = grad_up
                    bias_ref[0:1, both] += jnp.sum(grad_up.astype(F32), axis=0, keepdims=True)
                    grad_normed += nt(grad_up, wu[side][:, where])
            xhat = xhat_ref[...]
            gain = gain_ref[...].astype(F32)[None, :]
            grad_resid1 = standardize_back(grad_normed * gain, xhat, scale_ref[:, 0:1])
            resid_ref[...] = grad_resid1
            grad_attn = grad_resid1.astype(BF16)
            attn_ref[...] = grad_attn
            local = width // 2
            mixed_ref[:, :local] = nt(grad_attn, wo[0][...]).astype(BF16)
            mixed_ref[:, local:] = nt(grad_attn, wo[1][...]).astype(BF16)
            add_rows(sums_ref, (grad_normed * xhat, grad_normed, grad_resid1))

        @pl.when(step >= tiles)
        def _():
            part, piece = (step - tiles) // 2, (step - tiles) % 2
            features = pl.ds(pl.multiple_of(piece * block, 128), block)
            units = pl.ds(pl.multiple_of(part * width, 128), width)
            gw_ref[...] = tn(normed_ref[:, features], up_all[:, units]).astype(BF16)

    tile = functools.partial(tile_spec, tiles)
    inputs = [(grad_down, tile(width)), (grad_resid2, tile(width)), (slope, tile(2 * hidden))]
    inputs += [(xhat1, tile(width)), (scale1, tile(128))]
    inputs += [(a, WHOLE) for a in (normed, gain1, *w_out, *w_up, *w_down)]
    outputs = [
        (shape((rows, hidden), BF16), tile(hidden)),
        (shape((rows, width), F32), tile(width)),
        (shape((rows, width), BF16), tile(width)),
        (shape((rows, width), BF16), tile(width)),
        (shape((8, width), F32), fixed_spec(width)),
        (shape((8, 2 * hidden), F32), fixed_spec(2 * hidden)),
        (shape((hidden, width), BF16), pl.BlockSpec((block, width), lambda i, sc: (jnp.maximum(i - tiles, 0), 0))),
    ]
    scratch = [pltpu.VMEM((rows, hidden), BF16)]
    steps = tiles + hidden // block
    return call(kernel, (steps,), inputs, outputs, scalars, "layer_backward", after, scratch=scratch, us=16, limit=40,
                stream=(0, 1, 2, 3, 4), settle=(0, 1, 2, 3))


def down_gradient(act, grad_down, scalars, after=()):
    rows, width = grad_down.shape
    hidden = act.shape[1]
    block = hidden // 4

    def kernel(_, ins, outs):
        outs[0][...] = tn(ins[0][...], ins[1][...])

    inputs = [
        (act, pl.BlockSpec((rows, block), lambda i, sc: (0, i))),
        (grad_down, pl.BlockSpec((rows, width), lambda i, sc: (0, 0))),
    ]
    outputs = [(shape((hidden, width), F32), pl.BlockSpec((block, width), lambda i, sc: (i, 0)))]
    return call(kernel, (4,), inputs, outputs, scalars, "down_gradient", after, us=3.5, stream=(0, 1))[0]


def up_gradient(normed, grad_up, scalars, after=()):
    rows, width = normed.shape
    parts = grad_up.shape[1] // width
    block = width // 2

    def kernel(_, ins, outs):
        outs[0][...] = tn(ins[0][...], ins[1][...])

    inputs = [
        (normed, pl.BlockSpec((rows, block), lambda i, sc: (0, i % 2))),
        (grad_up, pl.BlockSpec((rows, width), lambda i, sc: (0, i // 2))),
    ]
    outputs = [(shape((parts * width, width), F32), pl.BlockSpec((block, width), lambda i, sc: (i, 0)))]
    return call(kernel, (2 * parts,), inputs, outputs, scalars, "up_gradient", after, us=3.5, stream=(0, 1))[0]


def attention_gradient(x, grads, mixed, grad_attn, half, dtype, scalars, after=()):
    rows, width = x.shape
    local = width // 2

    def kernel(_, ins, outs):
        x_ref, grad_ref, mixed_ref, attn_ref = ins
        out_ref, sums_ref = outs
        step = pl.program_id(0)

        @pl.when(step < 3)
        def _():
            grad = grad_ref[...]
            out_ref[:, :local] = tn(x_ref[:, :local], grad).astype(dtype)
            out_ref[:, local:] = tn(x_ref[:, local:], grad).astype(dtype)
            sums_ref[...] = jnp.broadcast_to(jnp.sum(grad.astype(F32), axis=0, keepdims=True), sums_ref.shape)

        @pl.when(step == 3)
        def _():
            out_ref[...] = tn(mixed_ref[...], attn_ref[...]).astype(dtype)

    inputs = [
        (x, pl.BlockSpec((rows, width), lambda i, sc: (0, 0))),
        (grads, pl.BlockSpec((None, rows, local), lambda i, sc: (jnp.minimum(i, 2), 0, half))),
        (mixed, pl.BlockSpec((rows, local), lambda i, sc: (0, half))),
        (grad_attn, pl.BlockSpec((rows, width), lambda i, sc: (0, 0))),
    ]
    outputs = [
        (shape((4 * local, width), dtype), pl.BlockSpec((local, width), lambda i, sc: (i, 0))),
        (shape((3, 8, local), F32), pl.BlockSpec((None, 8, local), lambda i, sc: (jnp.minimum(i, 2), 0, 0))),
    ]
    return call(kernel, (4,), inputs, outputs, scalars, f"attention_gradient_{half}", after, us=4, stream=(0, 3))


def token_gradient(grads, grad_resid1, w_qkv, scalars, after=()):
    rows, width = grad_resid1.shape
    tiles, local = rows // EDGE, width // 2

    def kernel(_, ins, outs):
        total = ins[1][...]
        for c in range(3):
            total += nt(ins[0][c, :, :local], ins[2][c]) + nt(ins[0][c, :, local:], ins[3][c])
        outs[0][...] = total

    inputs = [
        (grads, pl.BlockSpec((3, EDGE, width), lambda i, sc: (0, i, 0))),
        (grad_resid1, pl.BlockSpec((EDGE, width), lambda i, sc: (i, 0))),
        (w_qkv[0], WHOLE),
        (w_qkv[1], WHOLE),
    ]
    outputs = [(shape((rows, width), F32), pl.BlockSpec((EDGE, width), lay(tiles)))]
    return call(kernel, (tiles,), inputs, outputs, scalars, "token_gradient", after, us=6, stream=(1,), settle=(0,))[0]


TAIL = 16


def parted(value):
    high = value.astype(BF16)
    return high, (value - high.astype(F32)).astype(BF16)


def tails(head_own, head_far, sums_up, sums1, sums2, scalars, after=()):
    local, width = head_own.shape[2], sums1.shape[1]
    units = sums_up.shape[1] // 2

    def kernel(sc, ins, outs):
        second = sc[MP] == 1
        for side, heads in enumerate((ins[0], ins[1])):
            lines = [jnp.concatenate([heads[0, 0:1, :], heads[2, 0:1, :]], axis=1)]
            at = side * units
            lines += [ins[2][0:1, at + c : at + c + width] for c in range(0, units, width)]
            first, last = ins[3][0:3, :], ins[4][0:3, :]
            lines.append(jnp.where(second, first, last) if side == 0 else jnp.where(second, last, first))
            lines.append(jnp.zeros((8 - sum(l.shape[0] for l in lines), width), F32))
            high, low = parted(jnp.concatenate(lines, axis=0))
            outs[side][:8], outs[side][8:] = high, low

    inputs = [(a, WHOLE) for a in (head_own, head_far, sums_up, sums1, sums2)]
    return call(kernel, (1,), inputs, [(shape((TAIL, width), BF16), WHOLE)] * 2, scalars, "tails", after)


def tail_sum(own, came):
    own, came = own.astype(F32), came.astype(F32)
    return (own[:8] + own[8:]) + (came[:8] + came[8:])


def fold(kept, came, step, scalars, name, after, tail=None, carry=()):
    rows, width = kept.shape
    half = rows // 2
    extra = 0 if tail is None else TAIL
    if half % 16:
        total, bit = kept + came[:rows].astype(F32), scalars[BITS + step]
        go = lax.dynamic_slice_in_dim(total, (1 - bit) * half, half).astype(BF16)
        if extra:
            both = tail_sum(tail[0][-TAIL:], tail[1][-TAIL:])
            high = lax.reduce_precision(both, 8, 7)
            go = jnp.concatenate([go, high.astype(BF16), (both - high).astype(BF16)], axis=0)
        return go, lax.dynamic_slice_in_dim(total, bit * half, half), *carry
    inputs = [kept, came] + ([] if tail is None else list(tail))

    def kernel(sc, ins, outs):
        bit = sc[BITS + step]
        stay = pl.ds(pl.multiple_of(bit * half, 16), half)
        go = pl.ds(pl.multiple_of((1 - bit) * half, 16), half)
        outs[0][:half] = (ins[0][go, :] + ins[1][go, :].astype(F32)).astype(BF16)
        outs[1][...] = ins[0][stay, :] + ins[1][stay, :].astype(F32)
        if extra:
            at, to = ins[2].shape[0] - TAIL, ins[3].shape[0] - TAIL
            high, low = parted(tail_sum(ins[2][at:, :], ins[3][to:, :]))
            outs[0][half : half + 8], outs[0][half + 8 :] = high, low

    outputs = [(shape((half + extra, width), BF16), WHOLE), (shape((half, width), F32), WHOLE)]
    return call(kernel, (1,), [(a, WHOLE) for a in inputs], outputs, scalars, name, after, limit=8, carry=carry)


def close(kept, came, scalars, name, after, tail=None, carry=()):
    rows, width = kept.shape
    if rows % 16:
        whole = (kept + came[:rows].astype(F32)).astype(BF16)
        return whole, None if tail is None else tail_sum(tail[0][-TAIL:], tail[1][-TAIL:]), *carry
    inputs = [kept, came] + ([] if tail is None else list(tail))

    def kernel(_, ins, outs):
        outs[0][...] = (ins[0][...] + ins[1][:rows, :].astype(F32)).astype(BF16)
        if tail is not None:
            at, to = ins[2].shape[0] - TAIL, ins[3].shape[0] - TAIL
            outs[1][...] = tail_sum(ins[2][at:, :], ins[3][to:, :])

    outputs = [(shape((rows, width), BF16), WHOLE)]
    if tail is not None:
        outputs.append((shape((8, width), F32), WHOLE))
    found = call(kernel, (1,), [(a, WHOLE) for a in inputs], outputs, scalars, name, after, limit=8, carry=carry)
    return found if tail is not None else (found[0], None, *found[1:])


def join(whole, came, step, scalars, name, after, carry=()):
    rows, width = whole.shape
    if rows % 16:
        ahead = scalars[BITS + step] == 0
        first, last = jnp.where(ahead, whole, came), jnp.where(ahead, came, whole)
        return jnp.concatenate([first, last], axis=0), *carry

    def kernel(sc, ins, outs):
        bit = sc[BITS + step]
        outs[0][pl.ds(pl.multiple_of(bit * rows, 16), rows), :] = ins[0][...]
        outs[0][pl.ds(pl.multiple_of((1 - bit) * rows, 16), rows), :] = ins[1][...]

    outputs = [(shape((2 * rows, width), BF16), WHOLE)]
    inputs = [(whole, WHOLE), (came, WHOLE)]
    return call(kernel, (1,), inputs, outputs, scalars, name, after, limit=8, carry=carry)


def finish(whole, came, kind, scalars, name, after, carry=()):
    rows, width = whole.shape
    block = width // 2
    each = rows // block

    def kernel(sc, ins, outs):
        step = pl.program_id(0)
        here = step // each == sc[BITS]
        rows_of = pl.ds(pl.multiple_of((step % each) * block, 16), block)

        def put(value):
            if kind != "attention":
                outs[0][...] = value
                return

            @pl.when(step < 3)
            def _():
                outs[0][:block], outs[0][block:] = value[:, :block], value[:, block:]

            @pl.when(step == 3)
            def _():
                outs[1][...] = value

        @pl.when(here)
        def _():
            put(ins[0][rows_of, :].astype(F32))

        @pl.when(jnp.logical_not(here))
        def _():
            put(ins[1][rows_of, :].astype(F32))

    if kind == "down":
        outputs = [(shape((2 * rows, width), F32), pl.BlockSpec((block, width), lambda i, sc: (i, 0)))]
    elif kind == "up":
        parts = 2 * rows // width
        outputs = [
            (shape((width, parts * width), F32), pl.BlockSpec((block, width), lambda i, sc: (i % 2, i // 2)))
        ]
    else:
        outputs = [
            (shape((3, width, block), F32), pl.BlockSpec((None, width, block), lambda i, sc: (jnp.minimum(i, 2), 0, 0))),
            (shape((block, width), F32), pl.BlockSpec((block, width), lambda i, sc: (0, 0))),
        ]
    inputs = [(whole, WHOLE), (came, WHOLE)]
    found = call(kernel, (2 * each,), inputs, outputs, scalars, name, after, limit=16, carry=carry, settle=(0, 1))
    return found[: len(outputs)], *found[len(outputs) :]


ORDER = """
a LB a UG b EB a AB ME b AG1 a AG0 b c a b a c b a c b a c b c b c a c c b TG c
""".split()


def program(n_dp):
    steps = n_dp.bit_length() - 1
    assert 1 << steps == n_dp
    orders = (list(range(steps)), [1, 0, *range(2, steps)])

    def swap(array):
        return lax.ppermute(array, "mp", [(0, 1), (1, 0)])

    def partner(array, step):
        pairs = [
            (2 * d + m, 2 * (d ^ (1 << orders[m][step])) + m) for d in range(n_dp) for m in range(2)
        ]
        return lax.ppermute(array, ("dp", "mp"), pairs)

    class Chain:
        def __init__(self, kind, own, came, scalars, tail=None):
            self.kind, self.kept, self.came, self.tail = kind, own, came, tail
            self.scalars, self.step, self.result, self.vectors = scalars, 0, None, None

        def advance(self, after, carry=()):
            step, name, scalars = self.step, f"{self.kind}_{self.step}", self.scalars
            back = 2 * steps - 1 - step
            if step < steps:
                sent, self.kept, *carry = fold(
                    self.kept, self.came, step, scalars, name, after, self.tail, carry
                )
                self.came = partner(sent, step)
                if self.tail is not None:
                    self.tail = (sent, self.came)
            elif step == steps:
                sent, self.vectors, *carry = close(
                    self.kept, self.came, scalars, name, after, self.tail, carry
                )
                self.whole, self.came = sent, partner(sent, back)
            elif back >= 0:
                sent, *carry = join(self.whole, self.came, back + 1, scalars, name, after, carry)
                self.whole, self.came = sent, partner(sent, back)
            else:
                self.result, *carry = finish(self.whole, self.came, self.kind, scalars, name, after, carry)
                sent = self.result[0]
            self.step += 1
            return (sent,), carry

    def per_device(
        tokens, cotangent, mask, lengths, counts, w_qkv, qv_bias, w_out, b_out, gain1, shift1,
        w_up, b_up, w_down, b_down, gain2, shift2,
    ):
        rows, width = tokens.shape
        dp, mp = lax.axis_index("dp"), lax.axis_index("mp")
        local, hidden = qv_bias.shape[1], w_up.shape[1]
        bits = [jnp.where(mp == 0, dp >> orders[0][s], dp >> orders[1][s]) & 1 for s in range(steps)]
        scalars = jnp.stack([mp, lengths[0], counts[0] * lengths[0], *bits]).astype(jnp.int32)

        w_qkv_far, qv_bias_far = swap(w_qkv), swap(qv_bias)
        w_out, w_up, w_down, up_bias = ((w, swap(w)) for w in (w_out, w_up, w_down, b_up))
        vectors = (b_out, gain1, shift1, b_down, gain2, shift2)
        bias_full, bias_edge, live = prepare(mask, rows, scalars)

        held = project(tokens, w_qkv, qv_bias, 0, scalars, ())
        query, keys, values, edge, x = project(tokens, w_qkv_far, qv_bias_far, 1, scalars, held[:4])
        far = swap(edge)
        mixed, lse = attend(query, keys, values, bias_full, scalars)
        mixed, lse_edge = attend_edge(query, keys, values, far, bias_edge, mixed, scalars)
        out, act, slope, normed, xhat1, scale1, grad_resid2, grad_down, sums2, gw = layer_forward(
            mixed, tokens, cotangent, live, vectors, up_bias, w_out, w_up, w_down, scalars
        )
        came = swap(gw)
        own = down_gradient(act, grad_down, scalars, (gw,))

        k = {}
        chains = {"a": Chain("down", own, came, scalars)}

        def run_layer_backward(after):
            k["up"], k["resid"], k["attn"], k["mixed"], k["sums1"], k["sums_up"], k["gw"] = layer_backward(
                grad_down, grad_resid2, slope, xhat1, scale1, normed, gain1, w_out, w_up, w_down, scalars, after
            )
            return (k["resid"],), "gw"

        def run_up_gradient(after):
            own = up_gradient(normed, k["up"], scalars, after)
            chains["b"] = Chain("up", own, k["gw"], scalars)
            return (own,), None

        def run_edge_back(after):
            k["grads"], k["near"], k["far"] = attend_edge_back(
                query, keys, values, far, bias_edge, mixed, k["mixed"], lse_edge, scalars, after
            )
            return (k["near"],), "far"

        def run_back(after):
            k["grads"] = attend_back(
                query, keys, values, bias_full, mixed, k["mixed"], lse, k["grads"], scalars, after
            )
            return (k["grads"],), None

        def run_merge(after):
            k["grads"] = merge_edge(k["near"], k["far"], k["grads"], scalars, after)
            return (k["grads"],), None

        def run_far_gradient(after):
            k["gw"], k["head_far"] = attention_gradient(
                x, k["grads"], mixed, k["attn"], 1, BF16, scalars, after
            )
            return (k["head_far"],), "gw"

        def run_own_gradient(after):
            own, head_own = attention_gradient(x, k["grads"], mixed, k["attn"], 0, F32, scalars, after)
            tail_own, tail_far = tails(head_own, k["head_far"], k["sums_up"], k["sums1"], sums2, scalars)
            chains["c"] = Chain("attention", own, k["gw"], scalars, (tail_own, swap(tail_far)))
            return (own, tail_own), None

        def run_token_gradient(after):
            k["tokens"] = token_gradient(k["grads"], k["resid"], (w_qkv, w_qkv_far), scalars, after)
            return (k["tokens"],), None

        work = {
            "LB": run_layer_backward, "UG": run_up_gradient, "EB": run_edge_back, "AB": run_back,
            "ME": run_merge, "AG1": run_far_gradient, "AG0": run_own_gradient, "TG": run_token_gradient,
        }
        after, leaving = (own,), []
        for name in ORDER:
            if name in work:
                after, left = work[name](after)
                leaving += [] if left is None else [left]
            else:
                after, carried = chains[name].advance(after, [k[n] for n in leaving])
                k.update((n, swap(c)) for n, c in zip(leaving, carried, strict=True))
                leaving = []
        while any(c.result is None for c in chains.values()):
            for c in chains.values():
                if c.result is None:
                    after, _ = c.advance(after)

        vectors = chains["c"].vectors
        head, up = vectors[0].reshape(2, local), vectors[1 : 1 + hidden // width].reshape(-1)
        mine = vectors[1 + hidden // width : 4 + hidden // width]
        other = swap(mine)
        g_gain2, g_shift2, g_b_down = jnp.where(mp == 0, mine, other)
        g_gain1, g_shift1, g_b_out = jnp.where(mp == 0, other, mine)
        gw_qkv, gw_out = chains["c"].result
        return (
            out, k["tokens"], gw_qkv, head, gw_out, g_b_out, g_gain1, g_shift1,
            chains["b"].result[0], up, chains["a"].result[0], g_b_down, g_gain2, g_shift2,
        )

    return per_device


def solution(mesh):
    rows, cols, one = P(("dp", "mp"), None), P(None, "mp"), P()
    in_specs = (
        rows, rows, P("dp"), P("dp"), P("dp"),
        P(None, None, "mp"), cols, P("mp", None), one, one, one,
        cols, P("mp"), P("mp", None), one, one, one,
    )
    out_specs = (
        rows, rows, P(None, None, "mp"), cols, P("mp", None), one, one, one,
        cols, P("mp"), P("mp", None), one, one, one,
    )
    return jax.shard_map(
        program(mesh.shape["dp"]), mesh=mesh, in_specs=in_specs, out_specs=out_specs, check_vma=False
    )
```

```python
import functools

import jax
import jax.numpy as jnp
from jax import lax
from jax.experimental import pallas as pl
from jax.experimental.pallas import tpu as pltpu
from jax.sharding import PartitionSpec as P

HEAD_DIM = 64
PAIR = 2 * HEAD_DIM
SPAN = 512
EDGE = SPAN // 2
LOG2E = 1.4426950408889634
MIB = 1 << 20
BF16 = jnp.bfloat16
F32 = jnp.float32
WHOLE = pl.BlockSpec(memory_space=pltpu.VMEM)
UNREAD = pl.BlockSpec(memory_space=pl.ANY)
FAR = pl.BlockSpec(memory_space=pltpu.HBM)
BIASES = 16
TOKEN = (jax.ShapeDtypeStruct((8, 128), F32), WHOLE)


def shape(dims, dtype):
    return jax.ShapeDtypeStruct(tuple(dims), dtype)


def nn(a, b):
    return lax.dot_general(a, b, (((1,), (0,)), ((), ())), preferred_element_type=F32)


def nt(a, b):
    return lax.dot_general(a, b, (((1,), (1,)), ((), ())), preferred_element_type=F32)


def tn(a, b):
    return lax.dot_general(a, b, (((0,), (0,)), ((), ())), preferred_element_type=F32)


def call(kernel, grid, inputs, outputs, scalars, name, after=(), aliases=None, limit=8, scratch=(), carry=()):
    n_in, n_out = len(inputs), len(outputs)

    def space(spec):
        return None if spec is UNREAD else pltpu.VMEM if spec is WHOLE else pltpu.HBM

    arrays = [a if s is UNREAD else pltpu.with_memory_space_constraint(a, space(s)) for a, s in inputs]
    shapes = [o if s is UNREAD else space(s)(o.shape, o.dtype) for o, s in outputs]
    held = (*after, *carry)
    aliases = {1 + k: v for k, v in (aliases or {}).items()}
    aliases |= {1 + n_in + len(after) + k: n_out + k for k in range(len(carry))}

    def body(scalar_ref, *refs):
        first = n_in + len(held)
        kernel(scalar_ref, refs[:n_in], refs[first : first + n_out], *refs[first + n_out + len(carry) :])

    return pl.pallas_call(
        body,
        grid_spec=pltpu.PrefetchScalarGridSpec(
            num_scalar_prefetch=1,
            grid=grid,
            in_specs=[s for _, s in inputs] + [UNREAD] * len(held),
            out_specs=[s for _, s in outputs] + [UNREAD] * len(carry),
            scratch_shapes=scratch,
        ),
        out_shape=shapes + [shape(a.shape, a.dtype) for a in carry],
        input_output_aliases=aliases,
        compiler_params=pltpu.CompilerParams(vmem_limit_bytes=limit * MIB),
        name=name,
    )(scalars, *arrays, *held)


def const(array):
    return array, pl.BlockSpec(array.shape, lambda i, sc: (0,) * len(array.shape))


def lanes(index, count=PAIR):
    return pl.ds(pl.multiple_of(index * count, 128), count)


MP, LENGTH, LIVE, BITS = range(4)


def lay(tiles):
    return lambda i, sc: ((jnp.minimum(i, tiles - 1) + sc[MP]) % tiles, 0)


def pack(tokens, w_out, qv_bias, b_up, scalars):
    rows, (local, width) = tokens.shape[0], w_out.shape

    def kernel(_, ins, outs):
        up = ins[3][...].astype(F32)[None, :]
        lines = [jnp.concatenate([ins[2][0:1, :], ins[2][1:2, :]], axis=1).astype(F32)]
        lines += [up[:, at : at + width] for at in range(0, up.shape[1], width)]
        lines.append(jnp.zeros((BIASES - len(lines), width), F32))
        outs[0][:local, :] = ins[1][...]
        outs[0][local : local + BIASES, :] = jnp.concatenate(lines, axis=0).astype(BF16)
        outs[0][local + BIASES :, :] = ins[0][...]

    shared = pl.BlockSpec((EDGE, width), lambda i, sc: ((1 - sc[MP]) * (rows // EDGE - 1), 0))
    inputs = [(tokens, shared), *(const(a) for a in (w_out, qv_bias, b_up))]
    outputs = [(shape((local + BIASES + EDGE, width), BF16), WHOLE)]
    return call(kernel, (1,), inputs, outputs, scalars, "pack")[0]


def prepare(mask, rows, scalars, after):
    slots = mask.shape[0]

    def kernel(sc, ins, outs, wide_ref):
        outs[3][...] = jnp.zeros_like(outs[3])
        mp, length = sc[MP], sc[LENGTH]
        place = lax.broadcasted_iota(jnp.int32, (1, slots), 1)
        live = jnp.where((ins[0][...].reshape(1, slots) == 1) & (place < sc[LIVE]), 1.0, 0.0)
        wide_ref[...] = jnp.broadcast_to(live, (128, slots)).T

        def rows_at(start, count):
            return wide_ref[pl.ds(pl.multiple_of(start, EDGE), count), :]

        def sequence(slot):
            return sum((slot >= times * length).astype(jnp.int32) for times in (1, 2, 3))

        def masked(keys, queries, live_keys):
            repeats = [live_keys] * (queries.shape[1] // 128)
            allowed = (sequence(keys) == sequence(queries)) & (
                (jnp.concatenate(repeats, axis=1) > 0.5) | (keys == queries)
            )
            return jnp.where(allowed, 0.0, -1e30).astype(BF16)

        whole = rows_at(mp * (slots - SPAN), SPAN)
        near = rows_at(SPAN + mp * EDGE, EDGE)
        far = rows_at(SPAN + (1 - mp) * EDGE, EDGE)
        outs[2][:SPAN], outs[2][SPAN:] = whole, near
        square = (SPAN, SPAN)
        outs[0][...] = masked(
            lax.broadcasted_iota(jnp.int32, square, 0), lax.broadcasted_iota(jnp.int32, square, 1), whole
        )
        tall = (SPAN, EDGE)
        keys = lax.broadcasted_iota(jnp.int32, tall, 0) + mp * EDGE
        keys = jnp.where(keys >= SPAN, keys - SPAN, keys)
        queries = lax.broadcasted_iota(jnp.int32, tall, 1) + mp * EDGE
        outs[1][...] = masked(keys, queries, jnp.concatenate([near, far], axis=0))

    outputs = [const(shape(dims, BF16)) for dims in ((SPAN, SPAN), (SPAN, EDGE))] + [const(shape((rows, 128), F32))]
    outputs.append(TOKEN)
    scratch = [pltpu.VMEM((slots, 128), F32)]
    return call(kernel, (1,), [const(mask)], outputs, scalars, "prepare", after, limit=12, scratch=scratch)


def biases_of(pack):
    return pack[-BIASES - EDGE : -EDGE, :].astype(F32)


def project(x, weights, packs, copied, scalars, after):
    rows, width = x.shape
    tiles, local = rows // EDGE, weights[0].shape[2]

    def kernel(sc, ins, outs, *done):
        x_ref, own_ref, other_ref, *packs = ins[:5]
        kind = pl.program_id(0)
        copies = [pltpu.make_async_copy(*c) for c in zip(ins[5:], outs[5:], done, strict=True)]

        @pl.when(kind == 0)
        def _():
            for copy in copies:
                copy.start()

        def bias_of(row):
            lines = [biases_of(pack)[0:1, row * local : (row + 1) * local] for pack in packs]
            return jnp.concatenate(lines, axis=1)

        def each_tile(index, finish):
            both = jnp.concatenate([own_ref[...], other_ref[index]], axis=1)
            for tile in range(tiles):
                at = pl.multiple_of(((tile + sc[MP]) % tiles) * EDGE, EDGE)
                block = x_ref[pl.ds(at, EDGE), :]
                outs[index][tile * EDGE : (tile + 1) * EDGE, :] = finish(nn(block, both))
                if index == 0:
                    outs[4][tile * EDGE : (tile + 1) * EDGE, :] = block
            if index > 0:
                outs[3][index - 1] = finish(nn(packs[1][local + BIASES :, :], both))

        finishes = (
            lambda v: (v + bias_of(0)).astype(BF16) * BF16(HEAD_DIM**-0.5),
            lambda v: v.astype(BF16),
            lambda v: (v + bias_of(1)).astype(BF16),
        )
        for index, finish in enumerate(finishes):
            pl.when(kind == index)(functools.partial(each_tile, index, finish))

        @pl.when(kind == 2)
        def _():
            for copy in copies:
                copy.wait()

    wide = shape((rows, 2 * local), BF16)
    outputs = [(wide, WHOLE)] * 3 + [(shape((2, EDGE, 2 * local), BF16), WHOLE), (shape((rows, width), BF16), WHOLE)]
    outputs += [(shape(a.shape, a.dtype), WHOLE) for a in copied]
    inputs = [const(x), (weights[0], pl.BlockSpec((None, width, local), lambda i, sc: (i, 0, 0)))]
    inputs += [(a, WHOLE) for a in (weights[1], *packs)] + [(a, FAR) for a in copied]
    scratch = [pltpu.SemaphoreType.DMA] * len(copied)
    return call(kernel, (3,), inputs, outputs, scalars, "project", after, limit=12, scratch=scratch)


def head_of(pair, index):
    lane = lax.broadcasted_iota(jnp.int32, pair.shape, 1)
    keep = lane < HEAD_DIM if index == 0 else lane >= HEAD_DIM
    return jnp.where(keep, pair, jnp.zeros_like(pair))


def span_rows(edge, ref, far_ref, which, pair):
    if not edge:
        return ref[:SPAN, lanes(pair)]
    return jnp.concatenate([ref[SPAN:, lanes(pair)], far_ref[which, :, lanes(pair)]], axis=0)


def in_turn(count, first, then):
    for i in range(count):
        then(i, first(i))


def staggered(count, first, then):
    ready = first(0)
    for i in range(count):
        following = first(i + 1) if i + 1 < count else None
        then(i, ready)
        ready = following


def attend(query, keys, values, far, bias, held, scalars):
    rows, width = query.shape
    pairs, edge = width // PAIR, far is not None
    group = pairs // 2
    count = EDGE if edge else SPAN
    here = slice(SPAN, SPAN + EDGE) if edge else slice(0, SPAN)

    def kernel(_, ins, outs):
        base = pl.program_id(0) * group
        far_ref = ins[4] if edge else None
        bias = ins[3][...].astype(F32)
        pair_of = [base + p for p in range(group)]
        queries = [ins[0][here, lanes(p)] for p in pair_of]
        keys = [span_rows(edge, ins[1], far_ref, 0, p) for p in pair_of]
        values_t = [span_rows(edge, ins[2], far_ref, 1, p).astype(F32).T.astype(BF16) for p in pair_of]
        mixed = []

        def first(i):
            return nt(keys[i // 2], head_of(queries[i // 2], i % 2))

        def then(i, scores):
            pair, index = pair_of[i // 2], i % 2
            scores = scores * LOG2E + bias
            top = jnp.max(scores, axis=0, keepdims=True)
            weights = jnp.exp2(scores - top)
            total = jnp.sum(weights, axis=0, keepdims=True)
            part = values_t[i // 2][index * HEAD_DIM : (index + 1) * HEAD_DIM]
            mixed.append(nn(part, weights.astype(BF16)) * (1.0 / total))
            outs[1][pair, index : index + 1, :] = top + jnp.log2(total)
            if index == 1:
                outs[0][here, lanes(pair)] = jnp.concatenate(mixed[-2:], axis=0).T.astype(BF16)

        staggered(2 * group, first, then)

    inputs = [(a, WHOLE) for a in (query, keys, values)] + [const(bias)]
    inputs += [(far, WHOLE), (held, WHOLE)] if edge else []
    outputs = [(shape((rows, width), BF16), WHOLE), (shape((pairs, 2, count), F32), WHOLE)]
    name = "attend_edge" if edge else "attend"
    return call(kernel, (2,), inputs, outputs, scalars, name, (), {5: 0} if edge else None, limit=12)


def attend_back(query, keys, values, far, bias, mixed, grad, lse, held, scalars, after):
    rows, width = query.shape
    pairs, edge = width // PAIR, far is not None
    group = pairs // 2
    here = slice(SPAN, SPAN + EDGE) if edge else slice(0, SPAN)

    def kernel(_, ins, outs):
        base = pl.program_id(0) * group
        far_ref = ins[7] if edge else None
        bias, lse_ref = ins[3][...].astype(F32), ins[6]
        loaded = []
        for pair in [base + p for p in range(group)]:
            query, mixed, grad = (ins[i][here, lanes(pair)] for i in (0, 4, 5))
            keys = span_rows(edge, ins[1], far_ref, 0, pair)
            values = span_rows(edge, ins[2], far_ref, 1, pair)
            keys_t = keys.astype(F32).T.astype(BF16)
            delta_terms = (mixed.astype(F32) * grad.astype(F32)).T
            loaded.append((pair, query, grad, keys, values, keys_t, delta_terms))
        grad_q, grad_k, grad_v = [], [], []

        def first(i):
            _, query, grad, keys, values, _, _ = loaded[i // 2]
            query_h, grad_h = head_of(query, i % 2), head_of(grad, i % 2)
            return query_h, grad_h, nt(keys, query_h), nt(values, grad_h)

        def then(i, ready):
            pair, _, _, _, _, keys_t, delta_terms = loaded[i // 2]
            index, (query_h, grad_h, scores, grad_probs) = i % 2, ready
            half = slice(index * HEAD_DIM, (index + 1) * HEAD_DIM)
            probs = jnp.exp2(scores * LOG2E + bias - lse_ref[pair, index : index + 1, :])
            delta = jnp.sum(delta_terms[half], axis=0, keepdims=True)
            grad_scores = (probs * (grad_probs - delta)).astype(BF16)
            grad_v.append(nn(probs.astype(BF16), grad_h))
            grad_k.append(nn(grad_scores, query_h))
            grad_q.append(nn(keys_t[half], grad_scores))
            if index == 0:
                return
            both = jnp.concatenate(grad_q[-2:], axis=0).T * HEAD_DIM**-0.5
            outs[0][0, here, lanes(pair)] = both.astype(BF16)
            away = lanes((pair + group) % pairs)
            for which, parts in enumerate((grad_k, grad_v)):
                value = parts[-2] + parts[-1]
                if edge:
                    outs[1][which, :, lanes(pair)] = value[:EDGE]
                    outs[2][which, :, away] = value[EDGE:].astype(BF16)
                else:
                    outs[0][1 + which, here, lanes(pair)] = value.astype(BF16)

        staggered(2 * group, first, then)

    inputs = [(a, WHOLE) for a in (query, keys, values)] + [const(bias)]
    inputs += [(a, WHOLE) for a in (mixed, grad, lse)]
    inputs.append((far if edge else held, WHOLE))
    outputs = [(shape((3, rows, width), BF16), WHOLE)]
    if edge:
        outputs += [(shape((2, EDGE, width), F32), WHOLE), (shape((2, EDGE, width), BF16), WHOLE)]
    name = "attend_edge_back" if edge else "attend_back"
    return call(kernel, (2,), inputs, outputs, scalars, name, after, None if edge else {7: 0}, limit=12)


def merge_edge(near, far, held, scalars, after):
    def kernel(_, ins, outs):
        for which in range(2):
            total = ins[0][which] + ins[1][which].astype(F32)
            outs[0][1 + which, SPAN:, :] = total.astype(BF16)

    inputs = [(near, WHOLE), (far, WHOLE), (held, WHOLE)]
    return call(kernel, (1,), inputs, [(shape(held.shape, BF16), WHOLE)], scalars, "merge_edge", after, {2: 0})[0]


def normal_parts(value):
    size = jnp.abs(value)
    t = 1.0 / (1.0 + (0.3275911 * 0.5**0.5) * size)
    bell = jnp.exp2((-0.5 * LOG2E) * (value * value))
    poly = t * (
        0.127414796 + t * (-0.142248368 + t * (0.7107068705 + t * (-0.7265760135 + t * 0.5307027145)))
    )
    tail = poly * bell
    return jnp.where(value >= 0, 1.0 - tail, tail), bell * 0.3989422804014327


def standardize(hidden):
    centred = hidden - jnp.mean(hidden, axis=-1, keepdims=True)
    scale = lax.rsqrt(jnp.mean(centred * centred, axis=-1, keepdims=True) + 1e-05)
    return centred * scale, scale


def standardize_back(grad, xhat, scale):
    mean_grad = jnp.mean(grad, axis=-1, keepdims=True)
    mean_both = jnp.mean(grad * xhat, axis=-1, keepdims=True)
    return scale * (grad - mean_grad - xhat * mean_both)


def add_rows(ref, values):
    @pl.when(pl.program_id(0) == 0)
    def _():
        ref[...] = jnp.zeros_like(ref)

    for row, value in enumerate(values):
        ref[row : row + 1, :] += jnp.sum(value, axis=0, keepdims=True)


CHUNK = 768
B_OUT, GAIN1, SHIFT1, B_DOWN, GAIN2, SHIFT2 = range(6)


def tile_of(tiles, columns):
    return pl.BlockSpec((EDGE, columns), lambda i, sc: (jnp.minimum(i, tiles - 1), 0))


def layer_forward(mixed, tokens, cotangent, live, vectors, packs, w_up, w_down, scalars):
    rows, width = tokens.shape
    tiles, hidden = rows // EDGE, w_up[0].shape[1]
    block, local = hidden // 4, width // 2

    def kernel(_, ins, outs, act_all):
        mixed_ref, tokens_ref, cot_ref, live_ref = ins[:4]
        vecs, packs, wu, wd = ins[4:10], ins[10:12], ins[12:14], ins[14:16]
        out_ref, act_ref, slope_ref, normed_ref, xhat_ref, scale_ref, grad_ref, low_ref, sums_ref, gw_ref = outs
        step = pl.program_id(0)

        def vec(row):
            return vecs[row][...].astype(F32)[None, :]

        @pl.when(step < tiles)
        def _():
            mine = pl.ds(pl.multiple_of(step * EDGE, EDGE), EDGE)
            attn = nn(mixed_ref[mine, :local], packs[0][:local, :]) + nn(mixed_ref[mine, local:], packs[1][:local, :])
            biases = [biases_of(pack) for pack in packs]
            xhat1, scale1 = standardize(tokens_ref[...].astype(F32) + attn + vec(B_OUT))
            xhat_ref[mine, :] = xhat1
            scale_ref[mine, :] = jnp.broadcast_to(scale1, (EDGE, 128))
            normed = xhat1 * vec(GAIN1) + vec(SHIFT1)
            low = normed.astype(BF16)
            normed_ref[mine, :] = low
            resid2 = [normed + vec(B_DOWN)]
            parts = [(side, at) for side in range(2) for at in range(0, hidden, CHUNK)]

            def first(i):
                side, at = parts[i]
                return nn(low, wu[side][:, at : at + CHUNK])

            def then(i, up):
                side, at = parts[i]
                where = slice(at, at + CHUNK)
                line = 1 + at // width
                up = up + biases[side][line : line + 1, at % width : at % width + CHUNK]
                big, small = normal_parts(up)
                act = (up * big).astype(BF16)
                if side == 0:
                    act_ref[mine, where] = act
                else:
                    act_all[mine, where] = act
                slope_ref[mine, side * hidden + at : side * hidden + at + CHUNK] = (big + up * small).astype(BF16)
                resid2[0] += nn(act, wd[side][where, :])

            staggered(len(parts), first, then)
            resid2 = resid2[0]
            xhat2, scale2 = standardize(resid2)
            out_ref[...] = (xhat2 * vec(GAIN2) + vec(SHIFT2)).astype(BF16)
            grad = cot_ref[...].astype(F32) * live_ref[:, 0:1]
            grad_resid2 = standardize_back(grad * vec(GAIN2), xhat2, scale2)
            grad_ref[mine, :] = grad_resid2
            low_ref[mine, :] = grad_resid2.astype(BF16)
            add_rows(sums_ref, (grad * xhat2, grad, grad_resid2))

        @pl.when(step >= tiles)
        def _():
            gw_ref[pl.ds(pl.multiple_of((step - tiles) * block, 128), block), :] = tn(
                act_all[:, lanes(step - tiles, block)], low_ref[...]
            ).astype(BF16)

    there = pl.BlockSpec((EDGE, width), lay(tiles))
    inputs = [(mixed, WHOLE), (tokens, there), (cotangent, there), (live, tile_of(tiles, 128))]
    inputs += [const(a) for a in vectors] + [(a, WHOLE) for a in (*packs, *w_up, *w_down)]
    outputs = [
        (shape((rows, width), BF16), there),
        (shape((rows, hidden), BF16), WHOLE),
        (shape((rows, 2 * hidden), BF16), WHOLE),
        (shape((rows, width), BF16), WHOLE),
        (shape((rows, width), F32), WHOLE),
        (shape((rows, 128), F32), WHOLE),
        (shape((rows, width), F32), WHOLE),
        (shape((rows, width), BF16), WHOLE),
        (shape((8, width), F32), WHOLE),
        (shape((hidden, width), BF16), WHOLE),
    ]
    scratch = [pltpu.VMEM((rows, hidden), BF16)]
    return call(kernel, (tiles + 4,), inputs, outputs, scalars, "layer_forward", limit=12, scratch=scratch)


def layer_backward(
    grad_down, grad_resid2, slope, xhat1, scale1, normed, gain1, packs, w_up, w_down, scalars, after
):
    rows, width = grad_down.shape
    tiles, hidden = rows // EDGE, w_up[0].shape[1]
    block, local = width // 2, width // 2
    parts = [(side, at) for side in range(2) for at in range(0, hidden, CHUNK)]

    def kernel(_, ins, outs, up_all, resid_all, gone):
        low_ref, grad_ref, slope_ref, xhat_ref, scale_ref, normed_ref, gain_ref = ins[:7]
        packs, wu, wd = ins[7:9], ins[9:11], ins[11:13]
        up_ref, resid_ref, attn_ref, mixed_ref, sums_ref, bias_ref, gw_ref = outs
        here = [slice(tile * EDGE, (tile + 1) * EDGE) for tile in range(tiles)]
        leaving = [
            pltpu.make_async_copy(resid_all.at[here[t], :], resid_ref.at[here[t], :], gone.at[t]) for t in range(tiles)
        ]
        gain = gain_ref[...].astype(F32)[None, :]
        grad_normed = [grad_ref[mine, :] for mine in here]
        sums, bias = [0.0, 0.0, 0.0], [0.0] * len(parts)

        def first(i):
            tile, (side, at) = i // len(parts), parts[i % len(parts)]
            return nt(low_ref[here[tile], :], wd[side][at : at + CHUNK, :])

        def then(i, grad_act):
            tile, (side, at) = i // len(parts), parts[i % len(parts)]
            mine, where = here[tile], slice(at, at + CHUNK)
            both = slice(side * hidden + at, side * hidden + at + CHUNK)
            grad_up = (grad_act * slope_ref[mine, both].astype(F32)).astype(BF16)
            if side == 0:
                up_ref[mine, where] = grad_up
            else:
                up_all[mine, where] = grad_up
            bias[i % len(parts)] += jnp.sum(grad_up.astype(F32), axis=0, keepdims=True)
            grad_normed[tile] += nt(grad_up, wu[side][:, where])
            if i % len(parts) == len(parts) - 1:
                end(tile)

        def end(tile):
            mine = here[tile]
            xhat = xhat_ref[mine, :]
            grad_resid1 = standardize_back(grad_normed[tile] * gain, xhat, scale_ref[mine, 0:1])
            resid_all[mine, :] = grad_resid1
            leaving[tile].start()
            grad_attn = grad_resid1.astype(BF16)
            attn_ref[mine, :] = grad_attn
            mixed_ref[mine, :local] = nt(grad_attn, packs[0][:local, :]).astype(BF16)
            mixed_ref[mine, local:] = nt(grad_attn, packs[1][:local, :]).astype(BF16)
            for row, value in enumerate((grad_normed[tile] * xhat, grad_normed[tile], grad_resid1)):
                sums[row] += jnp.sum(value, axis=0, keepdims=True)

        in_turn(tiles * len(parts), first, then)
        for row, value in enumerate(sums):
            sums_ref[row : row + 1, :] = value
        for (side, at), value in zip(parts, bias):
            bias_ref[0:1, side * hidden + at : side * hidden + at + CHUNK] = value
        for at in range(0, hidden, block):
            part, piece = at // block // 2, at // block % 2
            gw_ref[at : at + block, :] = tn(
                normed_ref[:, piece * block : (piece + 1) * block], up_all[:, part * width : (part + 1) * width]
            ).astype(BF16)
        for copy in leaving:
            copy.wait()

    inputs = [(a, WHOLE) for a in (grad_down, grad_resid2, slope, xhat1, scale1, normed)]
    inputs += [const(gain1)] + [(a, WHOLE) for a in (*packs, *w_up, *w_down)]
    outputs = [
        (shape((rows, hidden), BF16), WHOLE),
        (shape((rows, width), F32), FAR),
        (shape((rows, width), BF16), WHOLE),
        (shape((rows, width), BF16), WHOLE),
        (shape((8, width), F32), WHOLE),
        (shape((8, 2 * hidden), F32), WHOLE),
        (shape((hidden, width), BF16), WHOLE),
    ]
    scratch = [pltpu.VMEM((rows, hidden), BF16), pltpu.VMEM((rows, width), F32), pltpu.SemaphoreType.DMA((tiles,))]
    return call(kernel, (1,), inputs, outputs, scalars, "layer_backward", after, limit=16, scratch=scratch)


def down_gradient(act, grad_down, scalars, after=()):
    rows, width = grad_down.shape
    hidden = act.shape[1]
    block = hidden // 4

    def kernel(_, ins, outs):
        step = pl.program_id(0)
        rows_of = pl.ds(pl.multiple_of(step * block, 128), block)
        outs[0][rows_of, :] = tn(ins[0][:, lanes(step, block)], ins[1][...])

    inputs, outputs = [(act, WHOLE), (grad_down, WHOLE)], [(shape((hidden, width), F32), WHOLE)]
    return call(kernel, (4,), inputs, outputs, scalars, "down_gradient", after)[0]


def up_gradient(normed, grad_up, scalars, after=()):
    rows, width = normed.shape
    parts = grad_up.shape[1] // width
    block = width // 2

    def kernel(_, ins, outs):
        step = pl.program_id(0)
        rows_of = pl.ds(pl.multiple_of(step * block, 128), block)
        outs[0][rows_of, :] = tn(ins[0][:, lanes(step % 2, block)], ins[1][:, lanes(step // 2, width)])

    inputs, outputs = [(normed, WHOLE), (grad_up, WHOLE)], [(shape((parts * width, width), F32), WHOLE)]
    return call(kernel, (2 * parts,), inputs, outputs, scalars, "up_gradient", after)[0]


def attention_gradient(x, grads, mixed, grad_attn, half, dtype, scalars, after=()):
    rows, width = x.shape
    local = width // 2
    columns = slice(half * local, (half + 1) * local)

    def kernel(_, ins, outs):
        x_ref, grad_ref, mixed_ref, attn_ref = ins
        sums_ref = outs[2]
        step = pl.program_id(0)

        for part in range(3):

            @pl.when(step == part)
            def _():
                mine = slice(part % 2 * local, (part % 2 + 1) * local)
                grad = grad_ref[part, :, columns]
                outs[part // 2][mine, :local] = tn(x_ref[:, :local], grad).astype(dtype)
                outs[part // 2][mine, local:] = tn(x_ref[:, local:], grad).astype(dtype)
                sums_ref[part] = jnp.broadcast_to(jnp.sum(grad.astype(F32), axis=0, keepdims=True), (8, local))

        @pl.when(step == 3)
        def _():
            outs[1][local:, :] = tn(mixed_ref[:, columns], attn_ref[...]).astype(dtype)

    inputs = [(a, WHOLE) for a in (x, grads, mixed, grad_attn)]
    outputs = [(shape((2 * local, width), dtype), WHOLE)] * 2 + [(shape((3, 8, local), F32), WHOLE)]
    return call(kernel, (4,), inputs, outputs, scalars, f"attention_gradient_{half}", after)


def token_gradient(grads, grad_resid1, w_qkv, scalars, after=()):
    rows, width = grad_resid1.shape
    tiles, local = rows // EDGE, width // 2

    def kernel(sc, ins, outs, total):
        kind = pl.program_id(0)
        part = nt(ins[0][kind, :, :local], ins[2][...]) + nt(ins[0][kind, :, local:], ins[3][...])

        @pl.when(kind == 0)
        def _():
            total[...] = ins[1][...] + part

        @pl.when(kind == 1)
        def _():
            total[...] += part

        @pl.when(kind == 2)
        def _():
            for tile in range(tiles):
                at = pl.multiple_of(((tile + sc[MP]) % tiles) * EDGE, EDGE)
                mine = slice(tile * EDGE, (tile + 1) * EDGE)
                outs[0][pl.ds(at, EDGE), :] = total[mine, :] + part[mine]
            outs[1][...] = jnp.zeros_like(outs[1])

    weight = pl.BlockSpec((None, width, local), lambda i, sc: (i, 0, 0))
    inputs = [(grads, WHOLE), const(grad_resid1), (w_qkv[0], weight), (w_qkv[1], weight)]
    outputs = [(shape((rows, width), F32), pl.BlockSpec((rows, width), lambda i, sc: (0, 0))), TOKEN]
    scratch = [pltpu.VMEM((rows, width), F32)]
    return call(kernel, (3,), inputs, outputs, scalars, "token_gradient", after, scratch=scratch, limit=16)


TAIL = 16


def parted(value):
    high = value.astype(BF16)
    return high, (value - high.astype(F32)).astype(BF16)


def tails(head_own, head_far, sums_up, sums1, sums2, scalars, after=()):
    local, width = head_own.shape[2], sums1.shape[1]
    units = sums_up.shape[1] // 2

    def kernel(sc, ins, outs):
        second = sc[MP] == 1
        for side, heads in enumerate((ins[0], ins[1])):
            lines = [jnp.concatenate([heads[0, 0:1, :], heads[2, 0:1, :]], axis=1)]
            at = side * units
            lines += [ins[2][0:1, at + c : at + c + width] for c in range(0, units, width)]
            first, last = ins[3][0:3, :], ins[4][0:3, :]
            lines.append(jnp.where(second, first, last) if side == 0 else jnp.where(second, last, first))
            lines.append(jnp.zeros((8 - sum(l.shape[0] for l in lines), width), F32))
            high, low = parted(jnp.concatenate(lines, axis=0))
            outs[side][:8], outs[side][8:] = high, low

    inputs = [(a, WHOLE) for a in (head_own, head_far, sums_up, sums1, sums2)]
    return call(kernel, (1,), inputs, [(shape((TAIL, width), BF16), WHOLE)] * 2, scalars, "tails", after)


def tail_sum(own, came):
    own, came = own.astype(F32), came.astype(F32)
    return (own[:8] + own[8:]) + (came[:8] + came[8:])


def fold(kept, came, step, scalars, name, after, tail=None, carry=()):
    rows, width = kept.shape
    half = rows // 2
    extra = 0 if tail is None else TAIL
    if half % 16:
        total, bit = kept + came[:rows].astype(F32), scalars[BITS + step]
        go = lax.dynamic_slice_in_dim(total, (1 - bit) * half, half).astype(BF16)
        if extra:
            both = tail_sum(tail[0][-TAIL:], tail[1][-TAIL:])
            high = lax.reduce_precision(both, 8, 7)
            go = jnp.concatenate([go, high.astype(BF16), (both - high).astype(BF16)], axis=0)
        return go, lax.dynamic_slice_in_dim(total, bit * half, half), *carry
    inputs = [kept, came] + ([] if tail is None else list(tail))

    def kernel(sc, ins, outs):
        bit = sc[BITS + step]
        stay = pl.ds(pl.multiple_of(bit * half, 16), half)
        go = pl.ds(pl.multiple_of((1 - bit) * half, 16), half)
        outs[0][:half] = (ins[0][go, :] + ins[1][go, :].astype(F32)).astype(BF16)
        outs[1][...] = ins[0][stay, :] + ins[1][stay, :].astype(F32)
        if extra:
            at, to = ins[2].shape[0] - TAIL, ins[3].shape[0] - TAIL
            high, low = parted(tail_sum(ins[2][at:, :], ins[3][to:, :]))
            outs[0][half : half + 8], outs[0][half + 8 :] = high, low

    outputs = [(shape((half + extra, width), BF16), WHOLE), (shape((half, width), F32), WHOLE)]
    return call(kernel, (1,), [(a, WHOLE) for a in inputs], outputs, scalars, name, after, carry=carry)


def add(own, came, scalars, name, after, tail=None, carry=()):
    rows, width = came.shape[0] - (0 if tail is None else TAIL), own.shape[1]
    if rows % 16:
        whole = (own[:rows].astype(F32) + came[:rows].astype(F32)).astype(BF16)
        return whole, None if tail is None else tail_sum(tail[0][-TAIL:], tail[1][-TAIL:]), *carry

    def kernel(_, ins, outs):
        outs[0][...] = (ins[0][:rows, :].astype(F32) + ins[1][:rows, :].astype(F32)).astype(BF16)
        if tail is not None:
            at, to = ins[2].shape[0] - TAIL, ins[3].shape[0] - TAIL
            outs[1][...] = tail_sum(ins[2][at:, :], ins[3][to:, :])

    inputs = [own, came] + ([] if tail is None else list(tail))
    outputs = [(shape((rows, width), BF16), WHOLE)]
    if tail is not None:
        outputs.append((shape((8, width), F32), WHOLE))
    found = call(kernel, (1,), [(a, WHOLE) for a in inputs], outputs, scalars, name, after, carry=carry)
    return found if tail is not None else (found[0], None, *found[1:])


def add_on(own, came, scalars, name, after, tail, carry=()):
    rows, width = came.shape[0] - TAIL, own.shape[1]
    if rows % 16:
        both = tail_sum(tail[0][-TAIL:], tail[1][-TAIL:])
        high = lax.reduce_precision(both, 8, 7)
        whole = (own[:rows].astype(F32) + came[:rows].astype(F32)).astype(BF16)
        return jnp.concatenate([whole, high.astype(BF16), (both - high).astype(BF16)], axis=0), *carry

    def kernel(_, ins, outs):
        outs[0][:rows] = (ins[0][:rows, :].astype(F32) + ins[1][:rows, :].astype(F32)).astype(BF16)
        at, to = ins[2].shape[0] - TAIL, ins[3].shape[0] - TAIL
        high, low = parted(tail_sum(ins[2][at:, :], ins[3][to:, :]))
        outs[0][rows : rows + 8], outs[0][rows + 8 :] = high, low

    inputs = [(a, WHOLE) for a in (own, came, *tail)]
    outputs = [(shape((rows + TAIL, width), BF16), WHOLE)]
    return call(kernel, (1,), inputs, outputs, scalars, name, after, carry=carry)


def join(whole, came, step, scalars, name, after, carry=()):
    rows, width = whole.shape
    if rows % 16:
        ahead = scalars[BITS + step] == 0
        first, last = jnp.where(ahead, whole, came), jnp.where(ahead, came, whole)
        return jnp.concatenate([first, last], axis=0), *carry

    def kernel(sc, ins, outs):
        bit = sc[BITS + step]
        outs[0][pl.ds(pl.multiple_of(bit * rows, 16), rows), :] = ins[0][...]
        outs[0][pl.ds(pl.multiple_of((1 - bit) * rows, 16), rows), :] = ins[1][...]

    outputs = [(shape((2 * rows, width), BF16), WHOLE)]
    inputs = [(whole, WHOLE), (came, WHOLE)]
    return call(kernel, (1,), inputs, outputs, scalars, name, after, carry=carry)


def put(rows_in, mine, kind, held, scalars, name, after, carry=()):
    rows, width = rows_in.shape
    block = width // 2
    each = rows // block

    def kernel(sc, ins, outs, ready, done):
        here = sc[BITS] if mine else 1 - sc[BITS]

        def target(half, index):
            part = half * each + index
            if kind == "down":
                return outs[0].at[part * block : (part + 1) * block, :]
            if kind == "up":
                return outs[0].at[part % 2 * block : (part % 2 + 1) * block, part // 2 * width : (part // 2 + 1) * width]
            return outs[0].at[part + (0 if kind == "queries" else 2)] if kind == "queries" or part == 0 else outs[1]

        copies = []
        for index in range(each):
            value = ins[0][index * block : (index + 1) * block, :].astype(F32)
            for half in range(2):
                to = target(half, index)
                folded = to.shape[-1] == block
                source = ready[1].at[index] if folded else ready[0].at[index]
                copies.append((half, pltpu.make_async_copy(source, to, done.at[index])))

            def store(folded, index=index, value=value):
                if folded:
                    ready[1][index, :block, :], ready[1][index, block:, :] = value[:, :block], value[:, block:]
                else:
                    ready[0][index] = value

            for half in range(2):

                @pl.when(here == half)
                def _():
                    store(target(half, index).shape[-1] == block)
                    copies[2 * index + half][1].start()

        for half, copy in copies:
            pl.when(here == half)(copy.wait)
        outs[-1][...] = jnp.zeros_like(outs[-1])

    if kind == "down":
        shapes = [(2 * rows, width)]
    elif kind == "up":
        shapes = [(width, 2 * rows // width * width)]
    else:
        shapes = [(3, width, block), (block, width)]
    outputs = [(shape(dims, F32), FAR) for dims in shapes] + [TOKEN]
    inputs = [(rows_in, WHOLE), *((h, FAR) for h in held)]
    aliases = {1 + i: i for i in range(len(held))}
    scratch = [
        [pltpu.VMEM((each, block, width), F32), pltpu.VMEM((each, width, block), F32)],
        pltpu.SemaphoreType.DMA((each,)),
    ]
    found = call(kernel, (1,), inputs, outputs, scalars, name, after, aliases, scratch=scratch, carry=carry, limit=16)
    return found[: len(shapes)], found[len(shapes)], *found[len(outputs) :]


ORDER = """
a LB a UG EB a b AB a ME AG1 b AG0 c b d a b a d b c d a c d b TG c b d c d c a d c b d c
""".split()


def program(n_dp):
    steps = n_dp.bit_length() - 1
    assert 1 << steps == n_dp
    orders = (list(range(steps)), [1, 0, *range(2, steps)])

    def swap(array):
        return lax.ppermute(array, "mp", [(0, 1), (1, 0)])

    def partner(array, step):
        pairs = [
            (2 * d + m, 2 * (d ^ (1 << orders[m][step])) + m) for d in range(n_dp) for m in range(2)
        ]
        return lax.ppermute(array, ("dp", "mp"), pairs)

    halvings = max(steps - 1, 0)

    class Chain:
        def __init__(self, kind, own, came, scalars, shared, tail=None):
            self.kind, self.kept, self.came, self.tail, self.shared = kind, own, came, tail, shared
            self.scalars, self.step, self.result, self.vectors = scalars, 0, None, None

        def send(self, sent, bit):
            self.came = partner(sent, bit)
            self.step += 1
            if self.tail is not None:
                self.tail = (sent, self.came)
            return (sent,)

        def advance(self, after, carry=()):
            step, name, scalars = self.step, f"{self.kind}_{self.step}", self.scalars
            back = halvings - 1 - (step - steps)
            if step < halvings:
                sent, self.kept, *carry = fold(
                    self.kept, self.came, step, scalars, name, after, self.tail, carry
                )
                return self.send(sent, step), carry
            if step < steps:
                if self.tail is None:
                    sent, _, *carry = add(self.kept, self.came, scalars, name, after, None, carry)
                else:
                    sent, *carry = add_on(self.kept, self.came, scalars, name, after, self.tail, carry)
                self.kept = sent
                return self.send(sent, step), carry
            if step == steps:
                sent, self.vectors, *carry = add(
                    self.kept, self.came, scalars, name, after, self.tail, carry
                )
                self.tail = None
            elif back >= 0:
                sent, *carry = join(self.whole, self.came, back + 1, scalars, name, after, carry)
            else:
                held = self.result_half if self.kind in ("down", "up") else self.shared
                found, token, *carry = put(self.came, False, self.kind, held, scalars, name, after, carry)
                self.result = found
                if self.kind not in ("down", "up"):
                    self.shared[:] = found
                return (token,), carry
            self.whole = sent
            after = self.send(sent, back)
            if back == 0:
                held = () if self.kind in ("down", "up") else self.shared
                found, token = put(self.whole, True, self.kind, held, scalars, name + "_own", after)
                if self.kind in ("down", "up"):
                    self.result_half = found
                else:
                    self.shared[:] = found
                after = (token,)
            return after, carry

    def per_device(
        tokens, cotangent, mask, lengths, counts, w_qkv, qv_bias, w_out, b_out, gain1, shift1,
        w_up, b_up, w_down, b_down, gain2, shift2,
    ):
        rows, width = tokens.shape
        dp, mp = lax.axis_index("dp"), lax.axis_index("mp")
        local, hidden = qv_bias.shape[1], w_up.shape[1]
        bits = [jnp.where(mp == 0, dp >> orders[0][s], dp >> orders[1][s]) & 1 for s in range(steps)]
        scalars = jnp.stack([mp, lengths[0], counts[0] * lengths[0], *bits]).astype(jnp.int32)

        w_qkv = (w_qkv, swap(w_qkv))
        vectors = (b_out, gain1, shift1, b_down, gain2, shift2)
        mine = pack(tokens, w_out, qv_bias, b_up, mp.astype(jnp.int32)[None])
        packs = (mine, swap(mine))
        bias_full, bias_edge, live, token = prepare(mask, rows, scalars, (mine,))
        query, keys, values, far, x, w_up, w_down = project(
            tokens, w_qkv, packs, (w_up, w_down), scalars, (token,)
        )
        w_up, w_down = ((w, swap(w)) for w in (w_up, w_down))
        mixed, lse = attend(query, keys, values, None, bias_full, None, scalars)
        mixed, lse_edge = attend(query, keys, values, far, bias_edge, mixed, scalars)
        out, act, slope, normed, xhat1, scale1, grad_resid2, grad_down, sums2, gw = layer_forward(
            mixed, tokens, cotangent, live, vectors, packs, w_up, w_down, scalars
        )
        came = swap(gw)
        own = down_gradient(act, grad_down, scalars, (gw,))

        k = {}
        chains, shared = {"a": Chain("down", own, came, scalars, None)}, []

        def run_layer_backward(after):
            k["up"], k["resid"], k["attn"], k["mixed"], k["sums1"], k["sums_up"], k["gw"] = layer_backward(
                grad_down, grad_resid2, slope, xhat1, scale1, normed, gain1, packs, w_up, w_down, scalars, after
            )
            return (k["sums1"],), ("gw",)

        def run_up_gradient(after):
            own = up_gradient(normed, k["up"], scalars, after)
            chains["b"] = Chain("up", own, k["gw"], scalars, None)
            return (own,), None

        def run_edge_back(after):
            k["grads"], k["near"], k["far"] = attend_back(
                query, keys, values, far, bias_edge, mixed, k["mixed"], lse_edge, None, scalars, after
            )
            return (k["near"],), ("far",)

        def run_back(after):
            k["grads"] = attend_back(
                query, keys, values, None, bias_full, mixed, k["mixed"], lse, k["grads"], scalars, after
            )[0]
            return (k["grads"],), None

        def run_merge(after):
            k["grads"] = merge_edge(k["near"], k["far"], k["grads"], scalars, after)
            return (k["grads"],), None

        def run_far_gradient(after):
            k["gw"], k["gw_last"], k["head_far"] = attention_gradient(
                x, k["grads"], mixed, k["attn"], 1, BF16, scalars, after
            )
            return (k["head_far"],), ("gw", "gw_last")

        def run_own_gradient(after):
            own, last, head_own = attention_gradient(x, k["grads"], mixed, k["attn"], 0, F32, scalars, after)
            tail_own, tail_far = tails(head_own, k["head_far"], k["sums_up"], k["sums1"], sums2, scalars)
            chains["c"] = Chain("queries", own, k["gw"], scalars, shared)
            chains["d"] = Chain("values", last, k["gw_last"], scalars, shared, (tail_own, swap(tail_far)))
            return (own, tail_own), None

        def run_token_gradient(after):
            k["tokens"], token = token_gradient(k["grads"], k["resid"], w_qkv, scalars, after)
            return (token,), None

        work = {
            "LB": run_layer_backward, "UG": run_up_gradient, "EB": run_edge_back, "AB": run_back,
            "ME": run_merge, "AG1": run_far_gradient, "AG0": run_own_gradient, "TG": run_token_gradient,
        }
        after, leaving = (own,), []
        for name in ORDER:
            if name in work:
                after, left = work[name](after)
                leaving += left or ()
            else:
                after, carried = chains[name].advance(after, [k[n] for n in leaving])
                k.update((n, swap(c)) for n, c in zip(leaving, carried, strict=True))
                leaving = []
        while any(c.result is None for c in chains.values()):
            for c in chains.values():
                if c.result is None:
                    after, _ = c.advance(after)

        vectors = chains["d"].vectors
        head, up = vectors[0].reshape(2, local), vectors[1 : 1 + hidden // width].reshape(-1)
        mine = vectors[1 + hidden // width : 4 + hidden // width]
        other = swap(mine)
        g_gain2, g_shift2, g_b_down = jnp.where(mp == 0, mine, other)
        g_gain1, g_shift1, g_b_out = jnp.where(mp == 0, other, mine)
        gw_qkv, gw_out = shared
        return (
            out, k["tokens"], gw_qkv, head, gw_out, g_b_out, g_gain1, g_shift1,
            chains["b"].result[0], up, chains["a"].result[0], g_b_down, g_gain2, g_shift2,
        )

    return per_device


def solution(mesh):
    rows, cols, one = P(("dp", "mp"), None), P(None, "mp"), P()
    in_specs = (
        rows, rows, P("dp"), P("dp"), P("dp"),
        P(None, None, "mp"), cols, P("mp", None), one, one, one,
        cols, P("mp"), P("mp", None), one, one, one,
    )
    out_specs = (
        rows, rows, P(None, None, "mp"), cols, P("mp", None), one, one, one,
        cols, P("mp"), P("mp", None), one, one, one,
    )
    return jax.shard_map(
        program(mesh.shape["dp"]), mesh=mesh, in_specs=in_specs, out_specs=out_specs, check_vma=False
    )
```

```python
import functools

import jax
import jax.numpy as jnp
from jax import lax
from jax.experimental import pallas as pl
from jax.experimental.pallas import tpu as pltpu
from jax.sharding import PartitionSpec as P

HEAD_DIM = 64
PAIR = 2 * HEAD_DIM
SPAN = 512
EDGE = SPAN // 2
LOG2E = 1.4426950408889634
MIB = 1 << 20
BF16 = jnp.bfloat16
F32 = jnp.float32
WHOLE = pl.BlockSpec(memory_space=pltpu.VMEM)
UNREAD = pl.BlockSpec(memory_space=pl.ANY)
FAR = pl.BlockSpec(memory_space=pltpu.HBM)
BIASES = 16
TOKEN = (jax.ShapeDtypeStruct((8, 128), F32), WHOLE)


def shape(dims, dtype):
    return jax.ShapeDtypeStruct(tuple(dims), dtype)


def nn(a, b):
    return lax.dot_general(a, b, (((1,), (0,)), ((), ())), preferred_element_type=F32)


def nt(a, b):
    return lax.dot_general(a, b, (((1,), (1,)), ((), ())), preferred_element_type=F32)


def tn(a, b):
    return lax.dot_general(a, b, (((0,), (0,)), ((), ())), preferred_element_type=F32)


def call(kernel, grid, inputs, outputs, scalars, name, after=(), aliases=None, limit=8, scratch=(), carry=()):
    n_in, n_out = len(inputs), len(outputs)

    def space(spec):
        return None if spec is UNREAD else pltpu.VMEM if spec is WHOLE else pltpu.HBM

    arrays = [a if s is UNREAD else pltpu.with_memory_space_constraint(a, space(s)) for a, s in inputs]
    shapes = [o if s is UNREAD else space(s)(o.shape, o.dtype) for o, s in outputs]
    held = (*after, *carry)
    aliases = {1 + k: v for k, v in (aliases or {}).items()}
    aliases |= {1 + n_in + len(after) + k: n_out + k for k in range(len(carry))}

    def body(scalar_ref, *refs):
        first = n_in + len(held)
        kernel(scalar_ref, refs[:n_in], refs[first : first + n_out], *refs[first + n_out + len(carry) :])

    return pl.pallas_call(
        body,
        grid_spec=pltpu.PrefetchScalarGridSpec(
            num_scalar_prefetch=1,
            grid=grid,
            in_specs=[s for _, s in inputs] + [UNREAD] * len(held),
            out_specs=[s for _, s in outputs] + [UNREAD] * len(carry),
            scratch_shapes=scratch,
        ),
        out_shape=shapes + [shape(a.shape, a.dtype) for a in carry],
        input_output_aliases=aliases,
        compiler_params=pltpu.CompilerParams(vmem_limit_bytes=limit * MIB),
        name=name,
    )(scalars, *arrays, *held)


def const(array):
    return array, pl.BlockSpec(array.shape, lambda i, sc: (0,) * len(array.shape))


def lanes(index, count=PAIR):
    return pl.ds(pl.multiple_of(index * count, 128), count)


def rows_of(tile):
    return pl.ds(pl.multiple_of(tile * EDGE, EDGE), EDGE)


MP, LENGTH, LIVE, BITS = range(4)


def lay(tiles):
    return lambda i, sc: ((jnp.minimum(i, tiles - 1) + sc[MP]) % tiles, 0)


def pack(tokens, w_out, qv_bias, b_up, scalars):
    rows, (local, width) = tokens.shape[0], w_out.shape

    def kernel(_, ins, outs):
        up = ins[3][...].astype(F32)[None, :]
        lines = [jnp.concatenate([ins[2][0:1, :], ins[2][1:2, :]], axis=1).astype(F32)]
        lines += [up[:, at : at + width] for at in range(0, up.shape[1], width)]
        lines.append(jnp.zeros((BIASES - len(lines), width), F32))
        outs[0][:local, :] = ins[1][...]
        outs[0][local : local + BIASES, :] = jnp.concatenate(lines, axis=0).astype(BF16)
        outs[0][local + BIASES :, :] = ins[0][...]

    shared = pl.BlockSpec((EDGE, width), lambda i, sc: ((1 - sc[MP]) * (rows // EDGE - 1), 0))
    inputs = [(tokens, shared), *(const(a) for a in (w_out, qv_bias, b_up))]
    outputs = [(shape((local + BIASES + EDGE, width), BF16), WHOLE)]
    return call(kernel, (1,), inputs, outputs, scalars, "pack")[0]


def prepare(mask, rows, scalars, after):
    slots = mask.shape[0]

    def kernel(sc, ins, outs, wide_ref):
        outs[3][...] = jnp.zeros_like(outs[3])
        mp, length = sc[MP], sc[LENGTH]
        place = lax.broadcasted_iota(jnp.int32, (1, slots), 1)
        live = jnp.where((ins[0][...].reshape(1, slots) == 1) & (place < sc[LIVE]), 1.0, 0.0)
        wide_ref[...] = jnp.broadcast_to(live, (128, slots)).T

        def rows_at(start, count):
            return wide_ref[pl.ds(pl.multiple_of(start, EDGE), count), :]

        def sequence(slot):
            return sum((slot >= times * length).astype(jnp.int32) for times in (1, 2, 3))

        def masked(keys, queries, live_keys):
            repeats = [live_keys] * (queries.shape[1] // 128)
            allowed = (sequence(keys) == sequence(queries)) & (
                (jnp.concatenate(repeats, axis=1) > 0.5) | (keys == queries)
            )
            return jnp.where(allowed, 0.0, -1e30).astype(BF16)

        whole = rows_at(mp * (slots - SPAN), SPAN)
        near = rows_at(SPAN + mp * EDGE, EDGE)
        far = rows_at(SPAN + (1 - mp) * EDGE, EDGE)
        outs[2][:SPAN], outs[2][SPAN:] = whole, near
        square = (SPAN, SPAN)
        outs[0][...] = masked(
            lax.broadcasted_iota(jnp.int32, square, 0), lax.broadcasted_iota(jnp.int32, square, 1), whole
        )
        tall = (SPAN, EDGE)
        keys = lax.broadcasted_iota(jnp.int32, tall, 0) + mp * EDGE
        keys = jnp.where(keys >= SPAN, keys - SPAN, keys)
        queries = lax.broadcasted_iota(jnp.int32, tall, 1) + mp * EDGE
        outs[1][...] = masked(keys, queries, jnp.concatenate([near, far], axis=0))

    outputs = [(shape(dims, BF16), WHOLE) for dims in ((SPAN, SPAN), (SPAN, EDGE))] + [const(shape((rows, 128), F32))]
    outputs.append(TOKEN)
    scratch = [pltpu.VMEM((slots, 128), F32)]
    return call(kernel, (1,), [const(mask)], outputs, scalars, "prepare", after, limit=12, scratch=scratch)


def biases_of(pack):
    return pack[-BIASES - EDGE : -EDGE, :].astype(F32)


def project(x, weights, packs, copied, scalars, after):
    rows, width = x.shape
    tiles, local = rows // EDGE, weights[0].shape[2]

    def kernel(sc, ins, outs, *done):
        x_ref, own_ref, other_ref, *packs = ins[:5]
        kind = pl.program_id(0)
        copies = [pltpu.make_async_copy(*c) for c in zip(ins[5:], outs[5:], done, strict=True)]

        @pl.when(kind == 0)
        def _():
            for copy in copies:
                copy.start()

        def bias_of(row):
            lines = [biases_of(pack)[0:1, row * local : (row + 1) * local] for pack in packs]
            return jnp.concatenate(lines, axis=1)

        def each_tile(index, finish):
            both = jnp.concatenate([own_ref[...], other_ref[index]], axis=1)
            for tile in range(tiles):
                at = pl.multiple_of(((tile + sc[MP]) % tiles) * EDGE, EDGE)
                block = x_ref[pl.ds(at, EDGE), :]
                outs[index][tile * EDGE : (tile + 1) * EDGE, :] = finish(nn(block, both))
                if index == 0:
                    outs[4][tile * EDGE : (tile + 1) * EDGE, :] = block
            if index > 0:
                outs[3][index - 1] = finish(nn(packs[1][local + BIASES :, :], both))

        finishes = (
            lambda v: (v + bias_of(0)).astype(BF16) * BF16(HEAD_DIM**-0.5),
            lambda v: v.astype(BF16),
            lambda v: (v + bias_of(1)).astype(BF16),
        )
        for index, finish in enumerate(finishes):
            pl.when(kind == index)(functools.partial(each_tile, index, finish))

        @pl.when(kind == 2)
        def _():
            for copy in copies:
                copy.wait()

    wide = shape((rows, 2 * local), BF16)
    outputs = [(wide, WHOLE)] * 3 + [(shape((2, EDGE, 2 * local), BF16), WHOLE), (shape((rows, width), BF16), WHOLE)]
    outputs += [(shape(a.shape, a.dtype), WHOLE) for a in copied]
    inputs = [const(x), (weights[0], pl.BlockSpec((None, width, local), lambda i, sc: (i, 0, 0)))]
    inputs += [(a, WHOLE) for a in (weights[1], *packs)] + [(a, FAR) for a in copied]
    scratch = [pltpu.SemaphoreType.DMA] * len(copied)
    return call(kernel, (3,), inputs, outputs, scalars, "project", after, limit=12, scratch=scratch)


def head_of(pair, index):
    lane = lax.broadcasted_iota(jnp.int32, pair.shape, 1)
    keep = lane < HEAD_DIM if index == 0 else lane >= HEAD_DIM
    return jnp.where(keep, pair, jnp.zeros_like(pair))


def span_rows(edge, ref, far_ref, which, pair):
    if not edge:
        return ref[:SPAN, lanes(pair)]
    return jnp.concatenate([ref[SPAN:, lanes(pair)], far_ref[which, :, lanes(pair)]], axis=0)


def in_turn(count, first, then):
    for i in range(count):
        then(i, first(i))


def staggered(count, first, then):
    ready = first(0)
    for i in range(count):
        following = first(i + 1) if i + 1 < count else None
        then(i, ready)
        ready = following


def attend(query, keys, values, far, bias, held, scalars):
    rows, width = query.shape
    pairs, edge = width // PAIR, far is not None
    group = pairs // 2
    count = EDGE if edge else SPAN
    here = slice(SPAN, SPAN + EDGE) if edge else slice(0, SPAN)

    def kernel(_, ins, outs):
        pl.loop(0, 2)(functools.partial(some, ins, outs))

    def some(ins, outs, half):
        base = half * group
        far_ref = ins[4] if edge else None
        bias = ins[3][...].astype(F32)
        pair_of = [base + p for p in range(group)]
        queries = [ins[0][here, lanes(p)] for p in pair_of]
        keys = [span_rows(edge, ins[1], far_ref, 0, p) for p in pair_of]
        values_t = [span_rows(edge, ins[2], far_ref, 1, p).astype(F32).T.astype(BF16) for p in pair_of]
        mixed = []

        def first(i):
            return nt(keys[i // 2], head_of(queries[i // 2], i % 2))

        def then(i, scores):
            pair, index = pair_of[i // 2], i % 2
            scores = scores * LOG2E + bias
            top = jnp.max(scores, axis=0, keepdims=True)
            weights = jnp.exp2(scores - top)
            total = jnp.sum(weights, axis=0, keepdims=True)
            part = values_t[i // 2][index * HEAD_DIM : (index + 1) * HEAD_DIM]
            mixed.append(nn(part, weights.astype(BF16)) * (1.0 / total))
            outs[1][pair, index : index + 1, :] = top + jnp.log2(total)
            if index == 1:
                outs[0][here, lanes(pair)] = jnp.concatenate(mixed[-2:], axis=0).T.astype(BF16)

        staggered(2 * group, first, then)

    inputs = [(a, WHOLE) for a in (query, keys, values, bias)]
    inputs += [(far, WHOLE), (held, WHOLE)] if edge else []
    outputs = [(shape((rows, width), BF16), WHOLE), (shape((pairs, 2, count), F32), WHOLE)]
    name = "attend_edge" if edge else "attend"
    return call(kernel, (1,), inputs, outputs, scalars, name, (), {5: 0} if edge else None, limit=12)


def attend_back(query, keys, values, far, bias, mixed, grad, lse, held, scalars, after):
    rows, width = query.shape
    pairs, edge = width // PAIR, far is not None
    group = pairs // 2
    here = slice(SPAN, SPAN + EDGE) if edge else slice(0, SPAN)

    def kernel(_, ins, outs):
        pl.loop(0, 2)(functools.partial(some, ins, outs))

    def some(ins, outs, half_of_pairs):
        base = half_of_pairs * group
        far_ref = ins[7] if edge else None
        bias, lse_ref = ins[3][...].astype(F32), ins[6]
        loaded = []
        for pair in [base + p for p in range(group)]:
            query, mixed, grad = (ins[i][here, lanes(pair)] for i in (0, 4, 5))
            keys = span_rows(edge, ins[1], far_ref, 0, pair)
            values = span_rows(edge, ins[2], far_ref, 1, pair)
            keys_t = keys.astype(F32).T.astype(BF16)
            delta_terms = (mixed.astype(F32) * grad.astype(F32)).T
            loaded.append((pair, query, grad, keys, values, keys_t, delta_terms))
        grad_q, grad_k, grad_v = [], [], []

        def first(i):
            _, query, grad, keys, values, _, _ = loaded[i // 2]
            query_h, grad_h = head_of(query, i % 2), head_of(grad, i % 2)
            return query_h, grad_h, nt(keys, query_h), nt(values, grad_h)

        def then(i, ready):
            pair, _, _, _, _, keys_t, delta_terms = loaded[i // 2]
            index, (query_h, grad_h, scores, grad_probs) = i % 2, ready
            half = slice(index * HEAD_DIM, (index + 1) * HEAD_DIM)
            probs = jnp.exp2(scores * LOG2E + bias - lse_ref[pair, index : index + 1, :])
            delta = jnp.sum(delta_terms[half], axis=0, keepdims=True)
            grad_scores = (probs * (grad_probs - delta)).astype(BF16)
            grad_v.append(nn(probs.astype(BF16), grad_h))
            grad_k.append(nn(grad_scores, query_h))
            grad_q.append(nn(keys_t[half], grad_scores))
            if index == 0:
                return
            both = jnp.concatenate(grad_q[-2:], axis=0).T * HEAD_DIM**-0.5
            outs[0][0, here, lanes(pair)] = both.astype(BF16)
            away = lanes((pair + group) % pairs)
            for which, parts in enumerate((grad_k, grad_v)):
                value = parts[-2] + parts[-1]
                if edge:
                    outs[1][which, :, lanes(pair)] = value[:EDGE]
                    outs[2][which, :, away] = value[EDGE:].astype(BF16)
                else:
                    outs[0][1 + which, here, lanes(pair)] = value.astype(BF16)

        staggered(2 * group, first, then)

    inputs = [(a, WHOLE) for a in (query, keys, values, bias)]
    inputs += [(a, WHOLE) for a in (mixed, grad, lse)]
    inputs.append((far if edge else held, WHOLE))
    outputs = [(shape((3, rows, width), BF16), WHOLE)]
    if edge:
        outputs += [(shape((2, EDGE, width), F32), WHOLE), (shape((2, EDGE, width), BF16), WHOLE)]
    name = "attend_edge_back" if edge else "attend_back"
    return call(kernel, (1,), inputs, outputs, scalars, name, after, None if edge else {7: 0}, limit=12)


def merge_edge(near, far, held, scalars, after):
    def kernel(_, ins, outs):
        for which in range(2):
            total = ins[0][which] + ins[1][which].astype(F32)
            outs[0][1 + which, SPAN:, :] = total.astype(BF16)

    inputs = [(near, WHOLE), (far, WHOLE), (held, WHOLE)]
    return call(kernel, (1,), inputs, [(shape(held.shape, BF16), WHOLE)], scalars, "merge_edge", after, {2: 0})[0]


def normal_parts(value):
    size = jnp.abs(value)
    t = 1.0 / (1.0 + (0.3275911 * 0.5**0.5) * size)
    bell = jnp.exp2((-0.5 * LOG2E) * (value * value))
    poly = t * (
        0.127414796 + t * (-0.142248368 + t * (0.7107068705 + t * (-0.7265760135 + t * 0.5307027145)))
    )
    tail = poly * bell
    return jnp.where(value >= 0, 1.0 - tail, tail), bell * 0.3989422804014327


def standardize(hidden):
    centred = hidden - jnp.mean(hidden, axis=-1, keepdims=True)
    scale = lax.rsqrt(jnp.mean(centred * centred, axis=-1, keepdims=True) + 1e-05)
    return centred * scale, scale


def standardize_back(grad, xhat, scale):
    mean_grad = jnp.mean(grad, axis=-1, keepdims=True)
    mean_both = jnp.mean(grad * xhat, axis=-1, keepdims=True)
    return scale * (grad - mean_grad - xhat * mean_both)


def add_rows(ref, values):
    @pl.when(pl.program_id(0) == 0)
    def _():
        ref[...] = jnp.zeros_like(ref)

    for row, value in enumerate(values):
        ref[row : row + 1, :] += jnp.sum(value, axis=0, keepdims=True)


CHUNK = 768
B_OUT, GAIN1, SHIFT1, B_DOWN, GAIN2, SHIFT2 = range(6)


def tile_of(tiles, columns):
    return pl.BlockSpec((EDGE, columns), lambda i, sc: (jnp.minimum(i, tiles - 1), 0))


def layer_forward(mixed, x, cotangent, live, vectors, packs, w_up, w_down, scalars):
    rows, width = x.shape
    tiles, hidden = rows // EDGE, w_up[0].shape[1]
    block, local, taken = hidden // 4, width // 2, rows // 2
    parts = [(side, at) for side in range(2) for at in range(0, hidden, CHUNK)]

    def kernel(sc, ins, outs, act_all, cot_all, out_all, come, gone):
        mixed_ref, x_ref, cot_ref, live_ref = ins[:4]
        vecs, packs, wu, wd = ins[4:10], ins[10:12], ins[12:14], ins[14:16]
        out_ref, act_ref, slope_ref, normed_ref, xhat_ref, scale_ref, grad_ref, low_ref, sums_ref, gw_ref = outs
        here = [(rows_of(t), rows_of((t + sc[MP]) % tiles)) for t in range(tiles)]
        arriving = [pltpu.make_async_copy(cot_ref.at[p, :], cot_all.at[l, :], come.at[t]) for t, (l, p) in enumerate(here)]
        for copy in arriving:
            copy.start()
        sums_ref[...] = jnp.zeros_like(sums_ref)

        def vec(row):
            return vecs[row][...].astype(F32)[None, :]

        @pl.loop(0, 2)
        def _(tile):
            mine = pl.ds(pl.multiple_of(tile * taken, 128), taken)
            attn = nn(mixed_ref[mine, :local], packs[0][:local, :]) + nn(mixed_ref[mine, local:], packs[1][:local, :])
            biases = [biases_of(pack) for pack in packs]
            xhat1, scale1 = standardize(x_ref[mine, :].astype(F32) + attn + vec(B_OUT))
            xhat_ref[mine, :] = xhat1
            scale_ref[mine, :] = jnp.broadcast_to(scale1, (taken, 128))
            normed = xhat1 * vec(GAIN1) + vec(SHIFT1)
            low = normed.astype(BF16)
            normed_ref[mine, :] = low
            resid2 = [normed + vec(B_DOWN)]

            def first(i):
                side, at = parts[i]
                return nn(low, wu[side][:, at : at + CHUNK])

            def then(i, up):
                side, at = parts[i]
                where, line = slice(at, at + CHUNK), 1 + at // width
                up = up + biases[side][line : line + 1, at % width : at % width + CHUNK]
                big, small = normal_parts(up)
                act = (up * big).astype(BF16)
                if side == 0:
                    act_ref[mine, where] = act
                else:
                    act_all[mine, where] = act
                slope_ref[mine, side * hidden + at : side * hidden + at + CHUNK] = (big + up * small).astype(BF16)
                resid2[0] += nn(act, wd[side][where, :])

            in_turn(len(parts), first, then)
            xhat2, scale2 = standardize(resid2[0])
            out_all[mine, :] = (xhat2 * vec(GAIN2) + vec(SHIFT2)).astype(BF16)

            @pl.when(tile == 0)
            def _():
                for copy in arriving:
                    copy.wait()

            grad = cot_all[mine, :].astype(F32) * live_ref[mine, 0:1]
            grad_resid2 = standardize_back(grad * vec(GAIN2), xhat2, scale2)
            grad_ref[mine, :] = grad_resid2
            low_ref[mine, :] = grad_resid2.astype(BF16)
            for row, value in enumerate((grad * xhat2, grad, grad_resid2)):
                sums_ref[row : row + 1, :] += jnp.sum(value, axis=0, keepdims=True)

        leaving = [pltpu.make_async_copy(out_all.at[l, :], out_ref.at[p, :], gone.at[t]) for t, (l, p) in enumerate(here)]
        for copy in leaving:
            copy.start()

        @pl.loop(0, hidden // block)
        def _(part):
            gw_ref[pl.ds(pl.multiple_of(part * block, 128), block), :] = tn(
                act_all[:, lanes(part, block)], low_ref[...]
            ).astype(BF16)

        for copy in leaving:
            copy.wait()

    inputs = [(mixed, WHOLE), (x, WHOLE), (cotangent, FAR), const(live)]
    inputs += [const(a) for a in vectors] + [(a, WHOLE) for a in (*packs, *w_up, *w_down)]
    outputs = [
        (shape((rows, width), BF16), FAR),
        (shape((rows, hidden), BF16), WHOLE),
        (shape((rows, 2 * hidden), BF16), WHOLE),
        (shape((rows, width), BF16), WHOLE),
        (shape((rows, width), F32), WHOLE),
        (shape((rows, 128), F32), WHOLE),
        (shape((rows, width), F32), WHOLE),
        (shape((rows, width), BF16), WHOLE),
        (shape((8, width), F32), WHOLE),
        (shape((hidden, width), BF16), WHOLE),
    ]
    scratch = [pltpu.VMEM((rows, hidden), BF16), pltpu.VMEM((rows, width), BF16), pltpu.VMEM((rows, width), BF16)]
    scratch += [pltpu.SemaphoreType.DMA((tiles,))] * 2
    return call(kernel, (1,), inputs, outputs, scalars, "layer_forward", limit=14, scratch=scratch)


def layer_backward(
    grad_down, grad_resid2, slope, xhat1, scale1, normed, gain1, packs, w_up, w_down, scalars, after
):
    rows, width = grad_down.shape
    tiles, hidden = rows // EDGE, w_up[0].shape[1]
    block, local, taken = width // 2, width // 2, rows // 2
    parts = [(side, at) for side in range(2) for at in range(0, hidden, CHUNK)]

    def kernel(_, ins, outs, up_all, resid_all, gone):
        low_ref, grad_ref, slope_ref, xhat_ref, scale_ref, normed_ref, gain_ref = ins[:7]
        packs, wu, wd = ins[7:9], ins[9:11], ins[11:13]
        up_ref, resid_ref, attn_ref, mixed_ref, sums_ref, bias_ref, gw_ref = outs
        gain = gain_ref[...].astype(F32)[None, :]
        sums_ref[...] = jnp.zeros_like(sums_ref)
        bias_ref[...] = jnp.zeros_like(bias_ref)

        @pl.loop(0, 2)
        def _(tile):
            mine = pl.ds(pl.multiple_of(tile * taken, 128), taken)
            low = low_ref[mine, :]
            grad_normed = grad_ref[mine, :]
            for side, at in parts:
                where, both = slice(at, at + CHUNK), slice(side * hidden + at, side * hidden + at + CHUNK)
                grad_act = nt(low, wd[side][where, :])
                grad_up = (grad_act * slope_ref[mine, both].astype(F32)).astype(BF16)
                if side == 0:
                    up_ref[mine, where] = grad_up
                else:
                    up_all[mine, where] = grad_up
                bias_ref[0:1, both] += jnp.sum(grad_up.astype(F32), axis=0, keepdims=True)
                grad_normed += nt(grad_up, wu[side][:, where])
            xhat = xhat_ref[mine, :]
            grad_resid1 = standardize_back(grad_normed * gain, xhat, scale_ref[mine, 0:1])
            resid_all[mine, :] = grad_resid1
            grad_attn = grad_resid1.astype(BF16)
            attn_ref[mine, :] = grad_attn
            mixed_ref[mine, :local] = nt(grad_attn, packs[0][:local, :]).astype(BF16)
            mixed_ref[mine, local:] = nt(grad_attn, packs[1][:local, :]).astype(BF16)
            for row, value in enumerate((grad_normed * xhat, grad_normed, grad_resid1)):
                sums_ref[row : row + 1, :] += jnp.sum(value, axis=0, keepdims=True)

        leaving = pltpu.make_async_copy(resid_all, resid_ref, gone)
        leaving.start()

        @pl.loop(0, hidden // block)
        def _(i):
            gw_ref[pl.ds(pl.multiple_of(i * block, 128), block), :] = tn(
                normed_ref[:, lanes(i % 2, block)], up_all[:, lanes(i // 2, width)]
            ).astype(BF16)

        leaving.wait()

    inputs = [(a, WHOLE) for a in (grad_down, grad_resid2, slope, xhat1, scale1, normed)]
    inputs += [const(gain1)] + [(a, WHOLE) for a in (*packs, *w_up, *w_down)]
    outputs = [
        (shape((rows, hidden), BF16), WHOLE),
        (shape((rows, width), F32), FAR),
        (shape((rows, width), BF16), WHOLE),
        (shape((rows, width), BF16), WHOLE),
        (shape((8, width), F32), WHOLE),
        (shape((8, 2 * hidden), F32), WHOLE),
        (shape((hidden, width), BF16), WHOLE),
    ]
    scratch = [pltpu.VMEM((rows, hidden), BF16), pltpu.VMEM((rows, width), F32), pltpu.SemaphoreType.DMA]
    return call(kernel, (1,), inputs, outputs, scalars, "layer_backward", after, limit=14, scratch=scratch)


def down_gradient(act, grad_down, scalars, after=()):
    rows, width = grad_down.shape
    hidden = act.shape[1]
    block = hidden // 4

    def kernel(_, ins, outs):
        @pl.loop(0, 4)
        def _(i):
            rows_out = pl.ds(pl.multiple_of(i * block, 128), block)
            outs[0][rows_out, :] = tn(ins[0][:, lanes(i, block)], ins[1][...])

    inputs, outputs = [(act, WHOLE), (grad_down, WHOLE)], [(shape((hidden, width), F32), WHOLE)]
    return call(kernel, (1,), inputs, outputs, scalars, "down_gradient", after)[0]


def up_gradient(normed, grad_up, scalars, after=()):
    rows, width = normed.shape
    parts = grad_up.shape[1] // width
    block = width // 2

    def kernel(_, ins, outs):
        @pl.loop(0, 2 * parts)
        def _(i):
            rows_out = pl.ds(pl.multiple_of(i * block, 128), block)
            outs[0][rows_out, :] = tn(ins[0][:, lanes(i % 2, block)], ins[1][:, lanes(i // 2, width)])

    inputs, outputs = [(normed, WHOLE), (grad_up, WHOLE)], [(shape((parts * width, width), F32), WHOLE)]
    return call(kernel, (1,), inputs, outputs, scalars, "up_gradient", after)[0]


def attention_gradient(x, grads, mixed, grad_attn, half, dtype, scalars, after=()):
    rows, width = x.shape
    local = width // 2
    columns = slice(half * local, (half + 1) * local)

    def kernel(_, ins, outs):
        x_ref, grad_ref, mixed_ref, attn_ref = ins
        sums_ref = outs[2]
        for part in range(3):
            mine = slice(part % 2 * local, (part % 2 + 1) * local)
            grad = grad_ref[part, :, columns]
            outs[part // 2][mine, :local] = tn(x_ref[:, :local], grad).astype(dtype)
            outs[part // 2][mine, local:] = tn(x_ref[:, local:], grad).astype(dtype)
            sums_ref[part] = jnp.broadcast_to(jnp.sum(grad.astype(F32), axis=0, keepdims=True), (8, local))
        outs[1][local:, :] = tn(mixed_ref[:, columns], attn_ref[...]).astype(dtype)

    inputs = [(a, WHOLE) for a in (x, grads, mixed, grad_attn)]
    outputs = [(shape((2 * local, width), dtype), WHOLE)] * 2 + [(shape((3, 8, local), F32), WHOLE)]
    return call(kernel, (1,), inputs, outputs, scalars, f"attention_gradient_{half}", after)


def token_gradient(grads, grad_resid1, w_qkv, scalars, after=()):
    rows, width = grad_resid1.shape
    tiles, local = rows // EDGE, width // 2

    def kernel(sc, ins, outs, total, weights, resid, come, gone):
        arriving = [pltpu.make_async_copy(ins[2 + side], weights.at[side], come.at[side]) for side in range(2)]
        arriving.append(pltpu.make_async_copy(ins[1], resid, come.at[2]))
        for copy in arriving:
            copy.start()
        here = [slice(tile * EDGE, (tile + 1) * EDGE) for tile in range(tiles)]

        def part(mine, side):
            columns = slice(side * local, (side + 1) * local)
            return sum(nt(ins[0][k, mine, columns], weights[side, k]) for k in range(3))

        arriving[0].wait()
        for mine in here:
            total[mine, :] = part(mine, 0)
        arriving[1].wait()
        arriving[2].wait()
        leaving = []
        for tile, mine in enumerate(here):
            there = rows_of((tile + sc[MP]) % tiles)
            total[mine, :] += resid[mine, :] + part(mine, 1)
            leaving.append(pltpu.make_async_copy(total.at[mine, :], outs[0].at[there, :], gone.at[tile]))
            leaving[-1].start()
        for copy in leaving:
            copy.wait()
        outs[1][...] = jnp.zeros_like(outs[1])

    inputs = [(grads, WHOLE)] + [(a, FAR) for a in (grad_resid1, *w_qkv)]
    outputs = [(shape((rows, width), F32), FAR), TOKEN]
    scratch = [pltpu.VMEM((rows, width), F32), pltpu.VMEM((2, *w_qkv[0].shape), BF16), pltpu.VMEM((rows, width), F32)]
    scratch += [pltpu.SemaphoreType.DMA((3,)), pltpu.SemaphoreType.DMA((tiles,))]
    return call(kernel, (1,), inputs, outputs, scalars, "token_gradient", after, scratch=scratch, limit=16)


TAIL = 16


def parted(value):
    high = value.astype(BF16)
    return high, (value - high.astype(F32)).astype(BF16)


def tails(head_own, head_far, sums_up, sums1, sums2, scalars, after=()):
    local, width = head_own.shape[2], sums1.shape[1]
    units = sums_up.shape[1] // 2

    def kernel(sc, ins, outs):
        second = sc[MP] == 1
        for side, heads in enumerate((ins[0], ins[1])):
            lines = [jnp.concatenate([heads[0, 0:1, :], heads[2, 0:1, :]], axis=1)]
            at = side * units
            lines += [ins[2][0:1, at + c : at + c + width] for c in range(0, units, width)]
            first, last = ins[3][0:3, :], ins[4][0:3, :]
            lines.append(jnp.where(second, first, last) if side == 0 else jnp.where(second, last, first))
            lines.append(jnp.zeros((8 - sum(l.shape[0] for l in lines), width), F32))
            high, low = parted(jnp.concatenate(lines, axis=0))
            outs[side][:8], outs[side][8:] = high, low

    inputs = [(a, WHOLE) for a in (head_own, head_far, sums_up, sums1, sums2)]
    return call(kernel, (1,), inputs, [(shape((TAIL, width), BF16), WHOLE)] * 2, scalars, "tails", after)


def tail_sum(own, came):
    own, came = own.astype(F32), came.astype(F32)
    return (own[:8] + own[8:]) + (came[:8] + came[8:])


def fold(kept, came, step, scalars, name, after, tail=None, carry=()):
    rows, width = kept.shape
    half = rows // 2
    extra = 0 if tail is None else TAIL
    if half % 16:
        total, bit = kept + came[:rows].astype(F32), scalars[BITS + step]
        go = lax.dynamic_slice_in_dim(total, (1 - bit) * half, half).astype(BF16)
        if extra:
            both = tail_sum(tail[0][-TAIL:], tail[1][-TAIL:])
            high = lax.reduce_precision(both, 8, 7)
            go = jnp.concatenate([go, high.astype(BF16), (both - high).astype(BF16)], axis=0)
        return go, lax.dynamic_slice_in_dim(total, bit * half, half), *carry
    inputs = [kept, came] + ([] if tail is None else list(tail))

    def kernel(sc, ins, outs):
        bit = sc[BITS + step]
        stay = pl.ds(pl.multiple_of(bit * half, 16), half)
        go = pl.ds(pl.multiple_of((1 - bit) * half, 16), half)
        outs[0][:half] = (ins[0][go, :] + ins[1][go, :].astype(F32)).astype(BF16)
        outs[1][...] = ins[0][stay, :] + ins[1][stay, :].astype(F32)
        if extra:
            at, to = ins[2].shape[0] - TAIL, ins[3].shape[0] - TAIL
            high, low = parted(tail_sum(ins[2][at:, :], ins[3][to:, :]))
            outs[0][half : half + 8], outs[0][half + 8 :] = high, low

    outputs = [(shape((half + extra, width), BF16), WHOLE), (shape((half, width), F32), WHOLE)]
    return call(kernel, (1,), [(a, WHOLE) for a in inputs], outputs, scalars, name, after, carry=carry)


def add(own, came, scalars, name, after, tail=None, carry=()):
    rows, width = came.shape[0] - (0 if tail is None else TAIL), own.shape[1]
    if rows % 16:
        whole = (own[:rows].astype(F32) + came[:rows].astype(F32)).astype(BF16)
        return whole, None if tail is None else tail_sum(tail[0][-TAIL:], tail[1][-TAIL:]), *carry

    def kernel(_, ins, outs):
        outs[0][...] = (ins[0][:rows, :].astype(F32) + ins[1][:rows, :].astype(F32)).astype(BF16)
        if tail is not None:
            at, to = ins[2].shape[0] - TAIL, ins[3].shape[0] - TAIL
            outs[1][...] = tail_sum(ins[2][at:, :], ins[3][to:, :])

    inputs = [own, came] + ([] if tail is None else list(tail))
    outputs = [(shape((rows, width), BF16), WHOLE)]
    if tail is not None:
        outputs.append((shape((8, width), F32), WHOLE))
    found = call(kernel, (1,), [(a, WHOLE) for a in inputs], outputs, scalars, name, after, carry=carry)
    return found if tail is not None else (found[0], None, *found[1:])


def add_on(own, came, scalars, name, after, tail, carry=()):
    rows, width = came.shape[0] - TAIL, own.shape[1]
    if rows % 16:
        both = tail_sum(tail[0][-TAIL:], tail[1][-TAIL:])
        high = lax.reduce_precision(both, 8, 7)
        whole = (own[:rows].astype(F32) + came[:rows].astype(F32)).astype(BF16)
        return jnp.concatenate([whole, high.astype(BF16), (both - high).astype(BF16)], axis=0), *carry

    def kernel(_, ins, outs):
        outs[0][:rows] = (ins[0][:rows, :].astype(F32) + ins[1][:rows, :].astype(F32)).astype(BF16)
        at, to = ins[2].shape[0] - TAIL, ins[3].shape[0] - TAIL
        high, low = parted(tail_sum(ins[2][at:, :], ins[3][to:, :]))
        outs[0][rows : rows + 8], outs[0][rows + 8 :] = high, low

    inputs = [(a, WHOLE) for a in (own, came, *tail)]
    outputs = [(shape((rows + TAIL, width), BF16), WHOLE)]
    return call(kernel, (1,), inputs, outputs, scalars, name, after, carry=carry)


def join(whole, came, step, scalars, name, after, carry=()):
    rows, width = whole.shape
    if rows % 16:
        ahead = scalars[BITS + step] == 0
        first, last = jnp.where(ahead, whole, came), jnp.where(ahead, came, whole)
        return jnp.concatenate([first, last], axis=0), *carry

    def kernel(sc, ins, outs):
        bit = sc[BITS + step]
        outs[0][pl.ds(pl.multiple_of(bit * rows, 16), rows), :] = ins[0][...]
        outs[0][pl.ds(pl.multiple_of((1 - bit) * rows, 16), rows), :] = ins[1][...]

    outputs = [(shape((2 * rows, width), BF16), WHOLE)]
    inputs = [(whole, WHOLE), (came, WHOLE)]
    return call(kernel, (1,), inputs, outputs, scalars, name, after, carry=carry)


def put(rows_in, mine, kind, held, scalars, name, after, carry=()):
    rows, width = rows_in.shape
    block = width // 2
    chunk = block // 3
    pieces = rows // chunk

    def kernel(sc, ins, outs, ready, done):
        here = sc[BITS] if mine else 1 - sc[BITS]

        def targets(half, piece):
            part, at = divmod(half * rows + piece * chunk, block)
            left, right = slice(0, block), slice(block, width)
            low, high = slice(at, at + chunk), slice(block + at, block + at + chunk)
            if kind == "down":
                return [(outs[0].at[part * block + at : part * block + at + chunk, :], slice(0, width))]
            if kind == "up":
                row, column = part % 2 * block + at, part // 2 * width
                return [(outs[0].at[row : row + chunk, column : column + width], slice(0, width))]
            if kind == "values" and part == 1:
                return [(outs[1].at[low, :], slice(0, width))]
            which = part if kind == "queries" else 2
            return [(outs[0].at[which, low, :], left), (outs[0].at[which, high, :], right)]

        def copies(half, piece):
            return [
                pltpu.make_async_copy(ready.at[piece * chunk : (piece + 1) * chunk, columns], to, done.at[piece, i])
                for i, (to, columns) in enumerate(targets(half, piece))
            ]

        for piece in range(pieces):
            at = slice(piece * chunk, (piece + 1) * chunk)
            ready[at, :] = ins[0][at, :].astype(F32)
            for half in range(2):

                @pl.when(here == half)
                def _():
                    for copy in copies(half, piece):
                        copy.start()

        outs[-1][...] = jnp.zeros_like(outs[-1])
        for half in range(2):

            @pl.when(here == half)
            def _():
                for piece in range(pieces):
                    for copy in copies(half, piece):
                        copy.wait()

    if kind == "down":
        shapes = [(2 * rows, width)]
    elif kind == "up":
        shapes = [(width, 2 * rows // width * width)]
    else:
        shapes = [(3, width, block), (block, width)]
    outputs = [(shape(dims, F32), FAR) for dims in shapes] + [TOKEN]
    inputs = [(rows_in, WHOLE), *((h, FAR) for h in held)]
    aliases = {1 + i: i for i in range(len(held))}
    scratch = [pltpu.VMEM((rows, width), F32), pltpu.SemaphoreType.DMA((pieces, 2))]
    found = call(kernel, (1,), inputs, outputs, scalars, name, after, aliases, scratch=scratch, carry=carry)
    return found[: len(shapes)], found[len(shapes)], *found[len(outputs) :]


ORDER = """
a LB a UG EB a b AB a ME AG1 b AG0 c b d a b a d b c d a c d b TG c b d c d c a d c b d c
""".split()


def program(n_dp):
    steps = n_dp.bit_length() - 1
    assert 1 << steps == n_dp
    orders = (list(range(steps)), [1, 0, *range(2, steps)])

    def swap(array):
        return lax.ppermute(array, "mp", [(0, 1), (1, 0)])

    def partner(array, step):
        pairs = [
            (2 * d + m, 2 * (d ^ (1 << orders[m][step])) + m) for d in range(n_dp) for m in range(2)
        ]
        return lax.ppermute(array, ("dp", "mp"), pairs)

    halvings = max(steps - 1, 0)

    class Chain:
        def __init__(self, kind, own, came, scalars, shared, tail=None):
            self.kind, self.kept, self.came, self.tail, self.shared = kind, own, came, tail, shared
            self.scalars, self.step, self.result, self.vectors = scalars, 0, None, None

        def send(self, sent, bit):
            self.came = partner(sent, bit)
            self.step += 1
            if self.tail is not None:
                self.tail = (sent, self.came)
            return (sent,)

        def advance(self, after, carry=()):
            step, name, scalars = self.step, f"{self.kind}_{self.step}", self.scalars
            back = halvings - 1 - (step - steps)
            if step < halvings:
                sent, self.kept, *carry = fold(
                    self.kept, self.came, step, scalars, name, after, self.tail, carry
                )
                return self.send(sent, step), carry
            if step < steps:
                if self.tail is None:
                    sent, _, *carry = add(self.kept, self.came, scalars, name, after, None, carry)
                else:
                    sent, *carry = add_on(self.kept, self.came, scalars, name, after, self.tail, carry)
                self.kept = sent
                return self.send(sent, step), carry
            if step == steps:
                sent, self.vectors, *carry = add(
                    self.kept, self.came, scalars, name, after, self.tail, carry
                )
                self.tail = None
            elif back >= 0:
                sent, *carry = join(self.whole, self.came, back + 1, scalars, name, after, carry)
            else:
                held = self.result_half if self.kind in ("down", "up") else self.shared
                found, token, *carry = put(self.came, False, self.kind, held, scalars, name, after, carry)
                self.result = found
                if self.kind not in ("down", "up"):
                    self.shared[:] = found
                return (token,), carry
            self.whole = sent
            after = self.send(sent, back)
            if back == 0:
                held = () if self.kind in ("down", "up") else self.shared
                found, token = put(self.whole, True, self.kind, held, scalars, name + "_own", after)
                if self.kind in ("down", "up"):
                    self.result_half = found
                else:
                    self.shared[:] = found
                after = (token,)
            return after, carry

    def per_device(
        tokens, cotangent, mask, lengths, counts, w_qkv, qv_bias, w_out, b_out, gain1, shift1,
        w_up, b_up, w_down, b_down, gain2, shift2,
    ):
        rows, width = tokens.shape
        dp, mp = lax.axis_index("dp"), lax.axis_index("mp")
        local, hidden = qv_bias.shape[1], w_up.shape[1]
        bits = [jnp.where(mp == 0, dp >> orders[0][s], dp >> orders[1][s]) & 1 for s in range(steps)]
        scalars = jnp.stack([mp, lengths[0], counts[0] * lengths[0], *bits]).astype(jnp.int32)

        w_qkv = (w_qkv, swap(w_qkv))
        vectors = (b_out, gain1, shift1, b_down, gain2, shift2)
        mine = pack(tokens, w_out, qv_bias, b_up, mp.astype(jnp.int32)[None])
        packs = (mine, swap(mine))
        bias_full, bias_edge, live, token = prepare(mask, rows, scalars, (mine,))
        query, keys, values, far, x, w_up, w_down = project(
            tokens, w_qkv, packs, (w_up, w_down), scalars, (token,)
        )
        w_up, w_down = ((w, swap(w)) for w in (w_up, w_down))
        mixed, lse = attend(query, keys, values, None, bias_full, None, scalars)
        mixed, lse_edge = attend(query, keys, values, far, bias_edge, mixed, scalars)
        out, act, slope, normed, xhat1, scale1, grad_resid2, grad_down, sums2, gw = layer_forward(
            mixed, x, cotangent, live, vectors, packs, w_up, w_down, scalars
        )
        came = swap(gw)
        own = down_gradient(act, grad_down, scalars, (gw,))

        k = {}
        chains, shared = {"a": Chain("down", own, came, scalars, None)}, []

        def run_layer_backward(after):
            k["up"], k["resid"], k["attn"], k["mixed"], k["sums1"], k["sums_up"], k["gw"] = layer_backward(
                grad_down, grad_resid2, slope, xhat1, scale1, normed, gain1, packs, w_up, w_down, scalars, after
            )
            return (k["sums1"],), ("gw",)

        def run_up_gradient(after):
            own = up_gradient(normed, k["up"], scalars, after)
            chains["b"] = Chain("up", own, k["gw"], scalars, None)
            return (own,), None

        def run_edge_back(after):
            k["grads"], k["near"], k["far"] = attend_back(
                query, keys, values, far, bias_edge, mixed, k["mixed"], lse_edge, None, scalars, after
            )
            return (k["near"],), ("far",)

        def run_back(after):
            k["grads"] = attend_back(
                query, keys, values, None, bias_full, mixed, k["mixed"], lse, k["grads"], scalars, after
            )[0]
            return (k["grads"],), None

        def run_merge(after):
            k["grads"] = merge_edge(k["near"], k["far"], k["grads"], scalars, after)
            return (k["grads"],), None

        def run_far_gradient(after):
            k["gw"], k["gw_last"], k["head_far"] = attention_gradient(
                x, k["grads"], mixed, k["attn"], 1, BF16, scalars, after
            )
            return (k["head_far"],), ("gw", "gw_last")

        def run_own_gradient(after):
            own, last, head_own = attention_gradient(x, k["grads"], mixed, k["attn"], 0, F32, scalars, after)
            tail_own, tail_far = tails(head_own, k["head_far"], k["sums_up"], k["sums1"], sums2, scalars)
            chains["c"] = Chain("queries", own, k["gw"], scalars, shared)
            chains["d"] = Chain("values", last, k["gw_last"], scalars, shared, (tail_own, swap(tail_far)))
            return (own, tail_own), None

        def run_token_gradient(after):
            k["tokens"], token = token_gradient(k["grads"], k["resid"], w_qkv, scalars, after)
            return (token,), None

        work = {
            "LB": run_layer_backward, "UG": run_up_gradient, "EB": run_edge_back, "AB": run_back,
            "ME": run_merge, "AG1": run_far_gradient, "AG0": run_own_gradient, "TG": run_token_gradient,
        }
        after, leaving = (own,), []
        for name in ORDER:
            if name in work:
                after, left = work[name](after)
                leaving += left or ()
            else:
                after, carried = chains[name].advance(after, [k[n] for n in leaving])
                k.update((n, swap(c)) for n, c in zip(leaving, carried, strict=True))
                leaving = []
        while any(c.result is None for c in chains.values()):
            for c in chains.values():
                if c.result is None:
                    after, _ = c.advance(after)

        vectors = chains["d"].vectors
        head, up = vectors[0].reshape(2, local), vectors[1 : 1 + hidden // width].reshape(-1)
        mine = vectors[1 + hidden // width : 4 + hidden // width]
        other = swap(mine)
        g_gain2, g_shift2, g_b_down = jnp.where(mp == 0, mine, other)
        g_gain1, g_shift1, g_b_out = jnp.where(mp == 0, other, mine)
        gw_qkv, gw_out = shared
        return (
            out, k["tokens"], gw_qkv, head, gw_out, g_b_out, g_gain1, g_shift1,
            chains["b"].result[0], up, chains["a"].result[0], g_b_down, g_gain2, g_shift2,
        )

    return per_device


def solution(mesh):
    rows, cols, one = P(("dp", "mp"), None), P(None, "mp"), P()
    in_specs = (
        rows, rows, P("dp"), P("dp"), P("dp"),
        P(None, None, "mp"), cols, P("mp", None), one, one, one,
        cols, P("mp"), P("mp", None), one, one, one,
    )
    out_specs = (
        rows, rows, P(None, None, "mp"), cols, P("mp", None), one, one, one,
        cols, P("mp"), P("mp", None), one, one, one,
    )
    return jax.shard_map(
        program(mesh.shape["dp"]), mesh=mesh, in_specs=in_specs, out_specs=out_specs, check_vma=False
    )
```

```python
import functools

import jax
import jax.numpy as jnp
from jax import lax
from jax.experimental import pallas as pl
from jax.experimental.pallas import tpu as pltpu
from jax.sharding import PartitionSpec as P

HEAD_DIM = 64
PAIR = 2 * HEAD_DIM
SPAN = 512
EDGE = SPAN // 2
LOG2E = 1.4426950408889634
MIB = 1 << 20
BF16 = jnp.bfloat16
F32 = jnp.float32
WHOLE = pl.BlockSpec(memory_space=pltpu.VMEM)
UNREAD = pl.BlockSpec(memory_space=pl.ANY)
FAR = pl.BlockSpec(memory_space=pltpu.HBM)
BIASES = 16
TOKEN = (jax.ShapeDtypeStruct((8, 128), F32), WHOLE)


def shape(dims, dtype):
    return jax.ShapeDtypeStruct(tuple(dims), dtype)


def nn(a, b):
    return lax.dot_general(a, b, (((1,), (0,)), ((), ())), preferred_element_type=F32)


def nt(a, b):
    return lax.dot_general(a, b, (((1,), (1,)), ((), ())), preferred_element_type=F32)


def tn(a, b):
    return lax.dot_general(a, b, (((0,), (0,)), ((), ())), preferred_element_type=F32)


def call(kernel, grid, inputs, outputs, scalars, name, after=(), aliases=None, limit=8, scratch=(), carry=()):
    n_in, n_out = len(inputs), len(outputs)

    def space(spec):
        return None if spec is UNREAD else pltpu.VMEM if spec is WHOLE else pltpu.HBM

    arrays = [a if s is UNREAD else pltpu.with_memory_space_constraint(a, space(s)) for a, s in inputs]
    shapes = [o if s is UNREAD else space(s)(o.shape, o.dtype) for o, s in outputs]
    held = (*after, *carry)
    fetched = [] if isinstance(scalars, Place) else [scalars]
    aliases = {len(fetched) + k: v for k, v in (aliases or {}).items()}
    aliases |= {len(fetched) + n_in + len(after) + k: n_out + k for k in range(len(carry))}

    def body(*refs):
        place, refs = (refs[0], refs[1:]) if fetched else (scalars, refs)
        first = n_in + len(held)
        kernel(place, refs[:n_in], refs[first : first + n_out], *refs[first + n_out + len(carry) :])

    return pl.pallas_call(
        body,
        grid_spec=pltpu.PrefetchScalarGridSpec(
            num_scalar_prefetch=len(fetched),
            grid=grid,
            in_specs=[s for _, s in inputs] + [UNREAD] * len(held),
            out_specs=[s for _, s in outputs] + [UNREAD] * len(carry),
            scratch_shapes=scratch,
        ),
        out_shape=shapes + [shape(a.shape, a.dtype) for a in carry],
        input_output_aliases=aliases,
        compiler_params=pltpu.CompilerParams(vmem_limit_bytes=limit * MIB),
        name=name,
    )(*fetched, *arrays, *held)


def const(array):
    return array, pl.BlockSpec(array.shape, lambda i, *sc: (0,) * len(array.shape))


def lanes(index, count=PAIR):
    return pl.ds(pl.multiple_of(index * count, 128), count)


def rows_of(tile):
    return pl.ds(pl.multiple_of(tile * EDGE, EDGE), EDGE)


class Place:
    def __init__(self, orders):
        self.orders = orders

    def __getitem__(self, index):
        if index == MP:
            return lax.axis_index("mp")
        dp, (first, second) = lax.axis_index("dp"), (order[index - BITS] for order in self.orders)
        if first == second:
            return (dp >> first) & 1
        return (dp >> jnp.where(lax.axis_index("mp") == 0, first, second)) & 1


MP, LENGTH, LIVE, BITS = range(4)


def lay(tiles):
    return lambda i, *sc: ((jnp.minimum(i, tiles - 1) + sc[0][MP]) % tiles, 0)


def pack(tokens, w_out, qv_bias, b_up, scalars):
    rows, (local, width) = tokens.shape[0], w_out.shape

    def kernel(_, ins, outs):
        up = ins[3][...].astype(F32)[None, :]
        lines = [jnp.concatenate([ins[2][0:1, :], ins[2][1:2, :]], axis=1).astype(F32)]
        lines += [up[:, at : at + width] for at in range(0, up.shape[1], width)]
        lines.append(jnp.zeros((BIASES - len(lines), width), F32))
        outs[0][:local, :] = ins[1][...]
        outs[0][local : local + BIASES, :] = jnp.concatenate(lines, axis=0).astype(BF16)
        outs[0][local + BIASES :, :] = ins[0][...]

    shared = pl.BlockSpec((EDGE, width), lambda i, *sc: ((1 - sc[0][MP]) * (rows // EDGE - 1), 0))
    inputs = [(tokens, shared), *(const(a) for a in (w_out, qv_bias, b_up))]
    outputs = [(shape((local + BIASES + EDGE, width), BF16), WHOLE)]
    return call(kernel, (1,), inputs, outputs, scalars, "pack")[0]


def prepare(mask, rows, scalars, after):
    slots = mask.shape[0]

    def kernel(sc, ins, outs, wide_ref):
        outs[3][...] = jnp.zeros_like(outs[3])
        mp, length = sc[MP], sc[LENGTH]
        place = lax.broadcasted_iota(jnp.int32, (1, slots), 1)
        live = jnp.where((ins[0][...].reshape(1, slots) == 1) & (place < sc[LIVE]), 1.0, 0.0)
        wide_ref[...] = jnp.broadcast_to(live, (128, slots)).T

        def rows_at(start, count):
            return wide_ref[pl.ds(pl.multiple_of(start, EDGE), count), :]

        def sequence(slot):
            return sum((slot >= times * length).astype(jnp.int32) for times in (1, 2, 3))

        def masked(keys, queries, live_keys):
            repeats = [live_keys] * (queries.shape[1] // 128)
            allowed = (sequence(keys) == sequence(queries)) & (
                (jnp.concatenate(repeats, axis=1) > 0.5) | (keys == queries)
            )
            return jnp.where(allowed, 0.0, -1e30).astype(BF16)

        whole = rows_at(mp * (slots - SPAN), SPAN)
        near = rows_at(SPAN + mp * EDGE, EDGE)
        far = rows_at(SPAN + (1 - mp) * EDGE, EDGE)
        outs[2][:SPAN], outs[2][SPAN:] = whole, near
        square = (SPAN, SPAN)
        outs[0][...] = masked(
            lax.broadcasted_iota(jnp.int32, square, 0), lax.broadcasted_iota(jnp.int32, square, 1), whole
        )
        tall = (SPAN, EDGE)
        keys = lax.broadcasted_iota(jnp.int32, tall, 0) + mp * EDGE
        keys = jnp.where(keys >= SPAN, keys - SPAN, keys)
        queries = lax.broadcasted_iota(jnp.int32, tall, 1) + mp * EDGE
        outs[1][...] = masked(keys, queries, jnp.concatenate([near, far], axis=0))

    outputs = [(shape(dims, BF16), WHOLE) for dims in ((SPAN, SPAN), (SPAN, EDGE))] + [const(shape((rows, 128), F32))]
    outputs.append(TOKEN)
    scratch = [pltpu.VMEM((slots, 128), F32)]
    return call(kernel, (1,), [const(mask)], outputs, scalars, "prepare", after, limit=12, scratch=scratch)


def biases_of(pack):
    return pack[-BIASES - EDGE : -EDGE, :].astype(F32)


def project(x, weights, packs, copied, scalars, after):
    rows, width = x.shape
    tiles, local = rows // EDGE, weights[0].shape[2]

    def kernel(sc, ins, outs, *done):
        x_ref, own_ref, other_ref, *packs = ins[:5]
        kind = pl.program_id(0)
        copies = [pltpu.make_async_copy(*c) for c in zip(ins[5:], outs[5:], done, strict=True)]

        @pl.when(kind == 0)
        def _():
            for copy in copies:
                copy.start()

        def bias_of(row):
            lines = [biases_of(pack)[0:1, row * local : (row + 1) * local] for pack in packs]
            return jnp.concatenate(lines, axis=1)

        def each_tile(index, finish):
            both = jnp.concatenate([own_ref[...], other_ref[index]], axis=1)
            for tile in range(tiles):
                at = pl.multiple_of(((tile + sc[MP]) % tiles) * EDGE, EDGE)
                block = x_ref[pl.ds(at, EDGE), :]
                outs[index][tile * EDGE : (tile + 1) * EDGE, :] = finish(nn(block, both))
                if index == 0:
                    outs[4][tile * EDGE : (tile + 1) * EDGE, :] = block
            if index > 0:
                outs[3][index - 1] = finish(nn(packs[1][local + BIASES :, :], both))

        finishes = (
            lambda v: (v + bias_of(0)).astype(BF16) * BF16(HEAD_DIM**-0.5),
            lambda v: v.astype(BF16),
            lambda v: (v + bias_of(1)).astype(BF16),
        )
        for index, finish in enumerate(finishes):
            pl.when(kind == index)(functools.partial(each_tile, index, finish))

        @pl.when(kind == 2)
        def _():
            for copy in copies:
                copy.wait()

    wide = shape((rows, 2 * local), BF16)
    outputs = [(wide, WHOLE)] * 3 + [(shape((2, EDGE, 2 * local), BF16), WHOLE), (shape((rows, width), BF16), WHOLE)]
    outputs += [(shape(a.shape, a.dtype), WHOLE) for a in copied]
    inputs = [const(x), (weights[0], pl.BlockSpec((None, width, local), lambda i, *sc: (i, 0, 0)))]
    inputs += [(a, WHOLE) for a in (weights[1], *packs)] + [(a, FAR) for a in copied]
    scratch = [pltpu.SemaphoreType.DMA] * len(copied)
    return call(kernel, (3,), inputs, outputs, scalars, "project", after, limit=12, scratch=scratch)


def head_of(pair, index):
    lane = lax.broadcasted_iota(jnp.int32, pair.shape, 1)
    keep = lane < HEAD_DIM if index == 0 else lane >= HEAD_DIM
    return jnp.where(keep, pair, jnp.zeros_like(pair))


def span_rows(edge, ref, far_ref, which, pair):
    if not edge:
        return ref[:SPAN, lanes(pair)]
    return jnp.concatenate([ref[SPAN:, lanes(pair)], far_ref[which, :, lanes(pair)]], axis=0)


def in_turn(count, first, then):
    for i in range(count):
        then(i, first(i))


def staggered(count, first, then):
    ready = first(0)
    for i in range(count):
        following = first(i + 1) if i + 1 < count else None
        then(i, ready)
        ready = following


def attend(query, keys, values, far, bias, held, scalars):
    rows, width = query.shape
    pairs, edge = width // PAIR, far is not None
    group = pairs // 2
    count = EDGE if edge else SPAN
    here = slice(SPAN, SPAN + EDGE) if edge else slice(0, SPAN)

    def kernel(_, ins, outs):
        pl.loop(0, 2)(functools.partial(some, ins, outs))

    def some(ins, outs, half):
        base = half * group
        far_ref = ins[4] if edge else None
        bias = ins[3][...].astype(F32)
        pair_of = [base + p for p in range(group)]
        queries = [ins[0][here, lanes(p)] for p in pair_of]
        keys = [span_rows(edge, ins[1], far_ref, 0, p) for p in pair_of]
        values_t = [span_rows(edge, ins[2], far_ref, 1, p).astype(F32).T.astype(BF16) for p in pair_of]
        mixed = []

        def first(i):
            return nt(keys[i // 2], head_of(queries[i // 2], i % 2))

        def then(i, scores):
            pair, index = pair_of[i // 2], i % 2
            scores = scores * LOG2E + bias
            top = jnp.max(scores, axis=0, keepdims=True)
            weights = jnp.exp2(scores - top)
            total = jnp.sum(weights, axis=0, keepdims=True)
            part = values_t[i // 2][index * HEAD_DIM : (index + 1) * HEAD_DIM]
            mixed.append(nn(part, weights.astype(BF16)) * (1.0 / total))
            outs[1][pair, index : index + 1, :] = top + jnp.log2(total)
            if index == 1:
                outs[0][here, lanes(pair)] = jnp.concatenate(mixed[-2:], axis=0).T.astype(BF16)

        staggered(2 * group, first, then)

    inputs = [(a, WHOLE) for a in (query, keys, values, bias)]
    inputs += [(far, WHOLE), (held, WHOLE)] if edge else []
    outputs = [(shape((rows, width), BF16), WHOLE), (shape((pairs, 2, count), F32), WHOLE)]
    name = "attend_edge" if edge else "attend"
    return call(kernel, (1,), inputs, outputs, scalars, name, (), {5: 0} if edge else None, limit=12)


def attend_back(query, keys, values, far, bias, mixed, grad, lse, held, scalars, after):
    rows, width = query.shape
    pairs, edge = width // PAIR, far is not None
    group = pairs // 2
    here = slice(SPAN, SPAN + EDGE) if edge else slice(0, SPAN)

    def kernel(_, ins, outs):
        pl.loop(0, 2)(functools.partial(some, ins, outs))

    def some(ins, outs, half_of_pairs):
        base = half_of_pairs * group
        far_ref = ins[7] if edge else None
        bias, lse_ref = ins[3][...].astype(F32), ins[6]
        loaded = []
        for pair in [base + p for p in range(group)]:
            query, mixed, grad = (ins[i][here, lanes(pair)] for i in (0, 4, 5))
            keys = span_rows(edge, ins[1], far_ref, 0, pair)
            values = span_rows(edge, ins[2], far_ref, 1, pair)
            keys_t = keys.astype(F32).T.astype(BF16)
            delta_terms = (mixed.astype(F32) * grad.astype(F32)).T
            loaded.append((pair, query, grad, keys, values, keys_t, delta_terms))
        grad_q, grad_k, grad_v = [], [], []

        def first(i):
            _, query, grad, keys, values, _, _ = loaded[i // 2]
            query_h, grad_h = head_of(query, i % 2), head_of(grad, i % 2)
            return query_h, grad_h, nt(keys, query_h), nt(values, grad_h)

        def then(i, ready):
            pair, _, _, _, _, keys_t, delta_terms = loaded[i // 2]
            index, (query_h, grad_h, scores, grad_probs) = i % 2, ready
            half = slice(index * HEAD_DIM, (index + 1) * HEAD_DIM)
            probs = jnp.exp2(scores * LOG2E + bias - lse_ref[pair, index : index + 1, :])
            delta = jnp.sum(delta_terms[half], axis=0, keepdims=True)
            grad_scores = (probs * (grad_probs - delta)).astype(BF16)
            grad_v.append(nn(probs.astype(BF16), grad_h))
            grad_k.append(nn(grad_scores, query_h))
            grad_q.append(nn(keys_t[half], grad_scores))
            if index == 0:
                return
            both = jnp.concatenate(grad_q[-2:], axis=0).T * HEAD_DIM**-0.5
            outs[0][0, here, lanes(pair)] = both.astype(BF16)
            away = lanes((pair + group) % pairs)
            for which, parts in enumerate((grad_k, grad_v)):
                value = parts[-2] + parts[-1]
                if edge:
                    outs[1][which, :, lanes(pair)] = value[:EDGE]
                    outs[2][which, :, away] = value[EDGE:].astype(BF16)
                else:
                    outs[0][1 + which, here, lanes(pair)] = value.astype(BF16)

        staggered(2 * group, first, then)

    inputs = [(a, WHOLE) for a in (query, keys, values, bias)]
    inputs += [(a, WHOLE) for a in (mixed, grad, lse)]
    inputs.append((far if edge else held, WHOLE))
    outputs = [(shape((3, rows, width), BF16), WHOLE)]
    if edge:
        outputs += [(shape((2, EDGE, width), F32), WHOLE), (shape((2, EDGE, width), BF16), WHOLE)]
    name = "attend_edge_back" if edge else "attend_back"
    return call(kernel, (1,), inputs, outputs, scalars, name, after, None if edge else {7: 0}, limit=12)


def merge_edge(near, far, held, scalars, after):
    def kernel(_, ins, outs):
        for which in range(2):
            total = ins[0][which] + ins[1][which].astype(F32)
            outs[0][1 + which, SPAN:, :] = total.astype(BF16)

    inputs = [(near, WHOLE), (far, WHOLE), (held, WHOLE)]
    return call(kernel, (1,), inputs, [(shape(held.shape, BF16), WHOLE)], scalars, "merge_edge", after, {2: 0})[0]


def normal_parts(value):
    size = jnp.abs(value)
    t = 1.0 / (1.0 + (0.3275911 * 0.5**0.5) * size)
    bell = jnp.exp2((-0.5 * LOG2E) * (value * value))
    poly = t * (
        0.127414796 + t * (-0.142248368 + t * (0.7107068705 + t * (-0.7265760135 + t * 0.5307027145)))
    )
    tail = poly * bell
    return jnp.where(value >= 0, 1.0 - tail, tail), bell * 0.3989422804014327


def standardize(hidden):
    centred = hidden - jnp.mean(hidden, axis=-1, keepdims=True)
    scale = lax.rsqrt(jnp.mean(centred * centred, axis=-1, keepdims=True) + 1e-05)
    return centred * scale, scale


def standardize_back(grad, xhat, scale):
    mean_grad = jnp.mean(grad, axis=-1, keepdims=True)
    mean_both = jnp.mean(grad * xhat, axis=-1, keepdims=True)
    return scale * (grad - mean_grad - xhat * mean_both)


def add_rows(ref, values):
    @pl.when(pl.program_id(0) == 0)
    def _():
        ref[...] = jnp.zeros_like(ref)

    for row, value in enumerate(values):
        ref[row : row + 1, :] += jnp.sum(value, axis=0, keepdims=True)


CHUNK = 768
B_OUT, GAIN1, SHIFT1, B_DOWN, GAIN2, SHIFT2 = range(6)


def tile_of(tiles, columns):
    return pl.BlockSpec((EDGE, columns), lambda i, *sc: (jnp.minimum(i, tiles - 1), 0))


def layer_forward(mixed, x, cotangent, live, vectors, packs, w_up, w_down, scalars):
    rows, width = x.shape
    tiles, hidden = rows // EDGE, w_up[0].shape[1]
    block, local, taken = hidden // 4, width // 2, rows // 2
    parts = [(side, at) for side in range(2) for at in range(0, hidden, CHUNK)]

    def kernel(sc, ins, outs, act_all, cot_all, out_all, come, gone):
        mixed_ref, x_ref, cot_ref, live_ref = ins[:4]
        vecs, packs, wu, wd = ins[4:10], ins[10:12], ins[12:14], ins[14:16]
        out_ref, act_ref, slope_ref, normed_ref, xhat_ref, scale_ref, grad_ref, low_ref, sums_ref, gw_ref = outs
        here = [(rows_of(t), rows_of((t + sc[MP]) % tiles)) for t in range(tiles)]
        arriving = [pltpu.make_async_copy(cot_ref.at[p, :], cot_all.at[l, :], come.at[t]) for t, (l, p) in enumerate(here)]
        for copy in arriving:
            copy.start()
        sums_ref[...] = jnp.zeros_like(sums_ref)

        def vec(row):
            return vecs[row][...].astype(F32)[None, :]

        @pl.loop(0, 2)
        def _(tile):
            mine = pl.ds(pl.multiple_of(tile * taken, 128), taken)
            attn = nn(mixed_ref[mine, :local], packs[0][:local, :]) + nn(mixed_ref[mine, local:], packs[1][:local, :])
            biases = [biases_of(pack) for pack in packs]
            xhat1, scale1 = standardize(x_ref[mine, :].astype(F32) + attn + vec(B_OUT))
            xhat_ref[mine, :] = xhat1
            scale_ref[mine, :] = jnp.broadcast_to(scale1, (taken, 128))
            normed = xhat1 * vec(GAIN1) + vec(SHIFT1)
            low = normed.astype(BF16)
            normed_ref[mine, :] = low
            resid2 = [normed + vec(B_DOWN)]

            def first(i):
                side, at = parts[i]
                return nn(low, wu[side][:, at : at + CHUNK])

            def then(i, up):
                side, at = parts[i]
                where, line = slice(at, at + CHUNK), 1 + at // width
                up = up + biases[side][line : line + 1, at % width : at % width + CHUNK]
                big, small = normal_parts(up)
                act = (up * big).astype(BF16)
                if side == 0:
                    act_ref[mine, where] = act
                else:
                    act_all[mine, where] = act
                slope_ref[mine, side * hidden + at : side * hidden + at + CHUNK] = (big + up * small).astype(BF16)
                resid2[0] += nn(act, wd[side][where, :])

            in_turn(len(parts), first, then)
            xhat2, scale2 = standardize(resid2[0])
            out_all[mine, :] = (xhat2 * vec(GAIN2) + vec(SHIFT2)).astype(BF16)

            @pl.when(tile == 0)
            def _():
                for copy in arriving:
                    copy.wait()

            grad = cot_all[mine, :].astype(F32) * live_ref[mine, 0:1]
            grad_resid2 = standardize_back(grad * vec(GAIN2), xhat2, scale2)
            grad_ref[mine, :] = grad_resid2
            low_ref[mine, :] = grad_resid2.astype(BF16)
            for row, value in enumerate((grad * xhat2, grad, grad_resid2)):
                sums_ref[row : row + 1, :] += jnp.sum(value, axis=0, keepdims=True)

        leaving = [pltpu.make_async_copy(out_all.at[l, :], out_ref.at[p, :], gone.at[t]) for t, (l, p) in enumerate(here)]
        for copy in leaving:
            copy.start()

        @pl.loop(0, hidden // block)
        def _(part):
            gw_ref[pl.ds(pl.multiple_of(part * block, 128), block), :] = tn(
                act_all[:, lanes(part, block)], low_ref[...]
            ).astype(BF16)

        for copy in leaving:
            copy.wait()

    inputs = [(mixed, WHOLE), (x, WHOLE), (cotangent, FAR), const(live)]
    inputs += [const(a) for a in vectors] + [(a, WHOLE) for a in (*packs, *w_up, *w_down)]
    outputs = [
        (shape((rows, width), BF16), FAR),
        (shape((rows, hidden), BF16), WHOLE),
        (shape((rows, 2 * hidden), BF16), WHOLE),
        (shape((rows, width), BF16), WHOLE),
        (shape((rows, width), F32), WHOLE),
        (shape((rows, 128), F32), WHOLE),
        (shape((rows, width), F32), WHOLE),
        (shape((rows, width), BF16), WHOLE),
        (shape((8, width), F32), WHOLE),
        (shape((hidden, width), BF16), WHOLE),
    ]
    scratch = [pltpu.VMEM((rows, hidden), BF16), pltpu.VMEM((rows, width), BF16), pltpu.VMEM((rows, width), BF16)]
    scratch += [pltpu.SemaphoreType.DMA((tiles,))] * 2
    return call(kernel, (1,), inputs, outputs, scalars, "layer_forward", limit=14, scratch=scratch)


def layer_backward(
    grad_down, grad_resid2, slope, xhat1, scale1, normed, gain1, packs, w_up, w_down, scalars, after
):
    rows, width = grad_down.shape
    tiles, hidden = rows // EDGE, w_up[0].shape[1]
    block, local, taken = width // 2, width // 2, rows // 2
    parts = [(side, at) for side in range(2) for at in range(0, hidden, CHUNK)]

    def kernel(_, ins, outs, up_all, resid_all, gone):
        low_ref, grad_ref, slope_ref, xhat_ref, scale_ref, normed_ref, gain_ref = ins[:7]
        packs, wu, wd = ins[7:9], ins[9:11], ins[11:13]
        up_ref, resid_ref, attn_ref, mixed_ref, sums_ref, bias_ref, gw_ref = outs
        gain = gain_ref[...].astype(F32)[None, :]
        sums_ref[...] = jnp.zeros_like(sums_ref)
        bias_ref[...] = jnp.zeros_like(bias_ref)

        @pl.loop(0, 2)
        def _(tile):
            mine = pl.ds(pl.multiple_of(tile * taken, 128), taken)
            low = low_ref[mine, :]
            grad_normed = grad_ref[mine, :]
            for side, at in parts:
                where, both = slice(at, at + CHUNK), slice(side * hidden + at, side * hidden + at + CHUNK)
                grad_act = nt(low, wd[side][where, :])
                grad_up = (grad_act * slope_ref[mine, both].astype(F32)).astype(BF16)
                if side == 0:
                    up_ref[mine, where] = grad_up
                else:
                    up_all[mine, where] = grad_up
                bias_ref[0:1, both] += jnp.sum(grad_up.astype(F32), axis=0, keepdims=True)
                grad_normed += nt(grad_up, wu[side][:, where])
            xhat = xhat_ref[mine, :]
            grad_resid1 = standardize_back(grad_normed * gain, xhat, scale_ref[mine, 0:1])
            resid_all[mine, :] = grad_resid1
            grad_attn = grad_resid1.astype(BF16)
            attn_ref[mine, :] = grad_attn
            mixed_ref[mine, :local] = nt(grad_attn, packs[0][:local, :]).astype(BF16)
            mixed_ref[mine, local:] = nt(grad_attn, packs[1][:local, :]).astype(BF16)
            for row, value in enumerate((grad_normed * xhat, grad_normed, grad_resid1)):
                sums_ref[row : row + 1, :] += jnp.sum(value, axis=0, keepdims=True)

        leaving = pltpu.make_async_copy(resid_all, resid_ref, gone)
        leaving.start()

        @pl.loop(0, hidden // block)
        def _(i):
            gw_ref[pl.ds(pl.multiple_of(i * block, 128), block), :] = tn(
                normed_ref[:, lanes(i % 2, block)], up_all[:, lanes(i // 2, width)]
            ).astype(BF16)

        leaving.wait()

    inputs = [(a, WHOLE) for a in (grad_down, grad_resid2, slope, xhat1, scale1, normed)]
    inputs += [const(gain1)] + [(a, WHOLE) for a in (*packs, *w_up, *w_down)]
    outputs = [
        (shape((rows, hidden), BF16), WHOLE),
        (shape((rows, width), F32), FAR),
        (shape((rows, width), BF16), WHOLE),
        (shape((rows, width), BF16), WHOLE),
        (shape((8, width), F32), WHOLE),
        (shape((8, 2 * hidden), F32), WHOLE),
        (shape((hidden, width), BF16), WHOLE),
    ]
    scratch = [pltpu.VMEM((rows, hidden), BF16), pltpu.VMEM((rows, width), F32), pltpu.SemaphoreType.DMA]
    return call(kernel, (1,), inputs, outputs, scalars, "layer_backward", after, limit=14, scratch=scratch)


def down_gradient(act, grad_down, scalars, after=()):
    rows, width = grad_down.shape
    hidden = act.shape[1]
    block = hidden // 4

    def kernel(_, ins, outs):
        @pl.loop(0, 4)
        def _(i):
            rows_out = pl.ds(pl.multiple_of(i * block, 128), block)
            outs[0][rows_out, :] = tn(ins[0][:, lanes(i, block)], ins[1][...])

    inputs, outputs = [(act, WHOLE), (grad_down, WHOLE)], [(shape((hidden, width), F32), WHOLE)]
    return call(kernel, (1,), inputs, outputs, scalars, "down_gradient", after)[0]


def up_gradient(normed, grad_up, scalars, after=()):
    rows, width = normed.shape
    parts = grad_up.shape[1] // width
    block = width // 2

    def kernel(_, ins, outs):
        @pl.loop(0, 2 * parts)
        def _(i):
            rows_out = pl.ds(pl.multiple_of(i * block, 128), block)
            outs[0][rows_out, :] = tn(ins[0][:, lanes(i % 2, block)], ins[1][:, lanes(i // 2, width)])

    inputs, outputs = [(normed, WHOLE), (grad_up, WHOLE)], [(shape((parts * width, width), F32), WHOLE)]
    return call(kernel, (1,), inputs, outputs, scalars, "up_gradient", after)[0]


def attention_gradient(x, grads, mixed, grad_attn, half, dtype, scalars, after=()):
    rows, width = x.shape
    local = width // 2
    columns = slice(half * local, (half + 1) * local)

    def kernel(_, ins, outs):
        x_ref, grad_ref, mixed_ref, attn_ref = ins
        sums_ref = outs[2]
        for part in range(3):
            mine = slice(part % 2 * local, (part % 2 + 1) * local)
            grad = grad_ref[part, :, columns]
            outs[part // 2][mine, :local] = tn(x_ref[:, :local], grad).astype(dtype)
            outs[part // 2][mine, local:] = tn(x_ref[:, local:], grad).astype(dtype)
            sums_ref[part] = jnp.broadcast_to(jnp.sum(grad.astype(F32), axis=0, keepdims=True), (8, local))
        outs[1][local:, :] = tn(mixed_ref[:, columns], attn_ref[...]).astype(dtype)

    inputs = [(a, WHOLE) for a in (x, grads, mixed, grad_attn)]
    outputs = [(shape((2 * local, width), dtype), WHOLE)] * 2 + [(shape((3, 8, local), F32), WHOLE)]
    return call(kernel, (1,), inputs, outputs, scalars, f"attention_gradient_{half}", after)


def token_gradient(grads, grad_resid1, w_qkv, scalars, after=()):
    rows, width = grad_resid1.shape
    tiles, local = rows // EDGE, width // 2

    def kernel(sc, ins, outs, total, weights, resid, come, gone):
        arriving = [pltpu.make_async_copy(ins[2 + side], weights.at[side], come.at[side]) for side in range(2)]
        arriving.append(pltpu.make_async_copy(ins[1], resid, come.at[2]))
        for copy in arriving:
            copy.start()
        here = [slice(tile * EDGE, (tile + 1) * EDGE) for tile in range(tiles)]

        def part(mine, side):
            columns = slice(side * local, (side + 1) * local)
            return sum(nt(ins[0][k, mine, columns], weights[side, k]) for k in range(3))

        arriving[0].wait()
        for mine in here:
            total[mine, :] = part(mine, 0)
        arriving[1].wait()
        arriving[2].wait()
        leaving = []
        for tile, mine in enumerate(here):
            there = rows_of((tile + sc[MP]) % tiles)
            total[mine, :] += resid[mine, :] + part(mine, 1)
            leaving.append(pltpu.make_async_copy(total.at[mine, :], outs[0].at[there, :], gone.at[tile]))
            leaving[-1].start()
        for copy in leaving:
            copy.wait()
        outs[1][...] = jnp.zeros_like(outs[1])

    inputs = [(grads, WHOLE)] + [(a, FAR) for a in (grad_resid1, *w_qkv)]
    outputs = [(shape((rows, width), F32), FAR), TOKEN]
    scratch = [pltpu.VMEM((rows, width), F32), pltpu.VMEM((2, *w_qkv[0].shape), BF16), pltpu.VMEM((rows, width), F32)]
    scratch += [pltpu.SemaphoreType.DMA((3,)), pltpu.SemaphoreType.DMA((tiles,))]
    return call(kernel, (1,), inputs, outputs, scalars, "token_gradient", after, scratch=scratch, limit=16)


TAIL = 16


def parted(value):
    high = value.astype(BF16)
    return high, (value - high.astype(F32)).astype(BF16)


def tails(head_own, head_far, sums_up, sums1, sums2, scalars, after=()):
    local, width = head_own.shape[2], sums1.shape[1]
    units = sums_up.shape[1] // 2

    def kernel(sc, ins, outs):
        second = sc[MP] == 1
        for side, heads in enumerate((ins[0], ins[1])):
            lines = [jnp.concatenate([heads[0, 0:1, :], heads[2, 0:1, :]], axis=1)]
            at = side * units
            lines += [ins[2][0:1, at + c : at + c + width] for c in range(0, units, width)]
            first, last = ins[3][0:3, :], ins[4][0:3, :]
            lines.append(jnp.where(second, first, last) if side == 0 else jnp.where(second, last, first))
            lines.append(jnp.zeros((8 - sum(l.shape[0] for l in lines), width), F32))
            high, low = parted(jnp.concatenate(lines, axis=0))
            outs[side][:8], outs[side][8:] = high, low

    inputs = [(a, WHOLE) for a in (head_own, head_far, sums_up, sums1, sums2)]
    return call(kernel, (1,), inputs, [(shape((TAIL, width), BF16), WHOLE)] * 2, scalars, "tails", after)


def tail_sum(own, came):
    own, came = own.astype(F32), came.astype(F32)
    return (own[:8] + own[8:]) + (came[:8] + came[8:])


def fold(kept, came, step, scalars, name, after, tail=None, carry=()):
    rows, width = kept.shape
    half = rows // 2
    extra = 0 if tail is None else TAIL
    if half % 16:
        total, bit = kept + came[:rows].astype(F32), scalars[BITS + step]
        go = lax.dynamic_slice_in_dim(total, (1 - bit) * half, half).astype(BF16)
        if extra:
            both = tail_sum(tail[0][-TAIL:], tail[1][-TAIL:])
            high = lax.reduce_precision(both, 8, 7)
            go = jnp.concatenate([go, high.astype(BF16), (both - high).astype(BF16)], axis=0)
        return go, lax.dynamic_slice_in_dim(total, bit * half, half), *carry
    inputs = [kept, came] + ([] if tail is None else list(tail))

    def kernel(sc, ins, outs):
        bit = sc[BITS + step]
        stay = pl.ds(pl.multiple_of(bit * half, 16), half)
        go = pl.ds(pl.multiple_of((1 - bit) * half, 16), half)
        outs[0][:half] = (ins[0][go, :] + ins[1][go, :].astype(F32)).astype(BF16)
        outs[1][...] = ins[0][stay, :] + ins[1][stay, :].astype(F32)
        if extra:
            at, to = ins[2].shape[0] - TAIL, ins[3].shape[0] - TAIL
            high, low = parted(tail_sum(ins[2][at:, :], ins[3][to:, :]))
            outs[0][half : half + 8], outs[0][half + 8 :] = high, low

    outputs = [(shape((half + extra, width), BF16), WHOLE), (shape((half, width), F32), WHOLE)]
    return call(kernel, (1,), [(a, WHOLE) for a in inputs], outputs, scalars, name, after, carry=carry)


def add(own, came, scalars, name, after, tail=None, carry=()):
    rows, width = came.shape[0] - (0 if tail is None else TAIL), own.shape[1]
    if rows % 16:
        whole = (own[:rows].astype(F32) + came[:rows].astype(F32)).astype(BF16)
        return whole, None if tail is None else tail_sum(tail[0][-TAIL:], tail[1][-TAIL:]), *carry

    def kernel(_, ins, outs):
        outs[0][...] = (ins[0][:rows, :].astype(F32) + ins[1][:rows, :].astype(F32)).astype(BF16)
        if tail is not None:
            at, to = ins[2].shape[0] - TAIL, ins[3].shape[0] - TAIL
            outs[1][...] = tail_sum(ins[2][at:, :], ins[3][to:, :])

    inputs = [own, came] + ([] if tail is None else list(tail))
    outputs = [(shape((rows, width), BF16), WHOLE)]
    if tail is not None:
        outputs.append((shape((8, width), F32), WHOLE))
    found = call(kernel, (1,), [(a, WHOLE) for a in inputs], outputs, scalars, name, after, carry=carry)
    return found if tail is not None else (found[0], None, *found[1:])


def add_on(own, came, scalars, name, after, tail, carry=()):
    rows, width = came.shape[0] - TAIL, own.shape[1]
    if rows % 16:
        both = tail_sum(tail[0][-TAIL:], tail[1][-TAIL:])
        high = lax.reduce_precision(both, 8, 7)
        whole = (own[:rows].astype(F32) + came[:rows].astype(F32)).astype(BF16)
        return jnp.concatenate([whole, high.astype(BF16), (both - high).astype(BF16)], axis=0), *carry

    def kernel(_, ins, outs):
        outs[0][:rows] = (ins[0][:rows, :].astype(F32) + ins[1][:rows, :].astype(F32)).astype(BF16)
        at, to = ins[2].shape[0] - TAIL, ins[3].shape[0] - TAIL
        high, low = parted(tail_sum(ins[2][at:, :], ins[3][to:, :]))
        outs[0][rows : rows + 8], outs[0][rows + 8 :] = high, low

    inputs = [(a, WHOLE) for a in (own, came, *tail)]
    outputs = [(shape((rows + TAIL, width), BF16), WHOLE)]
    return call(kernel, (1,), inputs, outputs, scalars, name, after, carry=carry)


def join(whole, came, step, scalars, name, after, carry=()):
    rows, width = whole.shape
    if rows % 16:
        ahead = scalars[BITS + step] == 0
        first, last = jnp.where(ahead, whole, came), jnp.where(ahead, came, whole)
        return jnp.concatenate([first, last], axis=0), *carry

    def kernel(sc, ins, outs):
        bit = sc[BITS + step]
        outs[0][pl.ds(pl.multiple_of(bit * rows, 16), rows), :] = ins[0][...]
        outs[0][pl.ds(pl.multiple_of((1 - bit) * rows, 16), rows), :] = ins[1][...]

    outputs = [(shape((2 * rows, width), BF16), WHOLE)]
    inputs = [(whole, WHOLE), (came, WHOLE)]
    return call(kernel, (1,), inputs, outputs, scalars, name, after, carry=carry)


def put(rows_in, mine, kind, held, scalars, name, after, carry=()):
    rows, width = rows_in.shape
    block = width // 2
    chunk = block // 3
    pieces = rows // chunk

    def kernel(sc, ins, outs, ready, done):
        here = sc[BITS] if mine else 1 - sc[BITS]

        def targets(half, piece):
            part, at = divmod(half * rows + piece * chunk, block)
            left, right = slice(0, block), slice(block, width)
            low, high = slice(at, at + chunk), slice(block + at, block + at + chunk)
            if kind == "down":
                return [(outs[0].at[part * block + at : part * block + at + chunk, :], slice(0, width))]
            if kind == "up":
                row, column = part % 2 * block + at, part // 2 * width
                return [(outs[0].at[row : row + chunk, column : column + width], slice(0, width))]
            if kind == "values" and part == 1:
                return [(outs[1].at[low, :], slice(0, width))]
            which = part if kind == "queries" else 2
            return [(outs[0].at[which, low, :], left), (outs[0].at[which, high, :], right)]

        def copies(half, piece):
            return [
                pltpu.make_async_copy(ready.at[piece * chunk : (piece + 1) * chunk, columns], to, done.at[piece, i])
                for i, (to, columns) in enumerate(targets(half, piece))
            ]

        for piece in range(pieces):
            at = slice(piece * chunk, (piece + 1) * chunk)
            ready[at, :] = ins[0][at, :].astype(F32)
            for half in range(2):

                @pl.when(here == half)
                def _():
                    for copy in copies(half, piece):
                        copy.start()

        outs[-1][...] = jnp.zeros_like(outs[-1])
        for half in range(2):

            @pl.when(here == half)
            def _():
                for piece in range(pieces):
                    for copy in copies(half, piece):
                        copy.wait()

    if kind == "down":
        shapes = [(2 * rows, width)]
    elif kind == "up":
        shapes = [(width, 2 * rows // width * width)]
    else:
        shapes = [(3, width, block), (block, width)]
    outputs = [(shape(dims, F32), FAR) for dims in shapes] + [TOKEN]
    inputs = [(rows_in, WHOLE), *((h, FAR) for h in held)]
    aliases = {1 + i: i for i in range(len(held))}
    scratch = [pltpu.VMEM((rows, width), F32), pltpu.SemaphoreType.DMA((pieces, 2))]
    found = call(kernel, (1,), inputs, outputs, scalars, name, after, aliases, scratch=scratch, carry=carry)
    return found[: len(shapes)], found[len(shapes)], *found[len(outputs) :]


ORDER = """
a LB a UG b EB a AB a ME AG1 b AG0 d b a c b TG a d b c d b c d a b c d c d c d a c b d c
""".split()


def program(n_dp):
    steps = n_dp.bit_length() - 1
    assert 1 << steps == n_dp
    orders = (list(range(steps)), [1, 0, *range(2, steps)])

    def swap(array):
        return lax.ppermute(array, "mp", [(0, 1), (1, 0)])

    def partner(array, step):
        pairs = [
            (2 * d + m, 2 * (d ^ (1 << orders[m][step])) + m) for d in range(n_dp) for m in range(2)
        ]
        return lax.ppermute(array, ("dp", "mp"), pairs)

    halvings = max(steps - 1, 0)

    class Chain:
        def __init__(self, kind, own, came, scalars, shared, tail=None):
            self.kind, self.kept, self.came, self.tail, self.shared = kind, own, came, tail, shared
            self.scalars, self.step, self.result, self.vectors = scalars, 0, None, None

        def send(self, sent, bit):
            self.came = partner(sent, bit)
            self.step += 1
            if self.tail is not None:
                self.tail = (sent, self.came)
            return (sent,)

        def advance(self, after, carry=()):
            step, name, scalars = self.step, f"{self.kind}_{self.step}", self.scalars
            back = halvings - 1 - (step - steps)
            if step < halvings:
                sent, self.kept, *carry = fold(
                    self.kept, self.came, step, scalars, name, after, self.tail, carry
                )
                return self.send(sent, step), carry
            if step < steps:
                if self.tail is None:
                    sent, _, *carry = add(self.kept, self.came, scalars, name, after, None, carry)
                else:
                    sent, *carry = add_on(self.kept, self.came, scalars, name, after, self.tail, carry)
                self.kept = sent
                return self.send(sent, step), carry
            if step == steps:
                sent, self.vectors, *carry = add(
                    self.kept, self.came, scalars, name, after, self.tail, carry
                )
                self.tail = None
            elif back >= 0:
                sent, *carry = join(self.whole, self.came, back + 1, scalars, name, after, carry)
            else:
                held = self.result_half if self.kind in ("down", "up") else self.shared
                found, token, *carry = put(self.came, False, self.kind, held, scalars, name, after, carry)
                self.result = found
                if self.kind not in ("down", "up"):
                    self.shared[:] = found
                return (token,), carry
            self.whole = sent
            after = self.send(sent, back)
            if back == 0:
                held = () if self.kind in ("down", "up") else self.shared
                found, token = put(self.whole, True, self.kind, held, scalars, name + "_own", after)
                if self.kind in ("down", "up"):
                    self.result_half = found
                else:
                    self.shared[:] = found
                after = (token,)
            return after, carry

    def per_device(
        tokens, cotangent, mask, lengths, counts, w_qkv, qv_bias, w_out, b_out, gain1, shift1,
        w_up, b_up, w_down, b_down, gain2, shift2,
    ):
        rows, width = tokens.shape
        mp, local, hidden = lax.axis_index("mp"), qv_bias.shape[1], w_up.shape[1]
        limits = jnp.stack([mp, lengths[0], counts[0] * lengths[0]]).astype(jnp.int32)
        scalars = Place(orders)

        w_qkv = (w_qkv, swap(w_qkv))
        vectors = (b_out, gain1, shift1, b_down, gain2, shift2)
        mine = pack(tokens, w_out, qv_bias, b_up, mp.astype(jnp.int32)[None])
        packs = (mine, swap(mine))
        bias_full, bias_edge, live, token = prepare(mask, rows, limits, (mine,))
        query, keys, values, far, x, w_up, w_down = project(
            tokens, w_qkv, packs, (w_up, w_down), scalars, (token,)
        )
        w_up, w_down = ((w, swap(w)) for w in (w_up, w_down))
        mixed, lse = attend(query, keys, values, None, bias_full, None, scalars)
        mixed, lse_edge = attend(query, keys, values, far, bias_edge, mixed, scalars)
        out, act, slope, normed, xhat1, scale1, grad_resid2, grad_down, sums2, gw = layer_forward(
            mixed, x, cotangent, live, vectors, packs, w_up, w_down, scalars
        )
        came = swap(gw)
        own = down_gradient(act, grad_down, scalars, (gw,))

        k = {}
        chains, shared = {"a": Chain("down", own, came, scalars, None)}, []

        def run_layer_backward(after):
            k["up"], k["resid"], k["attn"], k["mixed"], k["sums1"], k["sums_up"], k["gw"] = layer_backward(
                grad_down, grad_resid2, slope, xhat1, scale1, normed, gain1, packs, w_up, w_down, scalars, after
            )
            return (k["sums1"],), ("gw",)

        def run_up_gradient(after):
            own = up_gradient(normed, k["up"], scalars, after)
            chains["b"] = Chain("up", own, k["gw"], scalars, None)
            return (own,), None

        def run_edge_back(after):
            k["grads"], k["near"], k["far"] = attend_back(
                query, keys, values, far, bias_edge, mixed, k["mixed"], lse_edge, None, scalars, after
            )
            return (k["near"],), ("far",)

        def run_back(after):
            k["grads"] = attend_back(
                query, keys, values, None, bias_full, mixed, k["mixed"], lse, k["grads"], scalars, after
            )[0]
            return (k["grads"],), None

        def run_merge(after):
            k["grads"] = merge_edge(k["near"], k["far"], k["grads"], scalars, after)
            return (k["grads"],), None

        def run_far_gradient(after):
            k["gw"], k["gw_last"], k["head_far"] = attention_gradient(
                x, k["grads"], mixed, k["attn"], 1, BF16, scalars, after
            )
            return (k["head_far"],), ("gw", "gw_last")

        def run_own_gradient(after):
            own, last, head_own = attention_gradient(x, k["grads"], mixed, k["attn"], 0, F32, scalars, after)
            tail_own, tail_far = tails(head_own, k["head_far"], k["sums_up"], k["sums1"], sums2, scalars)
            chains["c"] = Chain("queries", own, k["gw"], scalars, shared)
            chains["d"] = Chain("values", last, k["gw_last"], scalars, shared, (tail_own, swap(tail_far)))
            return (own, tail_own), None

        def run_token_gradient(after):
            k["tokens"], token = token_gradient(k["grads"], k["resid"], w_qkv, scalars, after)
            return (token,), None

        work = {
            "LB": run_layer_backward, "UG": run_up_gradient, "EB": run_edge_back, "AB": run_back,
            "ME": run_merge, "AG1": run_far_gradient, "AG0": run_own_gradient, "TG": run_token_gradient,
        }
        after, leaving = (own,), []
        for name in ORDER:
            if name in work:
                after, left = work[name](after)
                leaving += left or ()
            else:
                after, carried = chains[name].advance(after, [k[n] for n in leaving])
                k.update((n, swap(c)) for n, c in zip(leaving, carried, strict=True))
                leaving = []
        while any(c.result is None for c in chains.values()):
            for c in chains.values():
                if c.result is None:
                    after, _ = c.advance(after)

        vectors = chains["d"].vectors
        head, up = vectors[0].reshape(2, local), vectors[1 : 1 + hidden // width].reshape(-1)
        mine = vectors[1 + hidden // width : 4 + hidden // width]
        other = swap(mine)
        g_gain2, g_shift2, g_b_down = jnp.where(mp == 0, mine, other)
        g_gain1, g_shift1, g_b_out = jnp.where(mp == 0, other, mine)
        gw_qkv, gw_out = shared
        return (
            out, k["tokens"], gw_qkv, head, gw_out, g_b_out, g_gain1, g_shift1,
            chains["b"].result[0], up, chains["a"].result[0], g_b_down, g_gain2, g_shift2,
        )

    return per_device


def solution(mesh):
    rows, cols, one = P(("dp", "mp"), None), P(None, "mp"), P()
    in_specs = (
        rows, rows, P("dp"), P("dp"), P("dp"),
        P(None, None, "mp"), cols, P("mp", None), one, one, one,
        cols, P("mp"), P("mp", None), one, one, one,
    )
    out_specs = (
        rows, rows, P(None, None, "mp"), cols, P("mp", None), one, one, one,
        cols, P("mp"), P("mp", None), one, one, one,
    )
    return jax.shard_map(
        program(mesh.shape["dp"]), mesh=mesh, in_specs=in_specs, out_specs=out_specs, check_vma=False
    )
```

```python
import functools

import jax
import jax.numpy as jnp
from jax import lax
from jax.experimental import pallas as pl
from jax.experimental.pallas import tpu as pltpu
from jax.sharding import PartitionSpec as P

HEAD_DIM = 64
PAIR = 2 * HEAD_DIM
SPAN = 512
EDGE = SPAN // 2
LOG2E = 1.4426950408889634
MIB = 1 << 20
BF16 = jnp.bfloat16
F32 = jnp.float32
WHOLE = pl.BlockSpec(memory_space=pltpu.VMEM)
UNREAD = pl.BlockSpec(memory_space=pl.ANY)
FAR = pl.BlockSpec(memory_space=pltpu.HBM)
BIASES = 16
TOKEN = (jax.ShapeDtypeStruct((8, 128), F32), WHOLE)


def shape(dims, dtype):
    return jax.ShapeDtypeStruct(tuple(dims), dtype)


def nn(a, b):
    return lax.dot_general(a, b, (((1,), (0,)), ((), ())), preferred_element_type=F32)


def nt(a, b):
    return lax.dot_general(a, b, (((1,), (1,)), ((), ())), preferred_element_type=F32)


def tn(a, b):
    return lax.dot_general(a, b, (((0,), (0,)), ((), ())), preferred_element_type=F32)


def call(kernel, grid, inputs, outputs, scalars, name, after=(), aliases=None, limit=8, scratch=(), carry=()):
    n_in, n_out = len(inputs), len(outputs)

    def space(spec):
        return None if spec is UNREAD else pltpu.VMEM if spec is WHOLE else pltpu.HBM

    arrays = [a if s is UNREAD else pltpu.with_memory_space_constraint(a, space(s)) for a, s in inputs]
    shapes = [o if s is UNREAD else space(s)(o.shape, o.dtype) for o, s in outputs]
    held = (*after, *carry)
    fetched = [] if isinstance(scalars, Place) else [scalars]
    aliases = {len(fetched) + k: v for k, v in (aliases or {}).items()}
    aliases |= {len(fetched) + n_in + len(after) + k: n_out + k for k in range(len(carry))}

    def body(*refs):
        place, refs = (refs[0], refs[1:]) if fetched else (scalars, refs)
        first = n_in + len(held)
        kernel(place, refs[:n_in], refs[first : first + n_out], *refs[first + n_out + len(carry) :])

    return pl.pallas_call(
        body,
        grid_spec=pltpu.PrefetchScalarGridSpec(
            num_scalar_prefetch=len(fetched),
            grid=grid,
            in_specs=[s for _, s in inputs] + [UNREAD] * len(held),
            out_specs=[s for _, s in outputs] + [UNREAD] * len(carry),
            scratch_shapes=scratch,
        ),
        out_shape=shapes + [shape(a.shape, a.dtype) for a in carry],
        input_output_aliases=aliases,
        compiler_params=pltpu.CompilerParams(vmem_limit_bytes=limit * MIB),
        name=name,
    )(*fetched, *arrays, *held)


def const(array):
    return array, pl.BlockSpec(array.shape, lambda i, *sc: (0,) * len(array.shape))


def lanes(index, count=PAIR):
    return pl.ds(pl.multiple_of(index * count, 128), count)


def rows_of(tile):
    return pl.ds(pl.multiple_of(tile * EDGE, EDGE), EDGE)


class Place:
    def __init__(self, orders):
        self.orders = orders

    def __getitem__(self, index):
        if index == MP:
            return lax.axis_index("mp")
        dp, (first, second) = lax.axis_index("dp"), (order[index - BITS] for order in self.orders)
        if first == second:
            return (dp >> first) & 1
        return (dp >> jnp.where(lax.axis_index("mp") == 0, first, second)) & 1


MP, LENGTH, LIVE, BITS = range(4)


def lay(tiles):
    return lambda i, *sc: ((jnp.minimum(i, tiles - 1) + sc[0][MP]) % tiles, 0)


def pack(tokens, w_out, qv_bias, b_up, scalars):
    rows, (local, width) = tokens.shape[0], w_out.shape

    def kernel(_, ins, outs):
        up = ins[3][...].astype(F32)[None, :]
        lines = [jnp.concatenate([ins[2][0:1, :], ins[2][1:2, :]], axis=1).astype(F32)]
        lines += [up[:, at : at + width] for at in range(0, up.shape[1], width)]
        lines.append(jnp.zeros((BIASES - len(lines), width), F32))
        outs[0][:local, :] = ins[1][...]
        outs[0][local : local + BIASES, :] = jnp.concatenate(lines, axis=0).astype(BF16)
        outs[0][local + BIASES :, :] = ins[0][...]

    shared = pl.BlockSpec((EDGE, width), lambda i, *sc: ((1 - sc[0][MP]) * (rows // EDGE - 1), 0))
    inputs = [(tokens, shared), *(const(a) for a in (w_out, qv_bias, b_up))]
    outputs = [(shape((local + BIASES + EDGE, width), BF16), WHOLE)]
    return call(kernel, (1,), inputs, outputs, scalars, "pack")[0]


def prepare(mask, rows, scalars, after):
    slots = mask.shape[0]

    def kernel(sc, ins, outs, live_ref):
        outs[3][...] = jnp.zeros_like(outs[3])
        mp, length = sc[MP], sc[LENGTH]
        place = lax.broadcasted_iota(jnp.int32, (1, slots), 1)
        live = jnp.where((ins[0][...].reshape(1, slots) == 1) & (place < sc[LIVE]), 1.0, 0.0)
        live_ref[...] = jnp.broadcast_to(live, (8, slots))

        def rows_at(start, count):
            row = live_ref[0:1, pl.ds(pl.multiple_of(start, EDGE), count)]
            return jnp.broadcast_to(row, (128, count)).T

        def sequence(slot):
            return sum((slot >= times * length).astype(jnp.int32) for times in (1, 2, 3))

        def masked(keys, queries, live_keys):
            repeats = [live_keys] * (queries.shape[1] // 128)
            allowed = (sequence(keys) == sequence(queries)) & (
                (jnp.concatenate(repeats, axis=1) > 0.5) | (keys == queries)
            )
            return jnp.where(allowed, 0.0, -1e30).astype(BF16)

        whole = rows_at(mp * (slots - SPAN), SPAN)
        near = rows_at(SPAN + mp * EDGE, EDGE)
        far = rows_at(SPAN + (1 - mp) * EDGE, EDGE)
        outs[2][:SPAN], outs[2][SPAN:] = whole, near
        square = (SPAN, SPAN)
        outs[0][...] = masked(
            lax.broadcasted_iota(jnp.int32, square, 0), lax.broadcasted_iota(jnp.int32, square, 1), whole
        )
        tall = (SPAN, EDGE)
        keys = lax.broadcasted_iota(jnp.int32, tall, 0) + mp * EDGE
        keys = jnp.where(keys >= SPAN, keys - SPAN, keys)
        queries = lax.broadcasted_iota(jnp.int32, tall, 1) + mp * EDGE
        outs[1][...] = masked(keys, queries, jnp.concatenate([near, far], axis=0))

    outputs = [(shape(dims, BF16), WHOLE) for dims in ((SPAN, SPAN), (SPAN, EDGE))] + [const(shape((rows, 128), F32))]
    outputs.append(TOKEN)
    scratch = [pltpu.VMEM((8, slots), F32)]
    return call(kernel, (1,), [const(mask)], outputs, scalars, "prepare", after, limit=12, scratch=scratch)


def biases_of(pack):
    return pack[-BIASES - EDGE : -EDGE, :].astype(F32)


def project(x, weights, packs, copied, scalars, after):
    rows, width = x.shape
    tiles, local = rows // EDGE, weights[0].shape[2]

    def kernel(sc, ins, outs, *done):
        x_ref, own_ref, other_ref, *packs = ins[:5]
        kind = pl.program_id(0)
        copies = [pltpu.make_async_copy(*c) for c in zip(ins[5:], outs[5:], done, strict=True)]

        @pl.when(kind == 0)
        def _():
            for copy in copies:
                copy.start()

        def bias_of(row):
            lines = [biases_of(pack)[0:1, row * local : (row + 1) * local] for pack in packs]
            return jnp.concatenate(lines, axis=1)

        def each_tile(index, finish):
            both = jnp.concatenate([own_ref[...], other_ref[index]], axis=1)
            for tile in range(tiles):
                at = pl.multiple_of(((tile + sc[MP]) % tiles) * EDGE, EDGE)
                block = x_ref[pl.ds(at, EDGE), :]
                outs[index][tile * EDGE : (tile + 1) * EDGE, :] = finish(nn(block, both))
                if index == 0:
                    outs[4][tile * EDGE : (tile + 1) * EDGE, :] = block
            if index > 0:
                outs[3][index - 1] = finish(nn(packs[1][local + BIASES :, :], both))

        finishes = (
            lambda v: (v + bias_of(0)).astype(BF16) * BF16(HEAD_DIM**-0.5),
            lambda v: v.astype(BF16),
            lambda v: (v + bias_of(1)).astype(BF16),
        )
        for index, finish in enumerate(finishes):
            pl.when(kind == index)(functools.partial(each_tile, index, finish))

        @pl.when(kind == 2)
        def _():
            for copy in copies:
                copy.wait()

    wide = shape((rows, 2 * local), BF16)
    outputs = [(wide, WHOLE)] * 3 + [(shape((2, EDGE, 2 * local), BF16), WHOLE), (shape((rows, width), BF16), WHOLE)]
    outputs += [(shape(a.shape, a.dtype), WHOLE) for a in copied]
    inputs = [const(x), (weights[0], pl.BlockSpec((None, width, local), lambda i, *sc: (i, 0, 0)))]
    inputs += [(a, WHOLE) for a in (weights[1], *packs)] + [(a, FAR) for a in copied]
    scratch = [pltpu.SemaphoreType.DMA] * len(copied)
    return call(kernel, (3,), inputs, outputs, scalars, "project", after, limit=12, scratch=scratch)


def head_of(pair, index):
    lane = lax.broadcasted_iota(jnp.int32, pair.shape, 1)
    keep = lane < HEAD_DIM if index == 0 else lane >= HEAD_DIM
    return jnp.where(keep, pair, jnp.zeros_like(pair))


def span_rows(edge, ref, far_ref, which, pair):
    if not edge:
        return ref[:SPAN, lanes(pair)]
    return jnp.concatenate([ref[SPAN:, lanes(pair)], far_ref[which, :, lanes(pair)]], axis=0)


def in_turn(count, first, then):
    for i in range(count):
        then(i, first(i))


def staggered(count, first, then):
    ready = first(0)
    for i in range(count):
        following = first(i + 1) if i + 1 < count else None
        then(i, ready)
        ready = following


def attend(query, keys, values, far, bias, held, scalars):
    rows, width = query.shape
    pairs, edge = width // PAIR, far is not None
    group = pairs // 2
    count = EDGE if edge else SPAN
    here = slice(SPAN, SPAN + EDGE) if edge else slice(0, SPAN)

    def kernel(_, ins, outs):
        pl.loop(0, 2)(functools.partial(some, ins, outs))

    def some(ins, outs, half):
        base = half * group
        far_ref = ins[4] if edge else None
        bias = ins[3][...].astype(F32)
        pair_of = [base + p for p in range(group)]
        queries = [ins[0][here, lanes(p)] for p in pair_of]
        keys = [span_rows(edge, ins[1], far_ref, 0, p) for p in pair_of]
        values_t = [span_rows(edge, ins[2], far_ref, 1, p).astype(F32).T.astype(BF16) for p in pair_of]
        mixed = []

        def first(i):
            return nt(keys[i // 2], head_of(queries[i // 2], i % 2))

        def then(i, scores):
            pair, index = pair_of[i // 2], i % 2
            scores = scores * LOG2E + bias
            top = jnp.max(scores, axis=0, keepdims=True)
            weights = jnp.exp2(scores - top)
            total = jnp.sum(weights, axis=0, keepdims=True)
            part = values_t[i // 2][index * HEAD_DIM : (index + 1) * HEAD_DIM]
            mixed.append(nn(part, weights.astype(BF16)) * (1.0 / total))
            outs[1][pair, index : index + 1, :] = top + jnp.log2(total)
            if index == 1:
                outs[0][here, lanes(pair)] = jnp.concatenate(mixed[-2:], axis=0).T.astype(BF16)

        staggered(2 * group, first, then)

    inputs = [(a, WHOLE) for a in (query, keys, values, bias)]
    inputs += [(far, WHOLE), (held, WHOLE)] if edge else []
    outputs = [(shape((rows, width), BF16), WHOLE), (shape((pairs, 2, count), F32), WHOLE)]
    name = "attend_edge" if edge else "attend"
    return call(kernel, (1,), inputs, outputs, scalars, name, (), {5: 0} if edge else None, limit=12)


def attend_back(query, keys, values, far, bias, mixed, grad, lse, held, scalars, after):
    rows, width = query.shape
    pairs, edge = width // PAIR, far is not None
    group = pairs // 2
    here = slice(SPAN, SPAN + EDGE) if edge else slice(0, SPAN)

    def kernel(_, ins, outs):
        pl.loop(0, 2)(functools.partial(some, ins, outs))

    def some(ins, outs, half_of_pairs):
        base = half_of_pairs * group
        far_ref = ins[7] if edge else None
        bias, lse_ref = ins[3][...].astype(F32), ins[6]
        loaded = []
        for pair in [base + p for p in range(group)]:
            query, mixed, grad = (ins[i][here, lanes(pair)] for i in (0, 4, 5))
            keys = span_rows(edge, ins[1], far_ref, 0, pair)
            values = span_rows(edge, ins[2], far_ref, 1, pair)
            keys_t = keys.astype(F32).T.astype(BF16)
            delta_terms = (mixed.astype(F32) * grad.astype(F32)).T
            loaded.append((pair, query, grad, keys, values, keys_t, delta_terms))
        grad_q, grad_k, grad_v = [], [], []

        def first(i):
            _, query, grad, keys, values, _, _ = loaded[i // 2]
            query_h, grad_h = head_of(query, i % 2), head_of(grad, i % 2)
            return query_h, grad_h, nt(keys, query_h), nt(values, grad_h)

        def then(i, ready):
            pair, _, _, _, _, keys_t, delta_terms = loaded[i // 2]
            index, (query_h, grad_h, scores, grad_probs) = i % 2, ready
            half = slice(index * HEAD_DIM, (index + 1) * HEAD_DIM)
            probs = jnp.exp2(scores * LOG2E + bias - lse_ref[pair, index : index + 1, :])
            delta = jnp.sum(delta_terms[half], axis=0, keepdims=True)
            grad_scores = (probs * (grad_probs - delta)).astype(BF16)
            grad_v.append(nn(probs.astype(BF16), grad_h))
            grad_k.append(nn(grad_scores, query_h))
            grad_q.append(nn(keys_t[half], grad_scores))
            if index == 0:
                return
            both = jnp.concatenate(grad_q[-2:], axis=0).T * HEAD_DIM**-0.5
            outs[0][0, here, lanes(pair)] = both.astype(BF16)
            away = lanes((pair + group) % pairs)
            for which, parts in enumerate((grad_k, grad_v)):
                value = parts[-2] + parts[-1]
                if edge:
                    outs[1][which, :, lanes(pair)] = value[:EDGE]
                    outs[2][which, :, away] = value[EDGE:].astype(BF16)
                else:
                    outs[0][1 + which, here, lanes(pair)] = value.astype(BF16)

        staggered(2 * group, first, then)

    inputs = [(a, WHOLE) for a in (query, keys, values, bias)]
    inputs += [(a, WHOLE) for a in (mixed, grad, lse)]
    inputs.append((far if edge else held, WHOLE))
    outputs = [(shape((3, rows, width), BF16), WHOLE)]
    if edge:
        outputs += [(shape((2, EDGE, width), F32), WHOLE), (shape((2, EDGE, width), BF16), WHOLE)]
    name = "attend_edge_back" if edge else "attend_back"
    return call(kernel, (1,), inputs, outputs, scalars, name, after, None if edge else {7: 0}, limit=12)


def merge_edge(near, far, held, scalars, after):
    def kernel(_, ins, outs):
        for which in range(2):
            total = ins[0][which] + ins[1][which].astype(F32)
            outs[0][1 + which, SPAN:, :] = total.astype(BF16)

    inputs = [(near, WHOLE), (far, WHOLE), (held, WHOLE)]
    return call(kernel, (1,), inputs, [(shape(held.shape, BF16), WHOLE)], scalars, "merge_edge", after, {2: 0})[0]


def normal_parts(value):
    size = jnp.abs(value)
    t = 1.0 / (1.0 + (0.3275911 * 0.5**0.5) * size)
    bell = jnp.exp2((-0.5 * LOG2E) * (value * value))
    poly = t * (
        0.127414796 + t * (-0.142248368 + t * (0.7107068705 + t * (-0.7265760135 + t * 0.5307027145)))
    )
    tail = poly * bell
    return jnp.where(value >= 0, 1.0 - tail, tail), bell * 0.3989422804014327


def standardize(hidden):
    centred = hidden - jnp.mean(hidden, axis=-1, keepdims=True)
    scale = lax.rsqrt(jnp.mean(centred * centred, axis=-1, keepdims=True) + 1e-05)
    return centred * scale, scale


def standardize_back(grad, xhat, scale):
    mean_grad = jnp.mean(grad, axis=-1, keepdims=True)
    mean_both = jnp.mean(grad * xhat, axis=-1, keepdims=True)
    return scale * (grad - mean_grad - xhat * mean_both)


def add_rows(ref, values):
    @pl.when(pl.program_id(0) == 0)
    def _():
        ref[...] = jnp.zeros_like(ref)

    for row, value in enumerate(values):
        ref[row : row + 1, :] += jnp.sum(value, axis=0, keepdims=True)


CHUNK = 768
B_OUT, GAIN1, SHIFT1, B_DOWN, GAIN2, SHIFT2 = range(6)


def tile_of(tiles, columns):
    return pl.BlockSpec((EDGE, columns), lambda i, *sc: (jnp.minimum(i, tiles - 1), 0))


def layer_forward(mixed, x, cotangent, live, vectors, packs, w_up, w_down, scalars):
    rows, width = x.shape
    tiles, hidden = rows // EDGE, w_up[0].shape[1]
    block, local, taken = hidden // 4, width // 2, rows // 2
    parts = [(side, at) for side in range(2) for at in range(0, hidden, CHUNK)]

    def kernel(sc, ins, outs, act_all, cot_all, out_all, come, gone):
        mixed_ref, x_ref, cot_ref, live_ref = ins[:4]
        vecs, packs, wu, wd = ins[4:10], ins[10:12], ins[12:14], ins[14:16]
        out_ref, act_ref, slope_ref, normed_ref, xhat_ref, scale_ref, grad_ref, low_ref, sums_ref, gw_ref = outs
        here = [(rows_of(t), rows_of((t + sc[MP]) % tiles)) for t in range(tiles)]
        arriving = [pltpu.make_async_copy(cot_ref.at[p, :], cot_all.at[l, :], come.at[t]) for t, (l, p) in enumerate(here)]
        for copy in arriving:
            copy.start()
        sums_ref[...] = jnp.zeros_like(sums_ref)

        def vec(row):
            return vecs[row][...].astype(F32)[None, :]

        @pl.loop(0, 2)
        def _(tile):
            mine = pl.ds(pl.multiple_of(tile * taken, 128), taken)
            attn = nn(mixed_ref[mine, :local], packs[0][:local, :]) + nn(mixed_ref[mine, local:], packs[1][:local, :])
            biases = [biases_of(pack) for pack in packs]
            xhat1, scale1 = standardize(x_ref[mine, :].astype(F32) + attn + vec(B_OUT))
            xhat_ref[mine, :] = xhat1
            scale_ref[mine, :] = jnp.broadcast_to(scale1, (taken, 128))
            normed = xhat1 * vec(GAIN1) + vec(SHIFT1)
            low = normed.astype(BF16)
            normed_ref[mine, :] = low
            resid2 = [normed + vec(B_DOWN)]

            def first(i):
                side, at = parts[i]
                return nn(low, wu[side][:, at : at + CHUNK])

            def then(i, up):
                side, at = parts[i]
                where, line = slice(at, at + CHUNK), 1 + at // width
                up = up + biases[side][line : line + 1, at % width : at % width + CHUNK]
                big, small = normal_parts(up)
                act = (up * big).astype(BF16)
                if side == 0:
                    act_ref[mine, where] = act
                else:
                    act_all[mine, where] = act
                slope_ref[mine, side * hidden + at : side * hidden + at + CHUNK] = (big + up * small).astype(BF16)
                resid2[0] += nn(act, wd[side][where, :])

            in_turn(len(parts), first, then)
            xhat2, scale2 = standardize(resid2[0])
            out_all[mine, :] = (xhat2 * vec(GAIN2) + vec(SHIFT2)).astype(BF16)

            @pl.when(tile == 0)
            def _():
                for copy in arriving:
                    copy.wait()

            grad = cot_all[mine, :].astype(F32) * live_ref[mine, 0:1]
            grad_resid2 = standardize_back(grad * vec(GAIN2), xhat2, scale2)
            grad_ref[mine, :] = grad_resid2
            low_ref[mine, :] = grad_resid2.astype(BF16)
            for row, value in enumerate((grad * xhat2, grad, grad_resid2)):
                sums_ref[row : row + 1, :] += jnp.sum(value, axis=0, keepdims=True)

        leaving = [pltpu.make_async_copy(out_all.at[l, :], out_ref.at[p, :], gone.at[t]) for t, (l, p) in enumerate(here)]
        for copy in leaving:
            copy.start()

        @pl.loop(0, hidden // block)
        def _(part):
            gw_ref[pl.ds(pl.multiple_of(part * block, 128), block), :] = tn(
                act_all[:, lanes(part, block)], low_ref[...]
            ).astype(BF16)

        for copy in leaving:
            copy.wait()

    inputs = [(mixed, WHOLE), (x, WHOLE), (cotangent, FAR), const(live)]
    inputs += [const(a) for a in vectors] + [(a, WHOLE) for a in (*packs, *w_up, *w_down)]
    outputs = [
        (shape((rows, width), BF16), FAR),
        (shape((rows, hidden), BF16), WHOLE),
        (shape((rows, 2 * hidden), BF16), WHOLE),
        (shape((rows, width), BF16), WHOLE),
        (shape((rows, width), F32), WHOLE),
        (shape((rows, 128), F32), WHOLE),
        (shape((rows, width), F32), WHOLE),
        (shape((rows, width), BF16), WHOLE),
        (shape((8, width), F32), WHOLE),
        (shape((hidden, width), BF16), WHOLE),
    ]
    scratch = [pltpu.VMEM((rows, hidden), BF16), pltpu.VMEM((rows, width), BF16), pltpu.VMEM((rows, width), BF16)]
    scratch += [pltpu.SemaphoreType.DMA((tiles,))] * 2
    return call(kernel, (1,), inputs, outputs, scalars, "layer_forward", limit=14, scratch=scratch)


def layer_backward(
    grad_down, grad_resid2, slope, xhat1, scale1, normed, gain1, packs, w_up, w_down, scalars, after
):
    rows, width = grad_down.shape
    tiles, hidden = rows // EDGE, w_up[0].shape[1]
    block, local, taken = width // 2, width // 2, rows // 2
    parts = [(side, at) for side in range(2) for at in range(0, hidden, CHUNK)]

    def kernel(_, ins, outs, up_all, resid_all, gone):
        low_ref, grad_ref, slope_ref, xhat_ref, scale_ref, normed_ref, gain_ref = ins[:7]
        packs, wu, wd = ins[7:9], ins[9:11], ins[11:13]
        up_ref, resid_ref, attn_ref, mixed_ref, sums_ref, bias_ref, gw_ref = outs
        gain = gain_ref[...].astype(F32)[None, :]
        sums_ref[...] = jnp.zeros_like(sums_ref)
        bias_ref[...] = jnp.zeros_like(bias_ref)

        @pl.loop(0, 2)
        def _(tile):
            mine = pl.ds(pl.multiple_of(tile * taken, 128), taken)
            low = low_ref[mine, :]
            grad_normed = grad_ref[mine, :]
            for side, at in parts:
                where, both = slice(at, at + CHUNK), slice(side * hidden + at, side * hidden + at + CHUNK)
                grad_act = nt(low, wd[side][where, :])
                grad_up = (grad_act * slope_ref[mine, both].astype(F32)).astype(BF16)
                if side == 0:
                    up_ref[mine, where] = grad_up
                else:
                    up_all[mine, where] = grad_up
                bias_ref[0:1, both] += jnp.sum(grad_up.astype(F32), axis=0, keepdims=True)
                grad_normed += nt(grad_up, wu[side][:, where])
            xhat = xhat_ref[mine, :]
            grad_resid1 = standardize_back(grad_normed * gain, xhat, scale_ref[mine, 0:1])
            resid_all[mine, :] = grad_resid1
            grad_attn = grad_resid1.astype(BF16)
            attn_ref[mine, :] = grad_attn
            mixed_ref[mine, :local] = nt(grad_attn, packs[0][:local, :]).astype(BF16)
            mixed_ref[mine, local:] = nt(grad_attn, packs[1][:local, :]).astype(BF16)
            for row, value in enumerate((grad_normed * xhat, grad_normed, grad_resid1)):
                sums_ref[row : row + 1, :] += jnp.sum(value, axis=0, keepdims=True)

        leaving = pltpu.make_async_copy(resid_all, resid_ref, gone)
        leaving.start()

        @pl.loop(0, hidden // block)
        def _(i):
            gw_ref[pl.ds(pl.multiple_of(i * block, 128), block), :] = tn(
                normed_ref[:, lanes(i % 2, block)], up_all[:, lanes(i // 2, width)]
            ).astype(BF16)

        leaving.wait()

    inputs = [(a, WHOLE) for a in (grad_down, grad_resid2, slope, xhat1, scale1, normed)]
    inputs += [const(gain1)] + [(a, WHOLE) for a in (*packs, *w_up, *w_down)]
    outputs = [
        (shape((rows, hidden), BF16), WHOLE),
        (shape((rows, width), F32), FAR),
        (shape((rows, width), BF16), WHOLE),
        (shape((rows, width), BF16), WHOLE),
        (shape((8, width), F32), WHOLE),
        (shape((8, 2 * hidden), F32), WHOLE),
        (shape((hidden, width), BF16), WHOLE),
    ]
    scratch = [pltpu.VMEM((rows, hidden), BF16), pltpu.VMEM((rows, width), F32), pltpu.SemaphoreType.DMA]
    return call(kernel, (1,), inputs, outputs, scalars, "layer_backward", after, limit=14, scratch=scratch)


def down_gradient(act, grad_down, scalars, after=()):
    rows, width = grad_down.shape
    hidden = act.shape[1]
    block = hidden // 4

    def kernel(_, ins, outs):
        @pl.loop(0, 4)
        def _(i):
            rows_out = pl.ds(pl.multiple_of(i * block, 128), block)
            outs[0][rows_out, :] = tn(ins[0][:, lanes(i, block)], ins[1][...])

    inputs, outputs = [(act, WHOLE), (grad_down, WHOLE)], [(shape((hidden, width), F32), WHOLE)]
    return call(kernel, (1,), inputs, outputs, scalars, "down_gradient", after)[0]


def up_gradient(normed, grad_up, scalars, after=()):
    rows, width = normed.shape
    parts = grad_up.shape[1] // width
    block = width // 2

    def kernel(_, ins, outs):
        @pl.loop(0, 2 * parts)
        def _(i):
            rows_out = pl.ds(pl.multiple_of(i * block, 128), block)
            outs[0][rows_out, :] = tn(ins[0][:, lanes(i % 2, block)], ins[1][:, lanes(i // 2, width)])

    inputs, outputs = [(normed, WHOLE), (grad_up, WHOLE)], [(shape((parts * width, width), F32), WHOLE)]
    return call(kernel, (1,), inputs, outputs, scalars, "up_gradient", after)[0]


def attention_gradient(x, grads, mixed, grad_attn, half, dtype, scalars, after=()):
    rows, width = x.shape
    local = width // 2
    columns = slice(half * local, (half + 1) * local)

    def kernel(_, ins, outs):
        x_ref, grad_ref, mixed_ref, attn_ref = ins
        sums_ref = outs[2]
        for part in range(3):
            mine = slice(part % 2 * local, (part % 2 + 1) * local)
            grad = grad_ref[part, :, columns]
            outs[part // 2][mine, :local] = tn(x_ref[:, :local], grad).astype(dtype)
            outs[part // 2][mine, local:] = tn(x_ref[:, local:], grad).astype(dtype)
            sums_ref[part] = jnp.broadcast_to(jnp.sum(grad.astype(F32), axis=0, keepdims=True), (8, local))
        outs[1][local:, :] = tn(mixed_ref[:, columns], attn_ref[...]).astype(dtype)

    inputs = [(a, WHOLE) for a in (x, grads, mixed, grad_attn)]
    outputs = [(shape((2 * local, width), dtype), WHOLE)] * 2 + [(shape((3, 8, local), F32), WHOLE)]
    return call(kernel, (1,), inputs, outputs, scalars, f"attention_gradient_{half}", after)


def token_gradient(grads, grad_resid1, w_qkv, scalars, after=()):
    rows, width = grad_resid1.shape
    tiles, local = rows // EDGE, width // 2

    def kernel(sc, ins, outs, total, weights, resid, come, gone):
        arriving = [pltpu.make_async_copy(ins[2 + side], weights.at[side], come.at[side]) for side in range(2)]
        arriving.append(pltpu.make_async_copy(ins[1], resid, come.at[2]))
        for copy in arriving:
            copy.start()
        here = [slice(tile * EDGE, (tile + 1) * EDGE) for tile in range(tiles)]

        def part(mine, side):
            columns = slice(side * local, (side + 1) * local)
            return sum(nt(ins[0][k, mine, columns], weights[side, k]) for k in range(3))

        arriving[0].wait()
        for mine in here:
            total[mine, :] = part(mine, 0)
        arriving[1].wait()
        arriving[2].wait()
        leaving = []
        for tile, mine in enumerate(here):
            there = rows_of((tile + sc[MP]) % tiles)
            total[mine, :] += resid[mine, :] + part(mine, 1)
            leaving.append(pltpu.make_async_copy(total.at[mine, :], outs[0].at[there, :], gone.at[tile]))
            leaving[-1].start()
        for copy in leaving:
            copy.wait()
        outs[1][...] = jnp.zeros_like(outs[1])

    inputs = [(grads, WHOLE)] + [(a, FAR) for a in (grad_resid1, *w_qkv)]
    outputs = [(shape((rows, width), F32), FAR), TOKEN]
    scratch = [pltpu.VMEM((rows, width), F32), pltpu.VMEM((2, *w_qkv[0].shape), BF16), pltpu.VMEM((rows, width), F32)]
    scratch += [pltpu.SemaphoreType.DMA((3,)), pltpu.SemaphoreType.DMA((tiles,))]
    return call(kernel, (1,), inputs, outputs, scalars, "token_gradient", after, scratch=scratch, limit=16)


TAIL = 16


def parted(value):
    high = value.astype(BF16)
    return high, (value - high.astype(F32)).astype(BF16)


def tails(head_own, head_far, sums_up, sums1, sums2, scalars, after=()):
    local, width = head_own.shape[2], sums1.shape[1]
    units = sums_up.shape[1] // 2

    def kernel(sc, ins, outs):
        second = sc[MP] == 1
        for side, heads in enumerate((ins[0], ins[1])):
            lines = [jnp.concatenate([heads[0, 0:1, :], heads[2, 0:1, :]], axis=1)]
            at = side * units
            lines += [ins[2][0:1, at + c : at + c + width] for c in range(0, units, width)]
            first, last = ins[3][0:3, :], ins[4][0:3, :]
            lines.append(jnp.where(second, first, last) if side == 0 else jnp.where(second, last, first))
            lines.append(jnp.zeros((8 - sum(l.shape[0] for l in lines), width), F32))
            high, low = parted(jnp.concatenate(lines, axis=0))
            outs[side][:8], outs[side][8:] = high, low

    inputs = [(a, WHOLE) for a in (head_own, head_far, sums_up, sums1, sums2)]
    return call(kernel, (1,), inputs, [(shape((TAIL, width), BF16), WHOLE)] * 2, scalars, "tails", after)


def tail_sum(own, came):
    own, came = own.astype(F32), came.astype(F32)
    return (own[:8] + own[8:]) + (came[:8] + came[8:])


def fold(kept, came, step, scalars, name, after, tail=None, carry=()):
    rows, width = kept.shape
    half = rows // 2
    extra = 0 if tail is None else TAIL
    if half % 16:
        total, bit = kept + came[:rows].astype(F32), scalars[BITS + step]
        go = lax.dynamic_slice_in_dim(total, (1 - bit) * half, half).astype(BF16)
        if extra:
            both = tail_sum(tail[0][-TAIL:], tail[1][-TAIL:])
            high = lax.reduce_precision(both, 8, 7)
            go = jnp.concatenate([go, high.astype(BF16), (both - high).astype(BF16)], axis=0)
        return go, lax.dynamic_slice_in_dim(total, bit * half, half), *carry
    inputs = [kept, came] + ([] if tail is None else list(tail))

    def kernel(sc, ins, outs):
        bit = sc[BITS + step]
        stay = pl.ds(pl.multiple_of(bit * half, 16), half)
        go = pl.ds(pl.multiple_of((1 - bit) * half, 16), half)
        outs[0][:half] = (ins[0][go, :] + ins[1][go, :].astype(F32)).astype(BF16)
        outs[1][...] = ins[0][stay, :] + ins[1][stay, :].astype(F32)
        if extra:
            at, to = ins[2].shape[0] - TAIL, ins[3].shape[0] - TAIL
            high, low = parted(tail_sum(ins[2][at:, :], ins[3][to:, :]))
            outs[0][half : half + 8], outs[0][half + 8 :] = high, low

    outputs = [(shape((half + extra, width), BF16), WHOLE), (shape((half, width), F32), WHOLE)]
    return call(kernel, (1,), [(a, WHOLE) for a in inputs], outputs, scalars, name, after, carry=carry)


def add(own, came, scalars, name, after, tail=None, carry=()):
    rows, width = came.shape[0] - (0 if tail is None else TAIL), own.shape[1]
    if rows % 16:
        whole = (own[:rows].astype(F32) + came[:rows].astype(F32)).astype(BF16)
        return whole, None if tail is None else tail_sum(tail[0][-TAIL:], tail[1][-TAIL:]), *carry

    def kernel(_, ins, outs):
        outs[0][...] = (ins[0][:rows, :].astype(F32) + ins[1][:rows, :].astype(F32)).astype(BF16)
        if tail is not None:
            at, to = ins[2].shape[0] - TAIL, ins[3].shape[0] - TAIL
            outs[1][...] = tail_sum(ins[2][at:, :], ins[3][to:, :])

    inputs = [own, came] + ([] if tail is None else list(tail))
    outputs = [(shape((rows, width), BF16), WHOLE)]
    if tail is not None:
        outputs.append((shape((8, width), F32), WHOLE))
    found = call(kernel, (1,), [(a, WHOLE) for a in inputs], outputs, scalars, name, after, carry=carry)
    return found if tail is not None else (found[0], None, *found[1:])


def add_on(own, came, scalars, name, after, tail, carry=()):
    rows, width = came.shape[0] - TAIL, own.shape[1]
    if rows % 16:
        both = tail_sum(tail[0][-TAIL:], tail[1][-TAIL:])
        high = lax.reduce_precision(both, 8, 7)
        whole = (own[:rows].astype(F32) + came[:rows].astype(F32)).astype(BF16)
        return jnp.concatenate([whole, high.astype(BF16), (both - high).astype(BF16)], axis=0), *carry

    def kernel(_, ins, outs):
        outs[0][:rows] = (ins[0][:rows, :].astype(F32) + ins[1][:rows, :].astype(F32)).astype(BF16)
        at, to = ins[2].shape[0] - TAIL, ins[3].shape[0] - TAIL
        high, low = parted(tail_sum(ins[2][at:, :], ins[3][to:, :]))
        outs[0][rows : rows + 8], outs[0][rows + 8 :] = high, low

    inputs = [(a, WHOLE) for a in (own, came, *tail)]
    outputs = [(shape((rows + TAIL, width), BF16), WHOLE)]
    return call(kernel, (1,), inputs, outputs, scalars, name, after, carry=carry)


def join(whole, came, step, scalars, name, after, carry=()):
    rows, width = whole.shape
    if rows % 16:
        ahead = scalars[BITS + step] == 0
        first, last = jnp.where(ahead, whole, came), jnp.where(ahead, came, whole)
        return jnp.concatenate([first, last], axis=0), *carry

    def kernel(sc, ins, outs):
        bit = sc[BITS + step]
        outs[0][pl.ds(pl.multiple_of(bit * rows, 16), rows), :] = ins[0][...]
        outs[0][pl.ds(pl.multiple_of((1 - bit) * rows, 16), rows), :] = ins[1][...]

    outputs = [(shape((2 * rows, width), BF16), WHOLE)]
    inputs = [(whole, WHOLE), (came, WHOLE)]
    return call(kernel, (1,), inputs, outputs, scalars, name, after, carry=carry)


def put(rows_in, mine, kind, held, scalars, name, after, carry=()):
    rows, width = rows_in.shape
    block = width // 2
    chunk = block // 3
    pieces = rows // chunk

    def kernel(sc, ins, outs, ready, done):
        here = sc[BITS] if mine else 1 - sc[BITS]

        def targets(half, piece):
            part, at = divmod(half * rows + piece * chunk, block)
            left, right = slice(0, block), slice(block, width)
            low, high = slice(at, at + chunk), slice(block + at, block + at + chunk)
            if kind == "down":
                return [(outs[0].at[part * block + at : part * block + at + chunk, :], slice(0, width))]
            if kind == "up":
                row, column = part % 2 * block + at, part // 2 * width
                return [(outs[0].at[row : row + chunk, column : column + width], slice(0, width))]
            if kind == "values" and part == 1:
                return [(outs[1].at[low, :], slice(0, width))]
            which = part if kind == "queries" else 2
            return [(outs[0].at[which, low, :], left), (outs[0].at[which, high, :], right)]

        def copies(half, piece):
            return [
                pltpu.make_async_copy(ready.at[piece * chunk : (piece + 1) * chunk, columns], to, done.at[piece, i])
                for i, (to, columns) in enumerate(targets(half, piece))
            ]

        for piece in range(pieces):
            at = slice(piece * chunk, (piece + 1) * chunk)
            ready[at, :] = ins[0][at, :].astype(F32)
            for half in range(2):

                @pl.when(here == half)
                def _():
                    for copy in copies(half, piece):
                        copy.start()

        outs[-1][...] = jnp.zeros_like(outs[-1])
        for half in range(2):

            @pl.when(here == half)
            def _():
                for piece in range(pieces):
                    for copy in copies(half, piece):
                        copy.wait()

    if kind == "down":
        shapes = [(2 * rows, width)]
    elif kind == "up":
        shapes = [(width, 2 * rows // width * width)]
    else:
        shapes = [(3, width, block), (block, width)]
    outputs = [(shape(dims, F32), FAR) for dims in shapes] + [TOKEN]
    inputs = [(rows_in, WHOLE), *((h, FAR) for h in held)]
    aliases = {1 + i: i for i in range(len(held))}
    scratch = [pltpu.VMEM((rows, width), F32), pltpu.SemaphoreType.DMA((pieces, 2))]
    found = call(kernel, (1,), inputs, outputs, scalars, name, after, aliases, scratch=scratch, carry=carry)
    return found[: len(shapes)], found[len(shapes)], *found[len(outputs) :]


ORDER = """
a LB a UG b EB a AB a ME AG1 b AG0 d b a c b TG a d b c d b c d a b c d c d c d a c b d c
""".split()


def program(n_dp):
    steps = n_dp.bit_length() - 1
    assert 1 << steps == n_dp
    orders = (list(range(steps)), [1, 0, *range(2, steps)])

    def swap(array):
        return lax.ppermute(array, "mp", [(0, 1), (1, 0)])

    def partner(array, step):
        pairs = [
            (2 * d + m, 2 * (d ^ (1 << orders[m][step])) + m) for d in range(n_dp) for m in range(2)
        ]
        return lax.ppermute(array, ("dp", "mp"), pairs)

    halvings = max(steps - 1, 0)

    class Chain:
        def __init__(self, kind, own, came, scalars, shared, tail=None):
            self.kind, self.kept, self.came, self.tail, self.shared = kind, own, came, tail, shared
            self.scalars, self.step, self.result, self.vectors = scalars, 0, None, None

        def send(self, sent, bit):
            self.came = partner(sent, bit)
            self.step += 1
            if self.tail is not None:
                self.tail = (sent, self.came)
            return (sent,)

        def advance(self, after, carry=()):
            step, name, scalars = self.step, f"{self.kind}_{self.step}", self.scalars
            back = halvings - 1 - (step - steps)
            if step < halvings:
                sent, self.kept, *carry = fold(
                    self.kept, self.came, step, scalars, name, after, self.tail, carry
                )
                return self.send(sent, step), carry
            if step < steps:
                if self.tail is None:
                    sent, _, *carry = add(self.kept, self.came, scalars, name, after, None, carry)
                else:
                    sent, *carry = add_on(self.kept, self.came, scalars, name, after, self.tail, carry)
                self.kept = sent
                return self.send(sent, step), carry
            if step == steps:
                sent, self.vectors, *carry = add(
                    self.kept, self.came, scalars, name, after, self.tail, carry
                )
                self.tail = None
            elif back >= 0:
                sent, *carry = join(self.whole, self.came, back + 1, scalars, name, after, carry)
            else:
                held = self.result_half if self.kind in ("down", "up") else self.shared
                found, token, *carry = put(self.came, False, self.kind, held, scalars, name, after, carry)
                self.result = found
                if self.kind not in ("down", "up"):
                    self.shared[:] = found
                return (token,), carry
            self.whole = sent
            after = self.send(sent, back)
            if back == 0:
                held = () if self.kind in ("down", "up") else self.shared
                found, token = put(self.whole, True, self.kind, held, scalars, name + "_own", after)
                if self.kind in ("down", "up"):
                    self.result_half = found
                else:
                    self.shared[:] = found
                after = (token,)
            return after, carry

    def per_device(
        tokens, cotangent, mask, lengths, counts, w_qkv, qv_bias, w_out, b_out, gain1, shift1,
        w_up, b_up, w_down, b_down, gain2, shift2,
    ):
        rows, width = tokens.shape
        mp, local, hidden = lax.axis_index("mp"), qv_bias.shape[1], w_up.shape[1]
        limits = jnp.stack([mp, lengths[0], counts[0] * lengths[0]]).astype(jnp.int32)
        scalars = Place(orders)

        w_qkv = (w_qkv, swap(w_qkv))
        vectors = (b_out, gain1, shift1, b_down, gain2, shift2)
        mine = pack(tokens, w_out, qv_bias, b_up, mp.astype(jnp.int32)[None])
        packs = (mine, swap(mine))
        bias_full, bias_edge, live, token = prepare(mask, rows, limits, (mine,))
        query, keys, values, far, x, w_up, w_down = project(
            tokens, w_qkv, packs, (w_up, w_down), scalars, (token,)
        )
        w_up, w_down = ((w, swap(w)) for w in (w_up, w_down))
        mixed, lse = attend(query, keys, values, None, bias_full, None, scalars)
        mixed, lse_edge = attend(query, keys, values, far, bias_edge, mixed, scalars)
        out, act, slope, normed, xhat1, scale1, grad_resid2, grad_down, sums2, gw = layer_forward(
            mixed, x, cotangent, live, vectors, packs, w_up, w_down, scalars
        )
        came = swap(gw)
        own = down_gradient(act, grad_down, scalars, (gw,))

        k = {}
        chains, shared = {"a": Chain("down", own, came, scalars, None)}, []

        def run_layer_backward(after):
            k["up"], k["resid"], k["attn"], k["mixed"], k["sums1"], k["sums_up"], k["gw"] = layer_backward(
                grad_down, grad_resid2, slope, xhat1, scale1, normed, gain1, packs, w_up, w_down, scalars, after
            )
            return (k["sums1"],), ("gw",)

        def run_up_gradient(after):
            own = up_gradient(normed, k["up"], scalars, after)
            chains["b"] = Chain("up", own, k["gw"], scalars, None)
            return (own,), None

        def run_edge_back(after):
            k["grads"], k["near"], k["far"] = attend_back(
                query, keys, values, far, bias_edge, mixed, k["mixed"], lse_edge, None, scalars, after
            )
            return (k["near"],), ("far",)

        def run_back(after):
            k["grads"] = attend_back(
                query, keys, values, None, bias_full, mixed, k["mixed"], lse, k["grads"], scalars, after
            )[0]
            return (k["grads"],), None

        def run_merge(after):
            k["grads"] = merge_edge(k["near"], k["far"], k["grads"], scalars, after)
            return (k["grads"],), None

        def run_far_gradient(after):
            k["gw"], k["gw_last"], k["head_far"] = attention_gradient(
                x, k["grads"], mixed, k["attn"], 1, BF16, scalars, after
            )
            return (k["head_far"],), ("gw", "gw_last")

        def run_own_gradient(after):
            own, last, head_own = attention_gradient(x, k["grads"], mixed, k["attn"], 0, F32, scalars, after)
            tail_own, tail_far = tails(head_own, k["head_far"], k["sums_up"], k["sums1"], sums2, scalars)
            chains["c"] = Chain("queries", own, k["gw"], scalars, shared)
            chains["d"] = Chain("values", last, k["gw_last"], scalars, shared, (tail_own, swap(tail_far)))
            return (own, tail_own), None

        def run_token_gradient(after):
            k["tokens"], token = token_gradient(k["grads"], k["resid"], w_qkv, scalars, after)
            return (token,), None

        work = {
            "LB": run_layer_backward, "UG": run_up_gradient, "EB": run_edge_back, "AB": run_back,
            "ME": run_merge, "AG1": run_far_gradient, "AG0": run_own_gradient, "TG": run_token_gradient,
        }
        after, leaving = (own,), []
        for name in ORDER:
            if name in work:
                after, left = work[name](after)
                leaving += left or ()
            else:
                after, carried = chains[name].advance(after, [k[n] for n in leaving])
                k.update((n, swap(c)) for n, c in zip(leaving, carried, strict=True))
                leaving = []
        while any(c.result is None for c in chains.values()):
            for c in chains.values():
                if c.result is None:
                    after, _ = c.advance(after)

        vectors = chains["d"].vectors
        head, up = vectors[0].reshape(2, local), vectors[1 : 1 + hidden // width].reshape(-1)
        mine = vectors[1 + hidden // width : 4 + hidden // width]
        other = swap(mine)
        g_gain2, g_shift2, g_b_down = jnp.where(mp == 0, mine, other)
        g_gain1, g_shift1, g_b_out = jnp.where(mp == 0, other, mine)
        gw_qkv, gw_out = shared
        return (
            out, k["tokens"], gw_qkv, head, gw_out, g_b_out, g_gain1, g_shift1,
            chains["b"].result[0], up, chains["a"].result[0], g_b_down, g_gain2, g_shift2,
        )

    return per_device


def solution(mesh):
    rows, cols, one = P(("dp", "mp"), None), P(None, "mp"), P()
    in_specs = (
        rows, rows, P("dp"), P("dp"), P("dp"),
        P(None, None, "mp"), cols, P("mp", None), one, one, one,
        cols, P("mp"), P("mp", None), one, one, one,
    )
    out_specs = (
        rows, rows, P(None, None, "mp"), cols, P("mp", None), one, one, one,
        cols, P("mp"), P("mp", None), one, one, one,
    )
    return jax.shard_map(
        program(mesh.shape["dp"]), mesh=mesh, in_specs=in_specs, out_specs=out_specs, check_vma=False
    )
```
